32 devices in a mesh: dp: 8 (over y, x, core), seq: 4 (over z).
Axes of the slice: x: 2, y: 2, z: 4, core: 2. Of those that a mesh axis runs over, the one named last changes fastest.
Arguments:
- tokens: bfloat16 [24, 1024, 768], P('dp', 'seq'), may hold values from -6 to 6
- cond: bfloat16 [24, 128], P('dp'), may hold values from -6 to 6
- lengths: int32 [24], P('dp'), may hold values from 128 to 1024, as said below
- gain_one: float32 [768], replicated, may hold values from 0.1 to 1.9
- gain_two: float32 [768], replicated, may hold values from 0.1 to 1.9
- w_ada: bfloat16 [128, 4608], replicated, may hold values from -0.5 to 0.5
- b_ada: float32 [4608], replicated, may hold values from -3 to 3
- w_qkv: bfloat16 [768, 2304], replicated, may hold values from -0.21875 to 0.21875
- w_out: bfloat16 [768, 768], replicated, may hold values from -0.3125 to 0.3125
- w_up: bfloat16 [768, 3072], replicated, may hold values from -0.21875 to 0.21875
- b_up: float32 [3072], replicated, may hold values from -3 to 3
- w_down: bfloat16 [3072, 768], replicated, may hold values from -0.109375 to 0.109375
- b_down: float32 [768], replicated, may hold values from -3 to 3
- cotangent: bfloat16 [24, 1024, 768], P('dp', 'seq'), may hold values from -8 to 8
Outputs:
- output: bfloat16 [24, 1024, 768], P('dp', 'seq')
- grad_tokens: float32 [24, 1024, 768], P('dp', 'seq')
- grad_cond: float32 [24, 128], P('dp')
- grad_gain_one: float32 [768], P(('dp', 'seq'))
- grad_gain_two: float32 [768], P(('dp', 'seq'))
- grad_w_ada: float32 [128, 4608], P(None, ('dp', 'seq'))
- grad_b_ada: float32 [4608], P(('dp', 'seq'))
- grad_w_qkv: float32 [768, 2304], P(('dp', 'seq'))
- grad_w_out: float32 [768, 768], P(('dp', 'seq'))
- grad_w_up: float32 [768, 3072], P(('dp', 'seq'))
- grad_b_up: float32 [3072], P(('dp', 'seq'))
- grad_w_down: float32 [3072, 768], P(('dp', 'seq'))
- grad_b_down: float32 [768], P(('dp', 'seq'))
The draws below stay inside these ranges and needn't reach their ends.
Inputs may be any that keep to these rules, and one draw needn't show every extreme that they name: `lengths`: each length is 128, 512 or 1024, each sequence's drawn independently; some sequence of the batch has 1024 and some other has 128.
All inputs are finite; a program needn't handle non-finite values.
Results may differ from the reference program's by a relative error of at most 0.015.
The reference program's roundings to bfloat16 on the way count: a program that leaves them out, or rounds other values in their place, can miss the bound.
Values may be sent and summed in bfloat16 or wider, within the bound.
No kernel may reach another device: no remote copies, remote signals or barrier semaphores. Data moves between devices by JAX's collectives and lax.ppermute only.
A program may use at most 256 MiB of HBM per device.

```python
import jax
import jax.numpy as jnp
from jax import lax

D = 768
HEADS = 12
HD = 64
FF = 3072
COND = 128
SLOTS = 1024
BATCH = 24


def draw_lengths(key, part):
    key = jax.random.fold_in(key, 17)
    pick_key, full_key, short_key = jax.random.split(key, 3)
    picks = jax.random.randint(pick_key, (BATCH,), 0, 3)
    spans = jnp.where(picks == 0, SLOTS // 8, jnp.where(picks == 1, SLOTS // 2, SLOTS))
    full_index = jax.random.randint(full_key, (), 0, BATCH)
    offset = jax.random.randint(short_key, (), 0, max(BATCH - 1, 1))
    short_index = (full_index + 1 + offset) % BATCH
    position = jnp.arange(BATCH)
    spans = jnp.where(position == short_index, SLOTS // 8, spans)
    spans = jnp.where(position == full_index, SLOTS, spans)
    return spans.astype(jnp.int32)


def with_spikes(values, rng, source, target, blocks, factor):
    owner, partner = [(jnp.arange(values.shape[dim]) // (values.shape[dim] // blocks)).reshape([-1 if axis == dim else 1 for axis in range(values.ndim)]) for dim in (source, target)]
    chosen = jax.random.permutation(rng, blocks)[partner]
    strong = (owner == chosen) | (owner == (partner + blocks // 2) % blocks)
    return jnp.where(strong, factor * values, values)


def steps_of(own_key, dims, cuts, smallest, high):
    loudness, own = 1.0, jax.random.fold_in(own_key, 6)
    for axis_at, parts in cuts:
        draws = jnp.exp(jax.random.uniform(jax.random.fold_in(own, axis_at), (parts,), jnp.float32, smallest / len(cuts), high / len(cuts)))
        loudness = loudness * jnp.repeat(draws, dims[axis_at] // parts).reshape([-1 if axis == axis_at else 1 for axis in range(len(dims))])
    return loudness


def gaussian(stream_key, extent, scale, limit, pieces=(), dtype=jnp.bfloat16):
    level = steps_of(stream_key, extent, pieces, -0.22, 0.18) if pieces else 1.0
    values = jax.random.normal(stream_key, extent, jnp.float32) * scale * level
    return jnp.minimum(jnp.maximum(values, -limit), limit).astype(dtype)


def noise_with(rng, shape, spread, limit, shards, heavy, held_as=jnp.bfloat16):
    values = spread * jax.random.normal(rng, shape, jnp.float32)
    if shards:
        values = values * steps_of(rng, shape, shards, -0.22, 0.18)
    return jnp.clip(with_spikes(values, jax.random.fold_in(rng, 3), *heavy), -limit, limit).astype(held_as)


def setup_inputs(seed: int = 0) -> dict:
    seeds = jax.random.split(jax.random.key(seed), 15)
    return {
        "tokens": gaussian(seeds[0], (BATCH, SLOTS, D), 1.0, 6.0, ((0, 8), (1, 4))),
        "cond": gaussian(seeds[1], (BATCH, COND), 1.0, 6.0, ((0, 8),)),
        "lengths": draw_lengths(jax.random.fold_in(seeds[14], 71), 0),
        "gain_one": jnp.clip(1.0 + 0.18 * jax.random.normal(seeds[3], (D,), jnp.float32), 0.1, 1.9),
        "gain_two": jnp.clip(1.0 + 0.18 * jax.random.normal(seeds[4], (D,), jnp.float32), 0.1, 1.9),
        "w_ada": gaussian(seeds[5], (COND, 6 * D), COND ** -0.5, 0.5),
        "b_ada": gaussian(seeds[6], (6 * D,), 0.5, 3.0, (), jnp.float32),
        "w_qkv": gaussian(seeds[7], (D, 3 * D), D ** -0.5, 0.21875),
        "w_out": gaussian(seeds[8], (D, D), (D // 2) ** -0.5, 0.3125),
        "w_up": gaussian(seeds[9], (D, FF), D ** -0.5, 0.21875),
        "b_up": gaussian(seeds[10], (FF,), 0.5, 3.0, (), jnp.float32),
        "w_down": gaussian(seeds[11], (FF, D), FF ** -0.5, 0.109375),
        "b_down": gaussian(seeds[12], (D,), 0.5, 3.0, (), jnp.float32),
        "cotangent": noise_with(seeds[13], (BATCH, SLOTS, D), 1.0, 8.0, ((0, 8), (1, 4)), (0, 2, 8, 2.0)),
    }


EPS = 1e-05
NEG = -1e+30
HIGH = lax.Precision.HIGHEST

@jax.custom_vjp
def low(v):
    return lax.optimization_barrier(v.astype(jnp.bfloat16)).astype(jnp.float32)

@jax.custom_vjp
def low_back(v):
    return v

def low_keep(v):
    return (low(v), None)

def low_pass(kept, grad):
    return (grad,)

def back_keep(v):
    return (v, None)

def back_low(kept, grad):
    return (low(grad),)
low.defvjp(low_keep, low_pass)
low_back.defvjp(back_keep, back_low)

def normalize(vector, gain):
    average = lax.optimization_barrier(jnp.mean(vector, axis=-1, keepdims=True))
    centred = vector - average
    return centred * lax.rsqrt(lax.optimization_barrier(jnp.mean(centred * centred, axis=-1, keepdims=True)) + EPS) * gain

def rotary(vector, cosine, sine_table):
    half_width = vector.shape[-1] // 2
    front_half = vector[..., :half_width]
    back_half = vector[..., half_width:]
    return jnp.concatenate([front_half * cosine - back_half * sine_table, back_half * cosine + front_half * sine_table], axis=-1)

def rotary_tables(slot_count):
    positions = jnp.arange(slot_count).astype(jnp.float32)
    inverse_freq = jnp.power(10000.0, -jnp.arange(HD // 2).astype(jnp.float32) * 2.0 / HD)
    angles = positions[:, None] * inverse_freq[None, :]
    return (jnp.cos(angles)[:, None, :], jnp.sin(angles)[:, None, :])

def layer_forward(tokens, cond, lengths, params):
    gain_one, gain_two, w_ada, b_ada, w_qkv, w_out, w_up, b_up, w_down, b_down = params
    group_size, slot_count, model_width = tokens.shape
    modulation = jnp.dot(cond, w_ada, precision=HIGH) + b_ada
    shift_one, scale_one, gate_one, shift_two, scale_two, gate_two = [modulation[:, None, block_index * model_width:(block_index + 1) * model_width] for block_index in range(6)]
    act_one = low(normalize(tokens, gain_one) * (1.0 + scale_one) + shift_one)
    projected = low_back(jnp.einsum('gtd,de->gte', act_one, w_qkv, precision=HIGH)).reshape(group_size, slot_count, 3, HEADS, HD)
    cosine, sine_table = rotary_tables(slot_count)
    queries = low(rotary(projected[:, :, 0], cosine, sine_table))
    keys = low(rotary(projected[:, :, 1], cosine, sine_table))
    values = low(projected[:, :, 2])
    scores = low_back(jnp.einsum('gqhe,gkhe->ghqk', queries, keys, precision=HIGH) * HD ** (-0.5))
    usable = jnp.arange(slot_count)[None, :] < lengths[:, None]
    scores = jnp.where(usable[:, None, None, :], scores, NEG)
    probs_rounded = low(jax.nn.softmax(scores, axis=-1))
    mixture = low(low_back(jnp.einsum('ghqk,gkhe->gqhe', probs_rounded, values, precision=HIGH))).reshape(group_size, slot_count, model_width)
    branch_one = low_back(jnp.einsum('gtd,de->gte', mixture, w_out, precision=HIGH))
    residual = tokens + gate_one * branch_one
    act_two = low(normalize(residual, gain_two) * (1.0 + scale_two) + shift_two)
    pre_gelu = low_back(jnp.einsum('gtd,df->gtf', act_two, w_up, precision=HIGH) + b_up)
    activated = low(jax.nn.gelu(pre_gelu, approximate=True))
    branch_two = low_back(jnp.einsum('gtf,fd->gtd', activated, w_down, precision=HIGH) + b_down)
    return residual + gate_two * branch_two

def reference(tokens, cond, lengths, gain_one, gain_two, w_ada, b_ada, w_qkv, w_out, w_up, b_up, w_down, b_down, cotangent):
    params = tuple((element.astype(jnp.float32) for element in (gain_one, gain_two, w_ada, b_ada, w_qkv, w_out, w_up, b_up, w_down, b_down)))
    group_size = 2 if BATCH % 2 == 0 else 1
    group_count = BATCH // group_size
    inputs = tokens.astype(jnp.float32).reshape(group_count, group_size, SLOTS, D)
    conds = cond.astype(jnp.float32).reshape(group_count, group_size, COND)
    spans = lengths.astype(jnp.int32).reshape(group_count, group_size)
    pulls = cotangent.astype(jnp.float32).reshape(group_count, group_size, SLOTS, D)

    def accumulate(totals, element):
        block_in, block_cond, block_len, block_pull = element

        def forward(block_x, block_c, weights):
            return layer_forward(block_x, block_c, block_len, weights)
        result, backward = jax.vjp(forward, block_in, block_cond, params)
        grad_in, grad_c, grad_weights = backward(block_pull)
        totals = jax.tree.map(jnp.add, totals, grad_weights)
        return (totals, (result.astype(jnp.bfloat16), grad_in, grad_c))
    zero_grads = tuple((jnp.zeros_like(element) for element in params))
    totals, (outputs, grad_inputs, grad_conds) = lax.scan(accumulate, zero_grads, (inputs, conds, spans, pulls))
    return (outputs.reshape(BATCH, SLOTS, D), grad_inputs.reshape(BATCH, SLOTS, D), grad_conds.reshape(BATCH, COND), totals[0], totals[1], totals[2], totals[3], totals[4], totals[5], totals[6], totals[7], totals[8], totals[9])
```

```python
import functools

import jax
import jax.numpy as jnp
import numpy as np
from jax import lax
from jax.experimental import pallas as pl
from jax.experimental.pallas import tpu as pltpu
from jax.sharding import PartitionSpec as P

HEADS = 12
HD = 64
EPS = 1e-05
HIGH = lax.Precision.HIGHEST
BF = jnp.bfloat16
F32 = jnp.float32
PACK = 4
BLOCK = PACK * HD
HALF = BLOCK // 2
SPANS = (128, 512, 1024)
GELU_C = float(np.sqrt(2.0 / np.pi))


def nn(left, right):
    return lax.dot_general(left, right, (((1,), (0,)), ((), ())), preferred_element_type=F32)


def nt(left, right):
    return lax.dot_general(left, right, (((1,), (1,)), ((), ())), preferred_element_type=F32)


def normalize(vector):
    average = jnp.mean(vector, axis=-1, keepdims=True)
    centred = vector - average
    inverse = lax.rsqrt(jnp.mean(centred * centred, axis=-1, keepdims=True) + EPS)
    return centred * inverse, inverse


def norm_back(grad_normed, normed, inverse):
    return inverse * (
        grad_normed
        - jnp.mean(grad_normed, axis=-1, keepdims=True)
        - normed * jnp.mean(grad_normed * normed, axis=-1, keepdims=True)
    )


def rows_sum(value):
    return jnp.sum(value, axis=0, keepdims=True)


def head_masks():
    lane = lax.broadcasted_iota(jnp.int32, (1, BLOCK), 1)
    split = [((lane % HALF) // (HD // 2) == h).astype(F32).astype(BF) for h in range(PACK)]
    plain = [(lane // HD == h).astype(F32).astype(BF) for h in range(PACK)]
    return split, plain


def prep_kernel(
    place, near_ref, far_ref, mod_ref, gain_ref, wq_ref, wk_ref, wv_ref, cos_ref, sin_ref,
    actt_ref, q_ref, k_ref, v_ref,
):
    step = pl.program_id(0)
    rows = near_ref.shape[1]
    source = jnp.where(step < 2, near_ref[0], far_ref[0]).astype(F32)
    normed, _ = normalize(source)
    act = (normed * gain_ref[...] * (1.0 + mod_ref[0, 1:2, :]) + mod_ref[0, 0:1, :]).astype(BF)
    actt_ref[...] = act.T
    cosine, sine = cos_ref[...], sin_ref[...]

    def turned(weight_ref, out_ref, factor):
        for block in range(weight_ref.shape[1] // BLOCK):
            at = block * BLOCK
            both = nn(act, weight_ref[:, at : at + BLOCK])
            front, back = both[:, :HALF], both[:, HALF:]
            out_ref[:, at : at + HALF] = (front * cosine - back * sine).astype(BF) * factor
            out_ref[:, at + HALF : at + BLOCK] = (back * cosine + front * sine).astype(BF) * factor

    @pl.when((place[0] ^ step) * rows < place[1])
    def _():
        turned(wk_ref, k_ref, BF(1.0))
        v_ref[...] = nn(act, wv_ref[...]).astype(BF)

    @pl.when(step == 0)
    def _():
        turned(wq_ref, q_ref, BF(HD**-0.5))


def attend_kernel(place, q_ref, k_ref, v_ref, mix_ref, lse_ref):
    split, plain = head_masks()
    lane = lax.broadcasted_iota(jnp.int32, (1, BLOCK), 1)
    narrow = lax.broadcasted_iota(jnp.int32, (1, 128), 1)

    def work(span):
        queries, keys, values = q_ref[...], k_ref[:span, :], v_ref[:span, :]
        mixed = jnp.zeros(q_ref.shape, F32)
        logs = jnp.zeros((q_ref.shape[0], 128), F32)
        for head in range(PACK):
            scores = nt(queries * split[head], keys)
            top = jnp.max(scores, axis=-1, keepdims=True)
            raised = jnp.exp(scores - top)
            total = jnp.sum(raised, axis=-1, keepdims=True)
            probs = (raised * (1.0 / total)).astype(BF)
            mixed = jnp.where(lane // HD == head, nn(probs, values), mixed)
            logs = jnp.where(narrow == head, top + jnp.log(total), logs)
        mix_ref[...] = mixed.astype(BF)
        lse_ref[0] = logs.T[:8, :]

    for span in SPANS:
        pl.when(place[1] == span)(functools.partial(work, span))


def attend_back_kernel(
    place, q_ref, k_ref, v_ref, g_ref, lse_ref, cosq_ref, sinq_ref, cosk_ref, sink_ref,
    dq_ref, dk_ref, dv_ref,
):
    split, plain = head_masks()
    part = HD // 2

    def unturn(both, cosine, sine, out_ref, span):
        front, back = both[:, :HALF], both[:, HALF:]
        out_ref[:span, :HALF] = (front * cosine + back * sine).astype(BF)
        out_ref[:span, HALF:] = (back * cosine - front * sine).astype(BF)

    def work(span):
        queries, grads = q_ref[...], g_ref[...]
        keys, values = k_ref[:span, :], v_ref[:span, :]
        keys_t = keys.T
        grad_keys = jnp.zeros((span, BLOCK), F32)
        grad_values = jnp.zeros((span, BLOCK), F32)
        fronts, backs = [], []
        for head in range(PACK):
            query, grad = queries * split[head], grads * plain[head]
            probs = jnp.exp(nt(keys, query) - lse_ref[0, head : head + 1, :])
            grad_probs = nt(values, grad)
            inner = rows_sum(probs * grad_probs)
            grad_scores = (probs * (grad_probs - inner)).astype(BF)
            grad_values = grad_values + nn(probs.astype(BF), grad)
            grad_keys = grad_keys + nn(grad_scores, query)
            at = head * part
            rows_t = jnp.concatenate(
                [keys_t[at : at + part], keys_t[HALF + at : HALF + at + part]], axis=0
            )
            grad_query = nn(rows_t, grad_scores)
            fronts.append(grad_query[:part])
            backs.append(grad_query[part:])
        grad_queries = jnp.concatenate(fronts + backs, axis=0).T * HD**-0.5
        unturn(grad_queries, cosq_ref[...], sinq_ref[...], dq_ref, dq_ref.shape[0])
        unturn(grad_keys, cosk_ref[:span, :], sink_ref[:span, :], dk_ref, span)
        dv_ref[:span, :] = grad_values.astype(BF)
        rest = dk_ref.shape[0] - span
        if rest:
            dk_ref[span:, :] = jnp.zeros((rest, BLOCK), BF)
            dv_ref[span:, :] = jnp.zeros((rest, BLOCK), BF)

    for span in SPANS:
        pl.when(place[1] == span)(functools.partial(work, span))


def mlp_kernel(
    mix0_ref, mix1_ref, mix2_ref, tok_ref, cot_ref, mod_ref, gain_ref, wout_ref, bdown_ref,
    wup_ref, bup_ref, wdown_ref,
    out_ref, gres_ref, gmix_ref, dwout_ref, sums_ref, dwup_ref, dwdown_ref, dbup_ref,
    resid, branch, act, act_t, slope, active, second, gsecond, gact, gpre,
):
    step = pl.program_id(0)
    tiles = pl.num_programs(0) // 2
    parts, rows, _ = tok_ref.shape
    mixes = (mix0_ref, mix1_ref, mix2_ref)

    def span(s):
        return slice(s * rows, (s + 1) * rows)

    def mod(s, which):
        return mod_ref[s, which : which + 1, :]

    @pl.when(step == 0)
    def _():
        for s in range(parts):
            one = nn(mixes[s][...], wout_ref[...])
            res = tok_ref[s].astype(F32) + mod(s, 2) * one
            branch[span(s), :] = one
            resid[span(s), :] = res
            normed, _ = normalize(res)
            value = (normed * gain_ref[...] * (1.0 + mod(s, 4)) + mod(s, 3)).astype(BF)
            act[span(s), :] = value
            act_t[:, span(s)] = value.T
            second[span(s), :] = jnp.zeros_like(res)
            gact[span(s), :] = jnp.zeros_like(res)

    @pl.when(step < tiles)
    def _():
        for s in range(parts):
            u = nn(act[span(s), :], wup_ref[...]) + bup_ref[...]
            square = u * u
            bent = jnp.tanh(GELU_C * (u + 0.044715 * (square * u)))
            value = (0.5 * u * (1.0 + bent)).astype(BF)
            slope[step, span(s), :] = 0.5 * (1.0 + bent) + 0.5 * u * (1.0 - bent * bent) * (
                GELU_C * (1.0 + 3 * 0.044715 * square)
            )
            active[step, span(s), :] = value
            second[span(s), :] += nn(value, wdown_ref[...])

    @pl.when(step == tiles - 1)
    def _():
        total = jnp.zeros(bdown_ref.shape, F32)
        for s in range(parts):
            two = second[span(s), :] + bdown_ref[...]
            out_ref[s] = (resid[span(s), :] + mod(s, 5) * two).astype(BF)
            pull = cot_ref[s].astype(F32)
            sums_ref[5 * parts + s : 5 * parts + s + 1, :] = rows_sum(pull * two)
            down = (pull * mod(s, 5)).astype(BF)
            gsecond[span(s), :] = down
            total = total + rows_sum(down.astype(F32))
        sums_ref[6 * parts : 6 * parts + 1, :] = total

    @pl.when(step >= tiles)
    def _():
        at = step - tiles
        total = jnp.zeros(bup_ref.shape, F32)
        for s in range(parts):
            pulled = nt(gsecond[span(s), :], wdown_ref[...])
            value = (pulled * slope[at, span(s), :]).astype(BF)
            gpre[span(s), :] = value
            total = total + rows_sum(value.astype(F32))
            gact[span(s), :] += nt(value, wup_ref[...])
        dbup_ref[...] = total
        dwdown_ref[...] = nn(active[at].T, gsecond[...])
        dwup_ref[...] = nn(act_t[...], gpre[...])

    @pl.when(step == 2 * tiles - 1)
    def _():
        total = jnp.zeros(bdown_ref.shape, F32)
        for s in range(parts):
            normed, inverse = normalize(resid[span(s), :])
            pull = gact[span(s), :]
            sums_ref[3 * parts + s : 3 * parts + s + 1, :] = rows_sum(pull)
            sums_ref[4 * parts + s : 4 * parts + s + 1, :] = rows_sum(
                pull * (normed * gain_ref[...])
            )
            scaled = pull * (1.0 + mod(s, 4))
            total = total + rows_sum(scaled * normed)
            grad = cot_ref[s].astype(F32) + norm_back(scaled * gain_ref[...], normed, inverse)
            gres_ref[s] = grad
            sums_ref[2 * parts + s : 2 * parts + s + 1, :] = rows_sum(grad * branch[span(s), :])
            one = (grad * mod(s, 2)).astype(BF)
            gmix_ref[s] = nt(one, wout_ref[...]).astype(BF)
            outer = nn(mixes[s][...].T, one)
            if s == 0:
                dwout_ref[...] = outer
            else:
                dwout_ref[...] += outer
        sums_ref[6 * parts + 1 : 6 * parts + 2, :] = total


def whole(array):
    rank = array.ndim
    return pl.BlockSpec(array.shape, lambda *_: (0,) * rank, pipeline_mode=pl.Buffered(1))


def limits(mib):
    return pltpu.CompilerParams(vmem_limit_bytes=mib * 2**20)


def cost(flops, bytes_accessed):
    return pl.CostEstimate(flops=int(flops), bytes_accessed=int(bytes_accessed), transcendentals=0)


def prepare(place, near, far, mod, s, gain, wq, wk, wv, cosine, sine):
    _, rows, width = near.shape
    slots = 4 * rows
    table = pl.BlockSpec((rows, HALF), lambda i, p: (p[0] ^ i, 0))
    piece = pl.BlockSpec((rows, width), lambda i, p: (p[0] ^ i, 0))
    return pl.pallas_call(
        prep_kernel,
        grid_spec=pltpu.PrefetchScalarGridSpec(
            num_scalar_prefetch=1,
            grid=(4,),
            in_specs=[
                pl.BlockSpec((1, rows, width), lambda i, p: (jnp.minimum(i, 1), 0, 0)),
                pl.BlockSpec((1, rows, width), lambda i, p: (jnp.maximum(i - 2, 0), 0, 0)),
                pl.BlockSpec((1,) + mod.shape[1:], lambda i, p: (s, 0, 0)),
                whole(gain), whole(wq), whole(wk), whole(wv), table, table,
            ],
            out_specs=[
                pl.BlockSpec((width, rows), lambda i, p: (0, p[0] ^ i)),
                pl.BlockSpec((rows, width), lambda i, p: (0, 0)),
                piece, piece,
            ],
        ),
        out_shape=[
            jax.ShapeDtypeStruct((width, slots), BF),
            jax.ShapeDtypeStruct((rows, width), BF),
            jax.ShapeDtypeStruct((slots, width), BF),
            jax.ShapeDtypeStruct((slots, width), BF),
        ],
        compiler_params=limits(40),
        cost_estimate=cost(2 * slots * width * width * 2.25, 10e6),
    )(place, near, far, mod, gain, wq, wk, wv, cosine, sine)


def attend(place, queries, keys, values):
    rows, width = queries.shape
    slots = keys.shape[0]
    groups = width // BLOCK
    own = pl.BlockSpec((rows, BLOCK), lambda j, p: (0, j))
    full = pl.BlockSpec((slots, BLOCK), lambda j, p: (0, j))
    return pl.pallas_call(
        attend_kernel,
        grid_spec=pltpu.PrefetchScalarGridSpec(
            num_scalar_prefetch=1,
            grid=(groups,),
            in_specs=[own, full, full],
            out_specs=[own, pl.BlockSpec((1, 8, rows), lambda j, p: (j, 0, 0))],
        ),
        out_shape=[
            jax.ShapeDtypeStruct((rows, width), BF),
            jax.ShapeDtypeStruct((groups, 8, rows), F32),
        ],
        compiler_params=limits(40),
        cost_estimate=cost(16 * rows * slots * width, 5e6),
    )(place, queries, keys, values)


def attend_back(place, queries, keys, values, grads, s, logs, cosine, sine):
    rows, width = queries.shape
    slots = keys.shape[0]
    groups = width // BLOCK
    own = pl.BlockSpec((rows, BLOCK), lambda j, p: (0, j))
    full = pl.BlockSpec((slots, BLOCK), lambda j, p: (0, j))
    own_table = pl.BlockSpec((rows, HALF), lambda j, p: (p[0], 0))
    full_table = pl.BlockSpec((slots, HALF), lambda j, p: (0, 0))
    return pl.pallas_call(
        attend_back_kernel,
        grid_spec=pltpu.PrefetchScalarGridSpec(
            num_scalar_prefetch=1,
            grid=(groups,),
            in_specs=[
                own, full, full,
                pl.BlockSpec((None, rows, BLOCK), lambda j, p: (s, 0, j)),
                pl.BlockSpec((1, 8, rows), lambda j, p: (j, 0, 0)),
                own_table, own_table, full_table, full_table,
            ],
            out_specs=[own, full, full],
        ),
        out_shape=[
            jax.ShapeDtypeStruct((rows, width), BF),
            jax.ShapeDtypeStruct((slots, width), BF),
            jax.ShapeDtypeStruct((slots, width), BF),
        ],
        compiler_params=limits(48),
        cost_estimate=cost(40 * rows * slots * width, 9e6),
    )(place, queries, keys, values, grads, logs, cosine, sine, cosine, sine)


def feed_forward(mixes, tokens, pulls, mod, gain, w_out, b_down, w_up, b_up, w_down):
    parts, rows, width = tokens.shape
    hidden = w_up.shape[1]
    tile = 512
    tiles = hidden // tile
    total = parts * rows
    late = lambda i: jnp.maximum(i - tiles, 0)
    wide = pl.BlockSpec((width, tile), lambda i: (0, i % tiles))
    bias = pl.BlockSpec((1, tile), lambda i: (0, i % tiles))
    tall = pl.BlockSpec((tile, width), lambda i: (i % tiles, 0))
    outs = [
        jax.ShapeDtypeStruct(tokens.shape, BF),
        jax.ShapeDtypeStruct(tokens.shape, F32),
        jax.ShapeDtypeStruct(tokens.shape, BF),
        jax.ShapeDtypeStruct((width, width), F32),
        jax.ShapeDtypeStruct((24, width), F32),
        jax.ShapeDtypeStruct((width, hidden), F32),
        jax.ShapeDtypeStruct((hidden, width), F32),
        jax.ShapeDtypeStruct((1, hidden), F32),
    ]
    return pl.pallas_call(
        mlp_kernel,
        grid=(2 * tiles,),
        in_specs=[whole(m) for m in mixes]
        + [whole(a) for a in (tokens, pulls, mod, gain, w_out, b_down)]
        + [wide, bias, tall],
        out_specs=[whole(o) for o in outs[:5]]
        + [
            pl.BlockSpec((width, tile), lambda i: (0, late(i))),
            pl.BlockSpec((tile, width), lambda i: (late(i), 0)),
            pl.BlockSpec((1, tile), lambda i: (0, late(i))),
        ],
        out_shape=outs,
        scratch_shapes=[
            pltpu.VMEM((total, width), F32),
            pltpu.VMEM((total, width), F32),
            pltpu.VMEM((total, width), BF),
            pltpu.VMEM((width, total), BF),
            pltpu.VMEM((tiles, total, tile), F32),
            pltpu.VMEM((tiles, total, tile), BF),
            pltpu.VMEM((total, width), F32),
            pltpu.VMEM((total, width), BF),
            pltpu.VMEM((total, width), F32),
            pltpu.VMEM((total, tile), BF),
        ],
        compiler_params=limits(60),
        cost_estimate=cost(2 * total * width * (6 * hidden + 3 * width), 50e6),
    )(*mixes, tokens, pulls, mod, gain, w_out, b_down, w_up, b_up, w_down)


def split_halves(weight):
    depth, width = weight.shape
    return (
        weight.reshape(depth, width // BLOCK, PACK, 2, HD // 2)
        .transpose(0, 1, 3, 2, 4)
        .reshape(depth, width)
    )


def join_halves(weight):
    depth, width = weight.shape
    return (
        weight.reshape(depth, width // BLOCK, 2, PACK, HD // 2)
        .transpose(0, 1, 3, 2, 4)
        .reshape(depth, width)
    )


def body(
    dp_size, seq_size,
    tokens, cond, lengths, gain_one, gain_two, w_ada, b_ada, w_qkv, w_out, w_up, b_up, w_down,
    b_down, cotangent,
):
    parts, rows, width = tokens.shape
    hidden = w_up.shape[1]
    slots = rows * seq_size
    dp_bits = dp_size.bit_length() - 1
    dp, seq = lax.axis_index("dp"), lax.axis_index("seq")
    core, side = dp & 1, seq // (seq_size // 2)
    stays = core == side
    own = jnp.where(stays, seq, seq ^ 2).astype(jnp.int32)

    def dp_swap(value, bit):
        return lax.ppermute(value, "dp", [(i, i ^ (1 << bit)) for i in range(dp_size)])

    def seq_swap(value, bit):
        return lax.ppermute(value, "seq", [(i, i ^ bit) for i in range(seq_size)])

    pairs = []
    for i in range(dp_size):
        for j in range(seq_size):
            if (i & 1) != j // (seq_size // 2):
                pairs.append((i * seq_size + j, (i ^ 1) * seq_size + (j ^ 2)))

    def regroup(value):
        moved = lax.ppermute(value, ("dp", "seq"), pairs)
        return jnp.where(stays, value, moved)

    cond_here = jnp.where(stays, cond, dp_swap(cond, 0))
    lengths_here = jnp.where(stays, lengths, dp_swap(lengths, 0))
    mod = jnp.dot(cond_here, w_ada, preferred_element_type=F32) + b_ada
    mod = mod.reshape(parts, 6, width)
    places = [jnp.stack([own, lengths_here[s]]).astype(jnp.int32) for s in range(parts)]
    frequency = np.power(10000.0, -np.arange(HD // 2) * 2.0 / HD).astype(np.float32)
    angles = jnp.arange(slots).astype(F32)[:, None] * jnp.asarray(frequency)[None, :]
    cosine = jnp.tile(jnp.cos(angles), (1, PACK))
    sine = jnp.tile(jnp.sin(angles), (1, PACK))
    wq = split_halves(w_qkv[:, :width])
    wk = split_halves(w_qkv[:, width : 2 * width])
    wv = w_qkv[:, 2 * width :]
    gain_one_row, gain_two_row = gain_one[None, :], gain_two[None, :]

    tokens_here, nears, fars = [], [], []
    for s in range(parts):
        mine = regroup(tokens[s])
        near = jnp.stack([mine, seq_swap(mine, 1)])
        tokens_here.append(mine)
        nears.append(near)
        fars.append(dp_swap(near, 0))
    pulls = jnp.stack([regroup(cotangent[s]) for s in range(parts)])

    saved, mixes = [], []
    for s in range(parts):
        act_t, queries, keys, values = prepare(
            places[s], nears[s], fars[s], mod, s, gain_one_row, wq, wk, wv, cosine, sine
        )
        mixture, logs = attend(places[s], queries, keys, values)
        saved.append((act_t, queries, keys, values, logs))
        mixes.append(mixture)

    output, grad_res, grad_mix, dw_out, sums, dw_up, dw_down, db_up = feed_forward(
        mixes, jnp.stack(tokens_here), pulls, mod, gain_two_row, w_out, b_down[None, :],
        w_up, b_up[None, :], w_down,
    )
    output = regroup(output)

    def reduce_rows(weight, bits):
        columns = weight.shape[1]
        piece = weight.shape[0] // (dp_size * seq_size)
        held = weight.reshape((2,) * dp_bits + (2, 2, piece, columns))
        names = [("dp", b) for b in reversed(range(dp_bits))] + [("seq", 1), ("seq", 0)]
        for axis, bit in [("dp", b) for b in bits] + [("seq", 0), ("seq", 1)]:
            at = names.index((axis, bit))
            index = ((dp if axis == "dp" else seq) >> bit) & 1
            keep = lax.dynamic_index_in_dim(held, index, at, keepdims=False)
            send = lax.dynamic_index_in_dim(held, 1 - index, at, keepdims=False).astype(BF)
            got = dp_swap(send, bit) if axis == "dp" else seq_swap(send, 1 << bit)
            held = keep + got.astype(F32)
            names.pop(at)
        return held

    forth = list(range(dp_bits))
    back = [0] + list(reversed(range(1, dp_bits)))
    g_w_down = reduce_rows(dw_down, back)
    g_w_up = reduce_rows(dw_up, forth)
    g_w_out = reduce_rows(dw_out, back)

    grad_tokens, first = [], []
    dw_q = dw_k = dw_v = 0.0
    gain_sum = 0.0
    for s in range(parts):
        act_t, queries, keys, values, logs = saved[s]
        dq, dk, dv = attend_back(
            places[s], queries, keys, values, grad_mix, s, logs, cosine, sine
        )
        dw_q = dw_q + nn(lax.dynamic_slice_in_dim(act_t, own * rows, rows, 1), dq)
        dw_k = dw_k + nn(act_t, dk)
        dw_v = dw_v + nn(act_t, dv)
        share = (nt(dk, wk) + nt(dv, wv)).reshape(seq_size, rows, width)
        pick = lambda k: lax.dynamic_index_in_dim(share, own ^ k, 0, keepdims=False)
        send = jnp.stack([pick(2), pick(3)]).astype(BF)
        got = dp_swap(send, 0).astype(F32)
        here = pick(0) + nt(dq, wq) + got[0]
        there = (pick(1) + got[1]).astype(BF)
        grad_act = here + seq_swap(there, 1).astype(F32)
        source = tokens_here[s].astype(F32)
        normed, inverse = normalize(source)
        scaled = grad_act * (1.0 + mod[s, 1:2, :])
        shift_sum = rows_sum(grad_act)
        scale_sum = rows_sum(grad_act * (normed * gain_one_row))
        gain_sum = gain_sum + rows_sum(scaled * normed)
        first.append((shift_sum, scale_sum))
        grad = grad_res[s] + norm_back(scaled * gain_one_row, normed, inverse)
        moved = lax.ppermute(grad.astype(BF), ("dp", "seq"), pairs)
        grad_tokens.append(jnp.where(stays, grad, moved.astype(F32)))
    dw_qkv = jnp.concatenate([dw_q, dw_k, dw_v], axis=1)
    g_w_qkv = jnp.concatenate(
        [
            reduce_rows(dw_qkv[:, : 3 * width // 2], forth),
            reduce_rows(dw_qkv[:, 3 * width // 2 :], back),
        ],
        axis=1,
    )
    g_w_qkv = jnp.concatenate(
        [
            join_halves(g_w_qkv[:, :width]),
            join_halves(g_w_qkv[:, width : 2 * width]),
            g_w_qkv[:, 2 * width :],
        ],
        axis=1,
    )

    grad_mod = jnp.concatenate(
        [
            jnp.concatenate([f[0] for f in first]),
            jnp.concatenate([f[1] for f in first]),
            sums[2 * parts : 3 * parts],
            sums[3 * parts : 4 * parts],
            sums[4 * parts : 5 * parts],
            sums[5 * parts : 6 * parts],
        ],
        axis=1,
    )
    share = jnp.dot(grad_mod, w_ada.astype(F32).T, precision=HIGH)
    shards = dp_size * seq_size
    cut = lambda v: v.reshape((2,) * dp_bits + (2, 2, -1))
    held = jnp.concatenate(
        [cut(v) for v in (gain_sum, sums[6 * parts + 1], db_up, sums[6 * parts])], axis=-1
    )
    lanes = grad_mod.reshape(parts, shards, -1).transpose(1, 0, 2)
    per = lanes.shape[-1]
    lanes = lanes.reshape((2,) * dp_bits + (2, 2, parts, per))
    conds = cond_here.astype(F32)
    names = [("dp", b) for b in reversed(range(dp_bits))] + [("seq", 1), ("seq", 0)]
    order = [("dp", 0), ("seq", 0), ("seq", 1)] + [("dp", b) for b in range(1, dp_bits)]
    for turn, (axis, bit) in enumerate(order):
        at = names.index((axis, bit))
        index = ((dp if axis == "dp" else seq) >> bit) & 1
        swap = (lambda v: dp_swap(v, bit)) if axis == "dp" else (lambda v: seq_swap(v, 1 << bit))
        pick = lambda v, i: lax.dynamic_index_in_dim(v, i, at, keepdims=False)
        sent = [pick(held, 1 - index), pick(lanes, 1 - index)]
        if turn < 2:
            sent.append(share)
        elif turn == 2:
            sent += [share, conds]
        else:
            sent.append(conds)
        sizes = np.cumsum([v.size for v in sent])[:-1]
        got = swap(jnp.concatenate([v.reshape(-1) for v in sent]))
        got = [g.reshape(v.shape) for g, v in zip(jnp.split(got, sizes), sent)]
        held = pick(held, index) + got[0]
        mine = pick(lanes, index)
        if turn < 2:
            lanes = mine + got[1]
            share = share + got[2]
        else:
            lanes = jnp.concatenate([mine, got[1]], axis=-2)
            conds = jnp.concatenate([conds, got[-1]], axis=0)
            if turn == 2:
                share = jnp.where(stays, share, got[2])
        names.pop(at)
    sizes = np.cumsum([width // shards, width // shards, hidden // shards])
    g_gain_one, g_gain_two, g_b_up, g_b_down = jnp.split(held, sizes)
    g_w_ada = jnp.dot(conds.T, lanes, precision=HIGH)
    g_b_ada = jnp.sum(lanes, axis=0)
    return (
        output,
        jnp.stack(grad_tokens),
        share,
        g_gain_one,
        g_gain_two,
        g_w_ada,
        g_b_ada,
        g_w_qkv,
        g_w_out,
        g_w_up,
        g_b_up,
        g_w_down,
        g_b_down,
    )


def solution(mesh):
    shards = ("dp", "seq")
    placed = (
        (P("dp", "seq", None), P("dp", None), P("dp"))
        + (P(),) * 10
        + (P("dp", "seq", None),)
    )
    return jax.shard_map(
        functools.partial(body, mesh.shape["dp"], mesh.shape["seq"]),
        mesh=mesh,
        in_specs=placed,
        out_specs=(
            P("dp", "seq", None),
            P("dp", "seq", None),
            P("dp", None),
            P(shards),
            P(shards),
            P(None, shards),
            P(shards),
            P(shards, None),
            P(shards, None),
            P(shards, None),
            P(shards),
            P(shards, None),
            P(shards),
        ),
        check_vma=False,
    )
```

```python
import functools

import jax
import jax.numpy as jnp
import numpy as np
from jax import lax
from jax.experimental import pallas as pl
from jax.experimental.pallas import tpu as pltpu
from jax.sharding import PartitionSpec as P

HEADS = 12
HD = 64
EPS = 1e-05
HIGH = lax.Precision.HIGHEST
BF = jnp.bfloat16
F32 = jnp.float32
PACK = 4
BLOCK = PACK * HD
LANES = 128
SPANS = (128, 512, 1024)
GELU_C = float(np.sqrt(2.0 / np.pi))


def nn(left, right):
    return lax.dot_general(left, right, (((1,), (0,)), ((), ())), preferred_element_type=F32)


def nt(left, right):
    return lax.dot_general(left, right, (((1,), (1,)), ((), ())), preferred_element_type=F32)


def normalize(vector):
    average = jnp.mean(vector, axis=-1, keepdims=True)
    centred = vector - average
    inverse = lax.rsqrt(jnp.mean(centred * centred, axis=-1, keepdims=True) + EPS)
    return centred * inverse, inverse


def norm_back(grad_normed, normed, inverse):
    return inverse * (
        grad_normed
        - jnp.mean(grad_normed, axis=-1, keepdims=True)
        - normed * jnp.mean(grad_normed * normed, axis=-1, keepdims=True)
    )


def rows_sum(value):
    return jnp.sum(value, axis=0, keepdims=True)


def head_masks():
    lane = lax.broadcasted_iota(jnp.int32, (1, BLOCK), 1)
    return [(lane // HD == h).astype(F32).astype(BF) for h in range(PACK)]


def swap_halves(value):
    half = HD // 2
    lane = lax.broadcasted_iota(jnp.int32, value.shape, 1)
    ahead = pltpu.roll(value, LANES - half, 1)
    behind = pltpu.roll(value, half, 1)
    return jnp.where(lane % HD < half, ahead, behind)


def prep_kernel(
    place, a_ref, b_ref, c_ref, d_ref, mod_ref, gain_ref, w_ref, cos_ref, sin_ref,
    actt_ref, q_ref, k_ref, v_ref,
):
    step = pl.program_id(0)
    rows, width = a_ref.shape
    source = jnp.where(
        step < 2,
        jnp.where(step == 0, a_ref[...], b_ref[...]),
        jnp.where(step == 2, c_ref[...], d_ref[...]),
    ).astype(F32)
    normed, _ = normalize(source)
    act = (normed * gain_ref[...] * (1.0 + mod_ref[0, 1:2, :]) + mod_ref[0, 0:1, :]).astype(BF)
    actt_ref[...] = act.T
    cosine, sine = cos_ref[...], sin_ref[...]

    def turned(start, out_ref, factor):
        for at in range(0, width, BLOCK):
            both = nn(act, w_ref[:, start + at : start + at + BLOCK])
            for lane in range(0, BLOCK, LANES):
                part = both[:, lane : lane + LANES]
                out_ref[:, at + lane : at + lane + LANES] = (
                    part * cosine + swap_halves(part) * sine
                ).astype(BF) * factor

    @pl.when((place[0] ^ step) * rows < place[1])
    def _():
        turned(width, k_ref, BF(1.0))
        v_ref[...] = nn(act, w_ref[:, 2 * width :]).astype(BF)

    @pl.when(step == 0)
    def _():
        turned(0, q_ref, BF(HD**-0.5))


def attend_kernel(place, q_ref, k_ref, v_ref, mix_ref, lse_ref):
    masks = head_masks()
    lane = lax.broadcasted_iota(jnp.int32, (1, BLOCK), 1)
    narrow = lax.broadcasted_iota(jnp.int32, (1, LANES), 1)

    def work(span):
        queries, keys, values = q_ref[...], k_ref[:span, :], v_ref[:span, :]
        mixed = jnp.zeros(q_ref.shape, F32)
        logs = jnp.zeros((q_ref.shape[0], LANES), F32)
        for head in range(PACK):
            scores = nt(queries * masks[head], keys)
            top = jnp.max(scores, axis=-1, keepdims=True)
            raised = jnp.exp(scores - top)
            total = jnp.sum(raised, axis=-1, keepdims=True)
            probs = (raised * (1.0 / total)).astype(BF)
            mixed = jnp.where(lane // HD == head, nn(probs, values), mixed)
            logs = jnp.where(narrow == head, top + jnp.log(total), logs)
        mix_ref[...] = mixed.astype(BF)
        lse_ref[0] = logs.T[:8, :]

    for span in SPANS:
        pl.when(place[1] == span)(functools.partial(work, span))


def attend_back_kernel(
    more, last, place, q_ref, k_ref, v_ref, g_ref, lse_ref, cosq_ref, sinq_ref, cosk_ref, sink_ref,
    wq_ref, wk_ref, wv_ref, actt_ref, owns_ref, *refs,
):
    refs = list(refs)
    before_ref = refs.pop(0) if more else None
    keep_ref, send_ref = refs.pop(0), refs.pop(0)
    outs = [refs.pop(0) for _ in range(4 if last else 1)]
    share, own_share, grad_q, grad_k, grad_v, weights = refs
    masks = head_masks()
    group = pl.program_id(0)
    rows = q_ref.shape[0]

    def unturn(value, cosine, sine, out_ref, span):
        for lane in range(0, BLOCK, LANES):
            part = value[:, lane : lane + LANES]
            out_ref[:span, lane : lane + LANES] = (
                part * cosine - swap_halves(part) * sine
            ).astype(BF)

    @pl.when(group == 0)
    def _():
        share[...] = jnp.zeros_like(share)
        own_share[...] = jnp.zeros_like(own_share)

    def work(span):
        queries, grads = q_ref[...], g_ref[...]
        keys, values = k_ref[:span, :], v_ref[:span, :]
        keys_t = keys.T
        grad_keys = jnp.zeros((span, BLOCK), F32)
        grad_values = jnp.zeros((span, BLOCK), F32)
        turned = []
        for head in range(PACK):
            query, grad = queries * masks[head], grads * masks[head]
            probs = jnp.exp(nt(keys, query) - lse_ref[0, head : head + 1, :])
            grad_probs = nt(values, grad)
            inner = rows_sum(probs * grad_probs)
            grad_scores = (probs * (grad_probs - inner)).astype(BF)
            grad_values = grad_values + nn(probs.astype(BF), grad)
            grad_keys = grad_keys + nn(grad_scores, query)
            turned.append(nn(keys_t[head * HD : (head + 1) * HD], grad_scores))
        grad_queries = jnp.concatenate(turned, axis=0).T * HD**-0.5
        unturn(grad_queries, cosq_ref[...], sinq_ref[...], grad_q, rows)
        unturn(grad_keys, cosk_ref[:span, :], sink_ref[:span, :], grad_k, span)
        grad_v[:span, :] = grad_values.astype(BF)
        share[:span, :] += nt(grad_k[:span, :], wk_ref[...]) + nt(grad_v[:span, :], wv_ref[...])
        act = actt_ref[:, :span]
        products = (
            nn(owns_ref[...], grad_q[...]),
            nn(act, grad_k[:span, :]),
            nn(act, grad_v[:span, :]),
        )
        for which, product in enumerate(products):
            lanes = slice(which * BLOCK, (which + 1) * BLOCK)
            if more:
                product = product + before_ref[0, :, lanes]
            if last:
                weights[:, lanes] = product
            else:
                outs[0][0, :, lanes] = product

    for span in SPANS:
        pl.when(place[1] == span)(functools.partial(work, span))
    own_share[...] += nt(grad_q[...], wq_ref[...])
    if last:
        cut = 2 * BLOCK + LANES
        first = jnp.concatenate([weights[:, :BLOCK], weights[:, 2 * BLOCK : cut]], axis=1)
        other = jnp.concatenate([weights[:, BLOCK : 2 * BLOCK], weights[:, cut:]], axis=1)
        part_rows(first, place[2], outs[0], outs[1])
        part_rows(other, place[2], outs[2], outs[3])

    @pl.when(group == pl.num_programs(0) - 1)
    def _():
        def piece(k):
            return share[pl.ds(pl.multiple_of((place[0] ^ k) * rows, rows), rows), :]

        keep_ref[0] = piece(0) + own_share[...]
        keep_ref[1] = piece(1)
        send_ref[0] = piece(2).astype(BF)
        send_ref[1] = piece(3).astype(BF)


def norm_back_kernel(
    keep_ref, core_ref, near_ref, tok_ref, gres_ref, mod_ref, gain_ref,
    grad_ref, send_ref, sums_ref,
):
    pull = keep_ref[0] + core_ref[0].astype(F32) + near_ref[...].astype(F32)
    normed, inverse = normalize(tok_ref[...].astype(F32))
    gain = gain_ref[...]
    sums_ref[...] = jnp.zeros_like(sums_ref)
    sums_ref[0:1, :] = rows_sum(pull)
    sums_ref[1:2, :] = rows_sum(pull * (normed * gain))
    scaled = pull * (1.0 + mod_ref[0, 1:2, :])
    sums_ref[2:3, :] = rows_sum(scaled * normed)
    grad = gres_ref[0] + norm_back(scaled * gain, normed, inverse)
    grad_ref[...] = grad
    send_ref[...] = grad.astype(BF)


def part_rows(value, core, keep_ref, send_ref):
    blocks, piece, columns = keep_ref.shape
    both = value.reshape(blocks, 2, piece, columns)
    keep_ref[...] = jnp.where(core == 0, both[:, 0], both[:, 1])
    send_ref[...] = jnp.where(core == 0, both[:, 1], both[:, 0]).astype(BF)


def combine_kernel(index, mine_ref, got_ref, other_ref, other_got_ref, keep_ref, send_ref):
    keep_ref[...] = mine_ref[...] + got_ref[...].astype(F32)
    send_ref[...] = (other_ref[...] + other_got_ref[...].astype(F32)).astype(BF)


def mlp_kernel(
    core, mix0_ref, mix1_ref, mix2_ref, tok_ref, cot_ref, mod_ref, gain_ref, wout_ref, bdown_ref,
    wup_ref, bup_ref, wdown_ref,
    out_ref, gres_ref, gmix_ref, sums_ref,
    keepup_ref, sendup_ref, keepdown_ref, senddown_ref, dbup_ref,
    resid, branch, act, act_t, slope, active, second, gsecond, gact, gpre,
):
    step = pl.program_id(0)
    tiles = pl.num_programs(0) // 2
    parts, rows, _ = tok_ref.shape
    mixes = (mix0_ref, mix1_ref, mix2_ref)

    def span(s):
        return slice(s * rows, (s + 1) * rows)

    def mod(s, which):
        return mod_ref[s, which : which + 1, :]

    @pl.when(step == 0)
    def _():
        for s in range(parts):
            one = nn(mixes[s][...], wout_ref[...])
            res = tok_ref[s].astype(F32) + mod(s, 2) * one
            branch[span(s), :] = one
            resid[span(s), :] = res
            normed, _ = normalize(res)
            value = (normed * gain_ref[...] * (1.0 + mod(s, 4)) + mod(s, 3)).astype(BF)
            act[span(s), :] = value
            act_t[:, span(s)] = value.T
            second[span(s), :] = jnp.zeros_like(res)
            gact[span(s), :] = jnp.zeros_like(res)

    @pl.when(step < tiles)
    def _():
        for s in range(parts):
            u = nn(act[span(s), :], wup_ref[...]) + bup_ref[...]
            square = u * u
            bent = jnp.tanh(GELU_C * (u + 0.044715 * (square * u)))
            value = (0.5 * u * (1.0 + bent)).astype(BF)
            slope[step, span(s), :] = 0.5 * (1.0 + bent) + 0.5 * u * (1.0 - bent * bent) * (
                GELU_C * (1.0 + 3 * 0.044715 * square)
            )
            active[step, span(s), :] = value
            second[span(s), :] += nn(value, wdown_ref[...])

    @pl.when(step == tiles - 1)
    def _():
        total = jnp.zeros(bdown_ref.shape, F32)
        for s in range(parts):
            two = second[span(s), :] + bdown_ref[...]
            out_ref[s] = (resid[span(s), :] + mod(s, 5) * two).astype(BF)
            pull = cot_ref[s].astype(F32)
            sums_ref[5 * parts + s : 5 * parts + s + 1, :] = rows_sum(pull * two)
            down = (pull * mod(s, 5)).astype(BF)
            gsecond[span(s), :] = down
            total = total + rows_sum(down.astype(F32))
        sums_ref[6 * parts : 6 * parts + 1, :] = total

    @pl.when((step >= tiles) & (step < 2 * tiles))
    def _():
        at = step - tiles
        total = jnp.zeros(bup_ref.shape, F32)
        for s in range(parts):
            pulled = nt(gsecond[span(s), :], wdown_ref[...])
            value = (pulled * slope[at, span(s), :]).astype(BF)
            gpre[span(s), :] = value
            total = total + rows_sum(value.astype(F32))
            gact[span(s), :] += nt(value, wup_ref[...])
        dbup_ref[...] = total
        part_rows(nn(active[at].T, gsecond[...]), core[0], keepdown_ref, senddown_ref)
        part_rows(nn(act_t[...], gpre[...]), core[0], keepup_ref, sendup_ref)

    @pl.when(step == 2 * tiles)
    def _():
        total = jnp.zeros(bdown_ref.shape, F32)
        outer = jnp.zeros(resid.shape[1:] * 2, F32)
        for s in range(parts):
            normed, inverse = normalize(resid[span(s), :])
            pull = gact[span(s), :]
            sums_ref[3 * parts + s : 3 * parts + s + 1, :] = rows_sum(pull)
            sums_ref[4 * parts + s : 4 * parts + s + 1, :] = rows_sum(
                pull * (normed * gain_ref[...])
            )
            scaled = pull * (1.0 + mod(s, 4))
            total = total + rows_sum(scaled * normed)
            grad = cot_ref[s].astype(F32) + norm_back(scaled * gain_ref[...], normed, inverse)
            gres_ref[s] = grad
            sums_ref[2 * parts + s : 2 * parts + s + 1, :] = rows_sum(grad * branch[span(s), :])
            one = (grad * mod(s, 2)).astype(BF)
            gmix_ref[s] = nt(one, wout_ref[...]).astype(BF)
            outer = outer + nn(mixes[s][...].T, one)
        part_rows(outer, core[0], keepup_ref, sendup_ref)
        sums_ref[6 * parts + 1 : 6 * parts + 2, :] = total


def whole(array):
    rank = array.ndim
    return pl.BlockSpec(array.shape, lambda *_: (0,) * rank, pipeline_mode=pl.Buffered(1))


def limits(mib=60):
    return pltpu.CompilerParams(vmem_limit_bytes=mib * 2**20)


def cost(flops, bytes_accessed):
    return pl.CostEstimate(
        flops=int(flops) // 8, bytes_accessed=int(bytes_accessed) // 8, transcendentals=0
    )


def prepare(place, pieces, mod, s, gain, w_qkv, cosine, sine):
    rows, width = pieces[0].shape
    slots = 4 * rows
    table = pl.BlockSpec((rows, LANES), lambda i, p: (p[0] ^ i, 0))
    piece = pl.BlockSpec((rows, width), lambda i, p: (p[0] ^ i, 0))
    return pl.pallas_call(
        prep_kernel,
        grid_spec=pltpu.PrefetchScalarGridSpec(
            num_scalar_prefetch=1,
            grid=(4,),
            in_specs=[whole(a) for a in pieces]
            + [pl.BlockSpec((1,) + mod.shape[1:], lambda i, p: (s, 0, 0))]
            + [whole(gain), whole(w_qkv), table, table],
            out_specs=[
                pl.BlockSpec((width, rows), lambda i, p: (0, p[0] ^ i)),
                pl.BlockSpec((rows, width), lambda i, p: (0, 0)),
                piece, piece,
            ],
        ),
        out_shape=[
            jax.ShapeDtypeStruct((width, slots), BF),
            jax.ShapeDtypeStruct((rows, width), BF),
            jax.ShapeDtypeStruct((slots, width), BF),
            jax.ShapeDtypeStruct((slots, width), BF),
        ],
        compiler_params=limits(32),
        cost_estimate=cost(2 * slots * width * width * 2.25, 10e6),
        name="prepare",
    )(place, *pieces, mod, gain, w_qkv, cosine, sine)


def attend(place, queries, keys, values):
    rows, width = queries.shape
    slots = keys.shape[0]
    groups = width // BLOCK
    own = pl.BlockSpec((rows, BLOCK), lambda j, p: (0, j))
    full = pl.BlockSpec((slots, BLOCK), lambda j, p: (0, j))
    return pl.pallas_call(
        attend_kernel,
        grid_spec=pltpu.PrefetchScalarGridSpec(
            num_scalar_prefetch=1,
            grid=(groups,),
            in_specs=[own, full, full],
            out_specs=[own, pl.BlockSpec((1, 8, rows), lambda j, p: (j, 0, 0))],
        ),
        out_shape=[
            jax.ShapeDtypeStruct((rows, width), BF),
            jax.ShapeDtypeStruct((groups, 8, rows), F32),
        ],
        compiler_params=limits(32),
        cost_estimate=cost(16 * rows * slots * width, 5e6),
        name="attend",
    )(place, queries, keys, values)


def attend_back(
    place, queries, keys, values, grads, s, logs, cosine, sine, w_qkv, act_t, before, last, dp_size
):
    rows, width = queries.shape
    slots = keys.shape[0]
    groups = width // BLOCK
    own = pl.BlockSpec((rows, BLOCK), lambda j, p: (0, j))
    full = pl.BlockSpec((slots, BLOCK), lambda j, p: (0, j))
    own_table = pl.BlockSpec((rows, LANES), lambda j, p: (p[0], 0))
    full_table = pl.BlockSpec((slots, LANES), lambda j, p: (0, 0))
    every = pl.BlockSpec((1, width, 3 * BLOCK), lambda j, p: (j, 0, 0))
    blocks, piece, columns = dp_size // 2, width // dp_size, BLOCK + LANES
    more = before is not None
    if last:
        part = (blocks, piece, groups * columns)
        weight_specs = [pl.BlockSpec((blocks, piece, columns), lambda j, p: (0, 0, j))] * 4
        weight_shapes = [jax.ShapeDtypeStruct(part, F32), jax.ShapeDtypeStruct(part, BF)] * 2
    else:
        weight_specs = [every]
        weight_shapes = [jax.ShapeDtypeStruct((groups, width, 3 * BLOCK), F32)]
    return pl.pallas_call(
        functools.partial(attend_back_kernel, more, last),
        grid_spec=pltpu.PrefetchScalarGridSpec(
            num_scalar_prefetch=1,
            grid=(groups,),
            in_specs=[
                own, full, full,
                pl.BlockSpec((None, rows, BLOCK), lambda j, p: (s, 0, j)),
                pl.BlockSpec((1, 8, rows), lambda j, p: (j, 0, 0)),
                own_table, own_table, full_table, full_table,
                pl.BlockSpec((width, BLOCK), lambda j, p: (0, j)),
                pl.BlockSpec((width, BLOCK), lambda j, p: (0, groups + j)),
                pl.BlockSpec((width, BLOCK), lambda j, p: (0, 2 * groups + j)),
                whole(act_t),
                pl.BlockSpec((width, rows), lambda j, p: (0, p[0])),
            ]
            + [every] * more,
            out_specs=[pl.BlockSpec((2, rows, width), lambda j, p: (0, 0, 0))] * 2 + weight_specs,
            scratch_shapes=[
                pltpu.VMEM((slots, width), F32),
                pltpu.VMEM((rows, width), F32),
                pltpu.VMEM((rows, BLOCK), BF),
                pltpu.VMEM((slots, BLOCK), BF),
                pltpu.VMEM((slots, BLOCK), BF),
                pltpu.VMEM((width, 3 * BLOCK), F32),
            ],
        ),
        out_shape=[
            jax.ShapeDtypeStruct((2, rows, width), F32),
            jax.ShapeDtypeStruct((2, rows, width), BF),
        ]
        + weight_shapes,
        compiler_params=limits(),
        cost_estimate=cost(60 * rows * slots * width, 12e6),
        name="attend_back",
    )(
        place, queries, keys, values, grads, logs, cosine, sine, cosine, sine, w_qkv, w_qkv, w_qkv,
        act_t, act_t, *([before] if more else []),
    )


def norm_one_back(keep, core_got, near_got, tokens, grad_res, s, mod, gain):
    rows, width = tokens.shape
    first = pl.BlockSpec((1, rows, width), lambda i: (0, 0, 0))
    return pl.pallas_call(
        norm_back_kernel,
        grid=(1,),
        in_specs=[
            first, first, whole(near_got), whole(tokens),
            pl.BlockSpec((1, rows, width), lambda i: (s, 0, 0)),
            pl.BlockSpec((1,) + mod.shape[1:], lambda i: (s, 0, 0)),
            whole(gain),
        ],
        out_specs=[pl.BlockSpec((rows, width), lambda i: (0, 0))] * 2
        + [pl.BlockSpec((8, width), lambda i: (0, 0))],
        out_shape=[
            jax.ShapeDtypeStruct((rows, width), F32),
            jax.ShapeDtypeStruct((rows, width), BF),
            jax.ShapeDtypeStruct((8, width), F32),
        ],
        compiler_params=limits(32),
        cost_estimate=cost(40 * rows * width, 6e6),
        name="norm_one_back",
    )(keep, core_got, near_got, tokens, grad_res, mod, gain)


def feed_forward(core, mixes, tokens, pulls, mod, gain, w_out, b_down, w_up, b_up, w_down, dp_size):
    parts, rows, width = tokens.shape
    hidden = w_up.shape[1]
    tile = width
    tiles = hidden // tile
    total = parts * rows
    blocks, piece = dp_size // 2, width // dp_size
    tall_piece = hidden // dp_size
    per_tile = tile // (2 * tall_piece)
    late = lambda i: jnp.maximum(i - tiles, 0)
    last = lambda i: jnp.minimum(late(i), tiles - 1)
    turn = lambda i: jnp.minimum(jnp.where(i < tiles, i, i - tiles), tiles - 1)
    wide = pl.BlockSpec((width, tile), lambda i, c: (0, turn(i)))
    bias = pl.BlockSpec((1, tile), lambda i, c: (0, turn(i)))
    tall = pl.BlockSpec((tile, width), lambda i, c: (turn(i), 0))
    out_wide = pl.BlockSpec((blocks, piece, tile), lambda i, c: (0, 0, late(i)))
    out_tall = pl.BlockSpec((per_tile, tall_piece, width), lambda i, c: (last(i), 0, 0))
    outs = [
        jax.ShapeDtypeStruct(tokens.shape, BF),
        jax.ShapeDtypeStruct(tokens.shape, F32),
        jax.ShapeDtypeStruct(tokens.shape, BF),
        jax.ShapeDtypeStruct((24, width), F32),
        jax.ShapeDtypeStruct((blocks, piece, hidden + width), F32),
        jax.ShapeDtypeStruct((blocks, piece, hidden + width), BF),
        jax.ShapeDtypeStruct((blocks, tall_piece, width), F32),
        jax.ShapeDtypeStruct((blocks, tall_piece, width), BF),
        jax.ShapeDtypeStruct((1, hidden), F32),
    ]
    return pl.pallas_call(
        mlp_kernel,
        grid_spec=pltpu.PrefetchScalarGridSpec(
            num_scalar_prefetch=1,
            grid=(2 * tiles + 1,),
            in_specs=[whole(m) for m in mixes]
            + [whole(a) for a in (tokens, pulls, mod, gain, w_out, b_down)]
            + [wide, bias, tall],
            out_specs=[whole(o) for o in outs[:4]]
            + [out_wide, out_wide, out_tall, out_tall]
            + [pl.BlockSpec((1, tile), lambda i, c: (0, last(i)))],
            scratch_shapes=[
                pltpu.VMEM((total, width), F32),
                pltpu.VMEM((total, width), F32),
                pltpu.VMEM((total, width), BF),
                pltpu.VMEM((width, total), BF),
                pltpu.VMEM((tiles, total, tile), F32),
                pltpu.VMEM((tiles, total, tile), BF),
                pltpu.VMEM((total, width), F32),
                pltpu.VMEM((total, width), BF),
                pltpu.VMEM((total, width), F32),
                pltpu.VMEM((total, tile), BF),
            ],
        ),
        out_shape=outs,
        compiler_params=limits(),
        cost_estimate=cost(2 * total * width * (6 * hidden + 3 * width), 50e6),
        name="feed_forward",
    )(core, *mixes, tokens, pulls, mod, gain, w_out, b_down, w_up, b_up, w_down)


def combine(index, keep, got):
    above, _, below, rows, columns = keep.shape
    tile = columns
    while tile * rows > 2**17 and tile % 256 == 0:
        tile //= 2
    block = (None, None, None, rows, tile)
    mine = pl.BlockSpec(block, lambda a, b, c, p: (a, p[0], b, 0, c))
    other = pl.BlockSpec(block, lambda a, b, c, p: (a, 1 - p[0], b, 0, c))
    out = pl.BlockSpec((None, None, rows, tile), lambda a, b, c, p: (a, b, 0, c))
    shape = (above, below, rows, columns)
    return pl.pallas_call(
        combine_kernel,
        grid_spec=pltpu.PrefetchScalarGridSpec(
            num_scalar_prefetch=1,
            grid=(above, below, columns // tile),
            in_specs=[mine, mine, other, other],
            out_specs=[out, out],
        ),
        out_shape=[jax.ShapeDtypeStruct(shape, F32), jax.ShapeDtypeStruct(shape, BF)],
        compiler_params=limits(32),
        cost_estimate=cost(keep.size * 2, keep.size * 9),
        name="combine",
    )(index, keep, got, keep, got)


def after(value, *others):
    return lax.optimization_barrier((value,) + others)[0]


def body(
    dp_size, seq_size,
    tokens, cond, lengths, gain_one, gain_two, w_ada, b_ada, w_qkv, w_out, w_up, b_up, w_down,
    b_down, cotangent,
):
    parts, rows, width = tokens.shape
    hidden = w_up.shape[1]
    slots = rows * seq_size
    dp_bits = dp_size.bit_length() - 1
    dp, seq = lax.axis_index("dp"), lax.axis_index("seq")
    core, side = dp & 1, seq // (seq_size // 2)
    stays = core == side
    own = jnp.where(stays, seq, seq ^ 2).astype(jnp.int32)

    def dp_swap(value, bit):
        return lax.ppermute(value, "dp", [(i, i ^ (1 << bit)) for i in range(dp_size)])

    def seq_swap(value, bit):
        return lax.ppermute(value, "seq", [(i, i ^ (1 << bit)) for i in range(seq_size)])

    def swap(value, axis, bit):
        return dp_swap(value, bit) if axis == "dp" else seq_swap(value, bit)

    def bit_of(axis, bit):
        return ((dp if axis == "dp" else seq) >> bit) & 1

    pairs = []
    for i in range(dp_size):
        for j in range(seq_size):
            if (i & 1) != j // (seq_size // 2):
                pairs.append((i * seq_size + j, (i ^ 1) * seq_size + (j ^ 2)))

    def regroup(value, moving=None):
        moved = lax.ppermute(value if moving is None else moving, ("dp", "seq"), pairs)
        return jnp.where(stays, value, moved.astype(value.dtype))

    both = jnp.concatenate([cond.astype(F32), lengths.astype(F32)[:, None]], axis=1)
    both = jnp.where(stays, both, dp_swap(both, 0))
    cond_here, lengths_here = both[:, :-1].astype(BF), both[:, -1].astype(jnp.int32)
    mine = [None] * parts
    mine[0] = regroup(after(tokens[0], both))
    mod = jnp.dot(cond_here, w_ada, preferred_element_type=F32) + b_ada
    mod = mod.reshape(parts, 6, width)
    places = [jnp.stack([own, lengths_here[s], core]).astype(jnp.int32) for s in range(parts)]
    core_index = core.astype(jnp.int32)[None]
    frequency = np.power(10000.0, -np.arange(HD // 2) * 2.0 / HD).astype(np.float32)
    angles = np.arange(slots).astype(np.float32)[:, None] * frequency[None, :]
    angles = angles.astype(np.float64)
    cosine = jnp.asarray(np.tile(np.cos(angles), (1, LANES // (HD // 2))).astype(np.float32))
    sine = np.sin(angles)
    sine = jnp.asarray(np.tile(np.concatenate([-sine, sine], 1), (1, LANES // HD)).astype(np.float32))
    gain_one_row, gain_two_row = gain_one[None, :], gain_two[None, :]

    saved, mixes = [], []
    here = after(mine[0], mod, *places)
    near = seq_swap(here, 0)
    mine[1] = regroup(after(tokens[1], here))
    group = (here, near, dp_swap(here, 0), dp_swap(near, 0))
    for s in range(parts):
        mine[s] = here
        last = s == parts - 1
        if not last:
            here = after(mine[s + 1], near)
            near = seq_swap(here, 0)
            ahead = tokens[s + 2] if s + 2 < parts else cotangent
            moving = regroup(after(ahead, here))
            if s + 2 < parts:
                mine[s + 2] = moving
            else:
                pulls = moving
        act_t, queries, keys, values = prepare(
            places[s], group, mod, s, gain_one_row, w_qkv, cosine, sine
        )
        if not last:
            far_here = dp_swap(here, 0)
        mixture, logs = attend(places[s], queries, keys, values)
        saved.append((act_t, queries, keys, values, logs))
        mixes.append(mixture)
        if not last:
            near = after(near, mixture)
            group = lax.optimization_barrier((here, near, far_here, dp_swap(near, 0), mixture))[:4]

    output, grad_res, grad_mix, sums, keep_up, send_up, keep_down, send_down, db_up = feed_forward(
        core_index, mixes, jnp.stack(mine), pulls, mod, gain_two_row, w_out,
        b_down[None, :], w_up, b_up[None, :], w_down, dp_size,
    )
    output = regroup(output)

    class Halving:
        def __init__(self, keep, send, order):
            self.keep, self.send = keep, send
            self.order = order + [("seq", 0), ("seq", 1)]
            self.at = ("dp", 0)
            self.names = [("dp", b) for b in reversed(range(1, dp_bits))]
            self.columns = keep.shape[-1]
            self.rows = keep.shape[-2]
            self.got = None

        def move(self):
            self.got = swap(self.send, *self.at)

        def merge(self):
            if not self.order:
                return self.keep.reshape(self.got.shape) + self.got.astype(F32)
            self.at = self.order.pop(0)
            if not self.names:
                self.names = [("seq", 1), ("seq", 0)]
                self.rows //= seq_size
            place = self.names.index(self.at)
            shape = (2**place, 2, 2 ** (len(self.names) - place - 1), self.rows, self.columns)
            self.names.pop(place)
            index = bit_of(*self.at).astype(jnp.int32)[None]
            self.keep, self.send = combine(
                index, self.keep.reshape(shape), self.got.reshape(shape)
            )

    forth = [("dp", b) for b in range(1, dp_bits)]
    back = forth[::-1]
    wide, tall = Halving(keep_up, send_up, forth), Halving(keep_down, send_down, back)
    wide.move()
    tall.move()

    def advance(*streams):
        for stream in streams:
            if stream.got is not None:
                stream.merge()
                stream.move()
        return [stream.send for stream in streams]

    shares, cores, nears = [], [], []

    def pass_on(s):
        there = (shares[s][0][1] + cores[s][1].astype(F32)).astype(BF)
        nears.append(seq_swap(there, 0))
        return there

    waits = []
    for s in range(parts):
        act_t, queries, keys, values, logs = saved[s]
        if s:
            waits = advance(wide, tall)
            cores.append(dp_swap(shares[-1][1], 0))
            waits.append(shares[-1][1])
        if s > 1:
            waits.append(pass_on(s - 2))
        if s == parts - 1:
            waits.append(output)
        keep, send, *weights = attend_back(
            places[s], after(queries, *waits), keys, values, grad_mix, s, logs, cosine, sine, w_qkv,
            act_t, weights[0] if s else None, s == parts - 1, dp_size,
        )
        shares.append((keep, send))

    first, grad_tokens = [], []

    def finish(s):
        grad, rounded, triple = norm_one_back(
            shares[s][0], cores[s], nears[s], mine[s], grad_res, s, mod, gain_one_row
        )
        first.append(triple)
        grad_tokens.append(regroup(grad, rounded))
        return rounded

    one, other = Halving(*weights[:2], forth), Halving(*weights[2:], back)
    one.move()
    other.move()
    cores.append(dp_swap(shares[-1][1], 0))
    pass_on(parts - 2)
    pass_on(parts - 1)
    for s in range(parts):
        finish(s)
    while wide.order:
        advance(wide, tall)
    g_wide, g_tall = wide.merge(), tall.merge()
    while one.order:
        advance(one, other)
    g_one, g_other = one.merge(), other.merge()
    piece = width // (dp_size * seq_size)
    g_wide = g_wide.reshape(piece, hidden + width)
    g_w_up, g_w_out = g_wide[:, :hidden], g_wide[:, hidden:]
    g_w_down = g_tall.reshape(hidden // (dp_size * seq_size), width)
    cut = lambda v: v.reshape(piece, width // BLOCK, BLOCK + LANES)
    g_one, g_other = cut(g_one), cut(g_other)
    g_w_qkv = jnp.concatenate(
        [
            g_one[..., :BLOCK].reshape(piece, width),
            g_other[..., :BLOCK].reshape(piece, width),
            jnp.concatenate([g_one[..., BLOCK:], g_other[..., BLOCK:]], axis=-1).reshape(
                piece, width
            ),
        ],
        axis=1,
    )

    blocks = jnp.stack([t[0] for t in first] + [t[1] for t in first])
    ours = jnp.concatenate([blocks, sums[2 * parts : 6 * parts]])
    totals = jnp.concatenate(
        [
            sum(t[2] for t in first)[None],
            sums[6 * parts : 6 * parts + 2],
            db_up.reshape(hidden // width, width),
        ]
    )
    held = jnp.concatenate([ours, totals])
    for axis in ("dp", "seq"):
        held = held + swap(held, axis, 0)
    count = ours.shape[0]
    ours = jnp.concatenate(
        [held[:count], jnp.pad(cond_here.astype(F32).reshape(1, -1), ((0, 0), (0, width - cond_here.size)))]
    )
    ours, totals = ours[None], held[count:]
    for axis, bit in [("seq", 1)] + [("dp", b) for b in range(1, dp_bits)]:
        got = swap(jnp.concatenate([ours.reshape(-1, width), totals]), axis, bit)
        amount = ours.shape[0] * ours.shape[1]
        if axis == "seq":
            mod_here = jnp.where(stays, ours[0, :count], got[:count])
        ours = jnp.concatenate([ours, got[:amount].reshape(ours.shape)])
        totals = totals + got[amount:]
    w_ada_f = w_ada.astype(F32)
    g_cond = sum(
        jnp.dot(
            mod_here[k * parts : (k + 1) * parts],
            w_ada_f[:, k * width : (k + 1) * width].T,
            precision=HIGH,
        )
        for k in range(6)
    )
    groups = ours.shape[0]
    conds = ours[:, count, : cond_here.size].reshape(groups * parts, -1)
    lanes = ours[:, :count].reshape(groups, 6, parts, width).transpose(0, 2, 1, 3)
    lanes = lanes.reshape(groups * parts, 6 * width)
    shards = dp_size * seq_size
    index = dp * seq_size + seq
    per = 6 * width // shards
    lanes = lax.dynamic_slice_in_dim(lanes, index * per, per, 1)
    g_w_ada = jnp.dot(conds.T, lanes, precision=HIGH)
    g_b_ada = jnp.sum(lanes, axis=0)
    mine_of = lambda v: lax.dynamic_slice_in_dim(v, index * (v.size // shards), v.size // shards, 0)
    g_gain_one, g_b_down, g_gain_two = mine_of(totals[0]), mine_of(totals[1]), mine_of(totals[2])
    g_b_up = mine_of(totals[3:].reshape(-1))
    return (
        output,
        jnp.stack(grad_tokens),
        g_cond,
        g_gain_one,
        g_gain_two,
        g_w_ada,
        g_b_ada,
        g_w_qkv,
        g_w_out,
        g_w_up,
        g_b_up,
        g_w_down,
        g_b_down,
    )


def solution(mesh):
    shards = ("dp", "seq")
    placed = (
        (P("dp", "seq", None), P("dp", None), P("dp"))
        + (P(),) * 10
        + (P("dp", "seq", None),)
    )
    return jax.shard_map(
        functools.partial(body, mesh.shape["dp"], mesh.shape["seq"]),
        mesh=mesh,
        in_specs=placed,
        out_specs=(
            P("dp", "seq", None),
            P("dp", "seq", None),
            P("dp", None),
            P(shards),
            P(shards),
            P(None, shards),
            P(shards),
            P(shards, None),
            P(shards, None),
            P(shards, None),
            P(shards),
            P(shards, None),
            P(shards),
        ),
        check_vma=False,
    )
```

```python
import functools

import jax
import jax.numpy as jnp
import numpy as np
from jax import lax
from jax.experimental import pallas as pl
from jax.experimental.pallas import tpu as pltpu
from jax.sharding import PartitionSpec as P

HEADS = 12
HD = 64
EPS = 1e-05
HIGH = lax.Precision.HIGHEST
BF = jnp.bfloat16
F32 = jnp.float32
PACK = 4
BLOCK = PACK * HD
LANES = 128
SPANS = (128, 512, 1024)
SCALE = 1000
GELU_C = float(np.sqrt(2.0 / np.pi))


def nn(left, right):
    return lax.dot_general(left, right, (((1,), (0,)), ((), ())), preferred_element_type=F32)


def nt(left, right):
    return lax.dot_general(left, right, (((1,), (1,)), ((), ())), preferred_element_type=F32)


def normalize(vector):
    average = jnp.mean(vector, axis=-1, keepdims=True)
    centred = vector - average
    inverse = lax.rsqrt(jnp.mean(centred * centred, axis=-1, keepdims=True) + EPS)
    return centred * inverse, inverse


def norm_back(grad_normed, normed, inverse):
    return inverse * (
        grad_normed
        - jnp.mean(grad_normed, axis=-1, keepdims=True)
        - normed * jnp.mean(grad_normed * normed, axis=-1, keepdims=True)
    )


def rows_sum(value):
    return jnp.sum(value, axis=0, keepdims=True)


def head_masks():
    lane = lax.broadcasted_iota(jnp.int32, (1, BLOCK), 1)
    return [(lane // HD == h).astype(F32).astype(BF) for h in range(PACK)]


def swap_halves(value):
    half = HD // 2
    lane = lax.broadcasted_iota(jnp.int32, value.shape, 1)
    ahead = pltpu.roll(value, LANES - half, 1)
    behind = pltpu.roll(value, half, 1)
    return jnp.where(lane % HD < half, ahead, behind)


def arrange_kernel(lengths, tok_ref, cond_ref, *refs):
    parts = tok_ref.shape[0]
    tok_refs, both_ref, order_ref = refs[:parts], refs[parts], refs[parts + 1]
    rank = []
    for s in range(parts):
        ahead = jnp.int32(0)
        for k in range(parts):
            if k < s:
                ahead = ahead + (lengths[k] >= lengths[s]).astype(jnp.int32)
            elif k > s:
                ahead = ahead + (lengths[k] > lengths[s]).astype(jnp.int32)
        rank.append(ahead)
    both_ref[...] = jnp.zeros_like(both_ref)
    for r in range(parts):
        at = jnp.int32(0)
        for k in range(1, parts):
            at = jnp.where(rank[k] == r, k, at)
        tok_refs[r][...] = tok_ref[at]
        width = cond_ref.shape[1]
        both_ref[r : r + 1, :width] = cond_ref[pl.ds(at, 1), :]
        both_ref[r : r + 1, width:] = jnp.full((1, LANES), lengths[at]).astype(F32)
        order_ref[r] = at
        order_ref[parts + r] = rank[r]


def arrange_pulls_kernel(order, pull_ref, *refs):
    for r, ref in enumerate(refs):
        ref[...] = pull_ref[order[r]]


def put_output_kernel(order, value_ref, moved_ref, out_ref):
    out_ref[...] = jnp.where(order[order.shape[0] - 1] == 1, value_ref[...], moved_ref[...])


def put_grad_kernel(order, value_ref, moved_ref, *refs):
    refs[-1][...] = jnp.where(
        order[order.shape[0] - 1] == 1, value_ref[...], moved_ref[...].astype(F32)
    )


def prep_kernel(
    place, a_ref, b_ref, c_ref, d_ref, mod_ref, gain_ref, w_ref, cos_ref, sin_ref,
    actt_ref, q_ref, k_ref, v_ref,
):
    step = pl.program_id(0)
    rows, width = a_ref.shape
    source = jnp.where(
        step < 2,
        jnp.where(step == 0, a_ref[...], b_ref[...]),
        jnp.where(step == 2, c_ref[...], d_ref[...]),
    ).astype(F32)
    normed, _ = normalize(source)
    act = (normed * gain_ref[...] * (1.0 + mod_ref[0, 1:2, :]) + mod_ref[0, 0:1, :]).astype(BF)
    actt_ref[...] = act.T
    cosine, sine = cos_ref[...], sin_ref[...]

    def turned(start, out_ref, factor):
        for at in range(0, width, BLOCK):
            both = nn(act, w_ref[:, start + at : start + at + BLOCK])
            for lane in range(0, BLOCK, LANES):
                part = both[:, lane : lane + LANES]
                out_ref[:, at + lane : at + lane + LANES] = (
                    part * cosine + swap_halves(part) * sine
                ).astype(BF) * factor

    @pl.when((place[0] ^ step) * rows < place[1])
    def _():
        turned(width, k_ref, BF(1.0))
        v_ref[...] = nn(act, w_ref[:, 2 * width :]).astype(BF)

    @pl.when(step == 0)
    def _():
        turned(0, q_ref, BF(HD**-0.5))


def attend_kernel(place, q_ref, k_ref, v_ref, mix_ref, lse_ref):
    masks = head_masks()
    lane = lax.broadcasted_iota(jnp.int32, (1, BLOCK), 1)
    narrow = lax.broadcasted_iota(jnp.int32, (1, LANES), 1)

    def work(span):
        queries, keys, values = q_ref[...], k_ref[:span, :], v_ref[:span, :]
        mixed = jnp.zeros(q_ref.shape, F32)
        logs = jnp.zeros((q_ref.shape[0], LANES), F32)
        for head in range(PACK):
            scores = nt(queries * masks[head], keys)
            top = jnp.max(scores, axis=-1, keepdims=True)
            raised = jnp.exp(scores - top)
            total = jnp.sum(raised, axis=-1, keepdims=True)
            probs = (raised * (1.0 / total)).astype(BF)
            mixed = jnp.where(lane // HD == head, nn(probs, values), mixed)
            logs = jnp.where(narrow == head, top + jnp.log(total), logs)
        mix_ref[...] = mixed.astype(BF)
        lse_ref[0] = logs.T[:8, :]

    for span in SPANS:
        pl.when(place[1] == span)(functools.partial(work, span))


def attend_back_kernel(
    more, last, place, q_ref, k_ref, v_ref, g_ref, lse_ref, cosq_ref, sinq_ref, cosk_ref, sink_ref,
    wq_ref, wk_ref, wv_ref, actt_ref, owns_ref, *refs,
):
    refs = list(refs)
    before_ref = refs.pop(0) if more else None
    keep_ref, send_ref = refs.pop(0), refs.pop(0)
    outs = [refs.pop(0) for _ in range(4 if last else 1)]
    share, own_share, grad_q, grad_k, grad_v, weights = refs
    masks = head_masks()
    group = pl.program_id(0)
    rows = q_ref.shape[0]

    def unturn(value, cosine, sine, out_ref, span):
        for lane in range(0, BLOCK, LANES):
            part = value[:, lane : lane + LANES]
            out_ref[:span, lane : lane + LANES] = (
                part * cosine - swap_halves(part) * sine
            ).astype(BF)

    @pl.when(group == 0)
    def _():
        share[...] = jnp.zeros_like(share)
        own_share[...] = jnp.zeros_like(own_share)

    def work(span):
        queries, grads = q_ref[...], g_ref[...]
        keys, values = k_ref[:span, :], v_ref[:span, :]
        keys_t = keys.T
        grad_keys = jnp.zeros((span, BLOCK), F32)
        grad_values = jnp.zeros((span, BLOCK), F32)
        turned = []
        for head in range(PACK):
            query, grad = queries * masks[head], grads * masks[head]
            probs = jnp.exp(nt(keys, query) - lse_ref[0, head : head + 1, :])
            grad_probs = nt(values, grad)
            inner = rows_sum(probs * grad_probs)
            grad_scores = (probs * (grad_probs - inner)).astype(BF)
            grad_values = grad_values + nn(probs.astype(BF), grad)
            grad_keys = grad_keys + nn(grad_scores, query)
            turned.append(nn(keys_t[head * HD : (head + 1) * HD], grad_scores))
        grad_queries = jnp.concatenate(turned, axis=0).T * HD**-0.5
        unturn(grad_queries, cosq_ref[...], sinq_ref[...], grad_q, rows)
        unturn(grad_keys, cosk_ref[:span, :], sink_ref[:span, :], grad_k, span)
        grad_v[:span, :] = grad_values.astype(BF)
        share[:span, :] += nt(grad_k[:span, :], wk_ref[...]) + nt(grad_v[:span, :], wv_ref[...])
        act = actt_ref[:, :span]
        products = (
            nn(owns_ref[...], grad_q[...]),
            nn(act, grad_k[:span, :]),
            nn(act, grad_v[:span, :]),
        )
        for which, product in enumerate(products):
            lanes = slice(which * BLOCK, (which + 1) * BLOCK)
            if more:
                product = product + before_ref[0, :, lanes]
            if last:
                weights[:, lanes] = product
            else:
                outs[0][0, :, lanes] = product

    for span in SPANS:
        pl.when(place[1] == span)(functools.partial(work, span))
    own_share[...] += nt(grad_q[...], wq_ref[...])
    if last:
        cut = 2 * BLOCK + LANES
        first = jnp.concatenate([weights[:, :BLOCK], weights[:, 2 * BLOCK : cut]], axis=1)
        other = jnp.concatenate([weights[:, BLOCK : 2 * BLOCK], weights[:, cut:]], axis=1)
        part_rows(first, place[2], outs[0], outs[1])
        part_rows(other, place[2], outs[2], outs[3])

    @pl.when(group == pl.num_programs(0) - 1)
    def _():
        def piece(k):
            return share[pl.ds(pl.multiple_of((place[0] ^ k) * rows, rows), rows), :]

        keep_ref[0] = piece(0) + own_share[...]
        keep_ref[1] = piece(1)
        send_ref[0] = piece(2).astype(BF)
        send_ref[1] = piece(3).astype(BF)


def norm_back_kernel(
    s, parts, keep_ref, core_ref, near_ref, tok_ref, gres_ref, mod_ref, gain_ref, before_ref,
    grad_ref, send_ref, sums_ref,
):
    def add(row, value):
        sums_ref[row : row + 1, :] = before_ref[row : row + 1, :] + rows_sum(value)

    pull = keep_ref[0] + core_ref[0].astype(F32) + near_ref[...].astype(F32)
    normed, inverse = normalize(tok_ref[...].astype(F32))
    gain = gain_ref[...]
    sums_ref[...] = before_ref[...]
    add(s, pull)
    add(parts + s, pull * (normed * gain))
    scaled = pull * (1.0 + mod_ref[0, 1:2, :])
    add(sums_ref.shape[0] - 8, scaled * normed)
    grad = gres_ref[0] + norm_back(scaled * gain, normed, inverse)
    grad_ref[...] = grad
    send_ref[...] = grad.astype(BF)


def part_rows(value, core, keep_ref, send_ref):
    blocks, piece, columns = keep_ref.shape
    both = value.reshape(blocks, 2, piece, columns)
    keep_ref[...] = jnp.where(core == 0, both[:, 0], both[:, 1]).astype(keep_ref.dtype)
    send_ref[...] = jnp.where(core == 0, both[:, 1], both[:, 0]).astype(BF)


def combine_kernel(index, *refs):
    for which in range(2):
        mine, got, other, other_got = refs[4 * which : 4 * which + 4]
        keep_ref, send_ref = refs[8 + 2 * which : 10 + 2 * which]
        keep_ref[...] = (mine[...].astype(F32) + got[...].astype(F32)).astype(keep_ref.dtype)
        send_ref[...] = (other[...].astype(F32) + other_got[...].astype(F32)).astype(BF)


def spread_kernel(place, keep_a, got_a, keep_b, got_b, *out_refs):
    rows, wide = keep_a.shape[1:]
    columns = keep_b.shape[2]
    if len(out_refs) == 2:
        out_refs = (out_refs[0].at[0], out_refs[1].at[0], out_refs[0].at[1], out_refs[1].at[1])
    for turn, out_ref in enumerate(out_refs):
        at = place[0] ^ turn
        out_ref[:, :wide] = (keep_a[at].astype(F32) + got_a[at].astype(F32)).astype(out_ref.dtype)
        below = keep_b[at].astype(F32) + got_b[at].astype(F32)
        for k in range(keep_b.shape[1] // rows):
            lanes = slice(wide + k * columns, wide + (k + 1) * columns)
            out_ref[:, lanes] = below[k * rows : (k + 1) * rows].astype(out_ref.dtype)


def mlp_kernel(
    core, mix0_ref, mix1_ref, mix2_ref, tok_ref, cot_ref, mod_ref, gain_ref, wout_ref, bdown_ref,
    wup_ref, bup_ref, wdown_ref,
    out_ref, gres_ref, gmix_ref, sums_ref,
    keepup_ref, sendup_ref, keepdown_ref, senddown_ref,
    resid, branch, act, act_t, slope, active, second, gsecond, gact, gpre,
):
    step = pl.program_id(0)
    tiles = pl.num_programs(0) // 2
    parts, rows, _ = tok_ref.shape
    mixes = (mix0_ref, mix1_ref, mix2_ref)

    def span(s):
        return slice(s * rows, (s + 1) * rows)

    def mod(s, which):
        return mod_ref[s, which : which + 1, :]

    @pl.when(step == 0)
    def _():
        sums_ref[...] = jnp.zeros_like(sums_ref)
        for s in range(parts):
            one = nn(mixes[s][...], wout_ref[...])
            res = tok_ref[s].astype(F32) + mod(s, 2) * one
            branch[span(s), :] = one
            resid[span(s), :] = res
            normed, _ = normalize(res)
            value = (normed * gain_ref[...] * (1.0 + mod(s, 4)) + mod(s, 3)).astype(BF)
            act[span(s), :] = value
            act_t[:, span(s)] = value.T
            second[span(s), :] = jnp.zeros_like(res)
            gact[span(s), :] = jnp.zeros_like(res)

    @pl.when(step < tiles)
    def _():
        for s in range(parts):
            u = nn(act[span(s), :], wup_ref[...]) + bup_ref[...]
            square = u * u
            bent = jnp.tanh(GELU_C * (u + 0.044715 * (square * u)))
            value = (0.5 * u * (1.0 + bent)).astype(BF)
            slope[step, span(s), :] = 0.5 * (1.0 + bent) + 0.5 * u * (1.0 - bent * bent) * (
                GELU_C * (1.0 + 3 * 0.044715 * square)
            )
            active[step, span(s), :] = value
            second[span(s), :] += nn(value, wdown_ref[...])

    @pl.when(step == tiles - 1)
    def _():
        total = jnp.zeros(bdown_ref.shape, F32)
        for s in range(parts):
            two = second[span(s), :] + bdown_ref[...]
            out_ref[s] = (resid[span(s), :] + mod(s, 5) * two).astype(BF)
            pull = cot_ref[s].astype(F32)
            sums_ref[5 * parts + s : 5 * parts + s + 1, :] = rows_sum(pull * two)
            down = (pull * mod(s, 5)).astype(BF)
            gsecond[span(s), :] = down
            total = total + rows_sum(down.astype(F32))
        sums_ref[6 * parts : 6 * parts + 1, :] = total

    @pl.when((step >= tiles) & (step < 2 * tiles))
    def _():
        at = step - tiles
        total = jnp.zeros(bup_ref.shape, F32)
        for s in range(parts):
            pulled = nt(gsecond[span(s), :], wdown_ref[...])
            value = (pulled * slope[at, span(s), :]).astype(BF)
            gpre[span(s), :] = value
            total = total + rows_sum(value.astype(F32))
            gact[span(s), :] += nt(value, wup_ref[...])
        sums_ref[pl.ds(6 * parts + 2 + at, 1), :] = total
        part_rows(nn(active[at].T, gsecond[...]), core[0], keepdown_ref, senddown_ref)
        part_rows(nn(act_t[...], gpre[...]), core[0], keepup_ref, sendup_ref)

    @pl.when(step == 2 * tiles)
    def _():
        total = jnp.zeros(bdown_ref.shape, F32)
        outer = jnp.zeros(resid.shape[1:] * 2, F32)
        for s in range(parts):
            normed, inverse = normalize(resid[span(s), :])
            pull = gact[span(s), :]
            sums_ref[3 * parts + s : 3 * parts + s + 1, :] = rows_sum(pull)
            sums_ref[4 * parts + s : 4 * parts + s + 1, :] = rows_sum(
                pull * (normed * gain_ref[...])
            )
            scaled = pull * (1.0 + mod(s, 4))
            total = total + rows_sum(scaled * normed)
            grad = cot_ref[s].astype(F32) + norm_back(scaled * gain_ref[...], normed, inverse)
            gres_ref[s] = grad
            sums_ref[2 * parts + s : 2 * parts + s + 1, :] = rows_sum(grad * branch[span(s), :])
            one = (grad * mod(s, 2)).astype(BF)
            gmix_ref[s] = nt(one, wout_ref[...]).astype(BF)
            outer = outer + nn(mixes[s][...].T, one)
        part_rows(outer, core[0], keepup_ref, sendup_ref)
        sums_ref[6 * parts + 1 : 6 * parts + 2, :] = total


def whole(array):
    rank = array.ndim
    return pl.BlockSpec(array.shape, lambda *_: (0,) * rank, pipeline_mode=pl.Buffered(1))


def limits(mib=60):
    return pltpu.CompilerParams(vmem_limit_bytes=mib * 2**20)


def cost(flops, bytes_accessed):
    return pl.CostEstimate(
        flops=int(flops) // SCALE, bytes_accessed=int(bytes_accessed) // SCALE, transcendentals=0
    )


def arrange(lengths, tokens, cond):
    parts, rows, width = tokens.shape
    shapes = [jax.ShapeDtypeStruct((rows, width), BF)] * parts
    shapes.append(jax.ShapeDtypeStruct((8, cond.shape[1] + LANES), F32))
    return pl.pallas_call(
        arrange_kernel,
        grid_spec=pltpu.PrefetchScalarGridSpec(
            num_scalar_prefetch=1,
            grid=(1,),
            in_specs=[whole(tokens), whole(cond)],
            out_specs=[whole(v) for v in shapes] + [pl.BlockSpec(memory_space=pltpu.SMEM)],
        ),
        out_shape=shapes + [jax.ShapeDtypeStruct((2 * parts,), jnp.int32)],
        compiler_params=limits(32),
        cost_estimate=cost(1e6, 3e6),
        name="arrange",
    )(lengths, tokens, cond)


def arrange_pulls(order, pulls):
    parts, rows, width = pulls.shape
    shapes = [jax.ShapeDtypeStruct((rows, width), BF)] * parts
    return pl.pallas_call(
        arrange_pulls_kernel,
        grid_spec=pltpu.PrefetchScalarGridSpec(
            num_scalar_prefetch=1,
            grid=(1,),
            in_specs=[whole(pulls)],
            out_specs=[whole(v) for v in shapes],
        ),
        out_shape=shapes,
        compiler_params=limits(32),
        cost_estimate=cost(1e6, 3e6),
        name="arrange_pulls",
    )(order, pulls)


def put_output(order, value, moved):
    parts, rows, width = value.shape
    block = pl.BlockSpec((1, rows, width), lambda i, p: (i, 0, 0))
    return pl.pallas_call(
        put_output_kernel,
        grid_spec=pltpu.PrefetchScalarGridSpec(
            num_scalar_prefetch=1,
            grid=(parts,),
            in_specs=[block, block],
            out_specs=pl.BlockSpec((1, rows, width), lambda i, p: (p[i], 0, 0)),
        ),
        out_shape=jax.ShapeDtypeStruct(value.shape, BF),
        compiler_params=limits(),
        cost_estimate=cost(1e6, 4e6),
        name="put_output",
    )(order, value, moved)


def put_grad(order, s, value, moved, parts, before):
    rows, width = value.shape
    more = before is not None
    return pl.pallas_call(
        put_grad_kernel,
        grid_spec=pltpu.PrefetchScalarGridSpec(
            num_scalar_prefetch=1,
            grid=(1,),
            in_specs=[pl.BlockSpec((rows, width), lambda i, p: (0, 0))] * 2
            + [pl.BlockSpec(memory_space=pl.ANY)] * more,
            out_specs=pl.BlockSpec((None, rows, width), lambda i, p: (p[s], 0, 0)),
        ),
        out_shape=jax.ShapeDtypeStruct((parts, rows, width), F32),
        input_output_aliases={3: 0} if more else {},
        compiler_params=limits(),
        cost_estimate=cost(1e6, 2e6),
        name="put_grad",
    )(order, value, moved, *([before] if more else []))


def prepare(place, pieces, mod, s, gain, w_qkv, cosine, sine):
    rows, width = pieces[0].shape
    slots = 4 * rows
    table = pl.BlockSpec((rows, LANES), lambda i, p: (p[0] ^ i, 0))
    piece = pl.BlockSpec((rows, width), lambda i, p: (p[0] ^ i, 0))
    return pl.pallas_call(
        prep_kernel,
        grid_spec=pltpu.PrefetchScalarGridSpec(
            num_scalar_prefetch=1,
            grid=(4,),
            in_specs=[whole(a) for a in pieces]
            + [pl.BlockSpec((1,) + mod.shape[1:], lambda i, p: (s, 0, 0))]
            + [whole(gain), whole(w_qkv), table, table],
            out_specs=[
                pl.BlockSpec((width, rows), lambda i, p: (0, p[0] ^ i)),
                pl.BlockSpec((rows, width), lambda i, p: (0, 0)),
                piece, piece,
            ],
        ),
        out_shape=[
            jax.ShapeDtypeStruct((width, slots), BF),
            jax.ShapeDtypeStruct((rows, width), BF),
            jax.ShapeDtypeStruct((slots, width), BF),
            jax.ShapeDtypeStruct((slots, width), BF),
        ],
        compiler_params=limits(32),
        cost_estimate=cost(2 * slots * width * width * 2.25, 10e6),
        name="prepare",
    )(place, *pieces, mod, gain, w_qkv, cosine, sine)


def attend(place, queries, keys, values):
    rows, width = queries.shape
    slots = keys.shape[0]
    groups = width // BLOCK
    own = pl.BlockSpec((rows, BLOCK), lambda j, p: (0, j))
    full = pl.BlockSpec((slots, BLOCK), lambda j, p: (0, j))
    return pl.pallas_call(
        attend_kernel,
        grid_spec=pltpu.PrefetchScalarGridSpec(
            num_scalar_prefetch=1,
            grid=(groups,),
            in_specs=[own, full, full],
            out_specs=[own, pl.BlockSpec((1, 8, rows), lambda j, p: (j, 0, 0))],
        ),
        out_shape=[
            jax.ShapeDtypeStruct((rows, width), BF),
            jax.ShapeDtypeStruct((groups, 8, rows), F32),
        ],
        compiler_params=limits(32),
        cost_estimate=cost(16 * rows * slots * width, 5e6),
        name="attend",
    )(place, queries, keys, values)


def attend_back(
    place, queries, keys, values, grads, s, logs, cosine, sine, w_qkv, act_t, before, last, dp_size
):
    rows, width = queries.shape
    slots = keys.shape[0]
    groups = width // BLOCK
    own = pl.BlockSpec((rows, BLOCK), lambda j, p: (0, j))
    full = pl.BlockSpec((slots, BLOCK), lambda j, p: (0, j))
    own_table = pl.BlockSpec((rows, LANES), lambda j, p: (p[0], 0))
    full_table = pl.BlockSpec((slots, LANES), lambda j, p: (0, 0))
    every = pl.BlockSpec((1, width, 3 * BLOCK), lambda j, p: (j, 0, 0))
    blocks, piece, columns = dp_size // 2, width // dp_size, BLOCK + LANES
    more = before is not None
    if last:
        part = (blocks, piece, groups * columns)
        weight_specs = [pl.BlockSpec((blocks, piece, columns), lambda j, p: (0, 0, j))] * 4
        weight_shapes = [jax.ShapeDtypeStruct(part, F32), jax.ShapeDtypeStruct(part, BF)] * 2
    else:
        weight_specs = [every]
        weight_shapes = [jax.ShapeDtypeStruct((groups, width, 3 * BLOCK), F32)]
    return pl.pallas_call(
        functools.partial(attend_back_kernel, more, last),
        grid_spec=pltpu.PrefetchScalarGridSpec(
            num_scalar_prefetch=1,
            grid=(groups,),
            in_specs=[
                own, full, full,
                pl.BlockSpec((None, rows, BLOCK), lambda j, p: (s, 0, j)),
                pl.BlockSpec((1, 8, rows), lambda j, p: (j, 0, 0)),
                own_table, own_table, full_table, full_table,
                pl.BlockSpec((width, BLOCK), lambda j, p: (0, j)),
                pl.BlockSpec((width, BLOCK), lambda j, p: (0, groups + j)),
                pl.BlockSpec((width, BLOCK), lambda j, p: (0, 2 * groups + j)),
                whole(act_t),
                pl.BlockSpec((width, rows), lambda j, p: (0, p[0])),
            ]
            + [every] * more,
            out_specs=[pl.BlockSpec((2, rows, width), lambda j, p: (0, 0, 0))] * 2 + weight_specs,
            scratch_shapes=[
                pltpu.VMEM((slots, width), F32),
                pltpu.VMEM((rows, width), F32),
                pltpu.VMEM((rows, BLOCK), BF),
                pltpu.VMEM((slots, BLOCK), BF),
                pltpu.VMEM((slots, BLOCK), BF),
                pltpu.VMEM((width, 3 * BLOCK), F32),
            ],
        ),
        out_shape=[
            jax.ShapeDtypeStruct((2, rows, width), F32),
            jax.ShapeDtypeStruct((2, rows, width), BF),
        ]
        + weight_shapes,
        compiler_params=limits(),
        cost_estimate=cost(60 * rows * slots * width, 12e6),
        name="attend_back",
    )(
        place, queries, keys, values, grads, logs, cosine, sine, cosine, sine, w_qkv, w_qkv, w_qkv,
        act_t, act_t, *([before] if more else []),
    )


def norm_one_back(keep, core_got, near_got, tokens, grad_res, s, mod, gain, sums):
    rows, width = tokens.shape
    first = pl.BlockSpec((1, rows, width), lambda i: (0, 0, 0))
    return pl.pallas_call(
        functools.partial(norm_back_kernel, s, mod.shape[0]),
        grid=(1,),
        in_specs=[
            first, first, whole(near_got), whole(tokens),
            pl.BlockSpec((1, rows, width), lambda i: (s, 0, 0)),
            pl.BlockSpec((1,) + mod.shape[1:], lambda i: (s, 0, 0)),
            whole(gain), whole(sums),
        ],
        out_specs=[pl.BlockSpec((rows, width), lambda i: (0, 0))] * 2
        + [pl.BlockSpec(sums.shape, lambda i: (0, 0))],
        out_shape=[
            jax.ShapeDtypeStruct((rows, width), F32),
            jax.ShapeDtypeStruct((rows, width), BF),
            jax.ShapeDtypeStruct(sums.shape, F32),
        ],
        compiler_params=limits(),
        cost_estimate=cost(40 * rows * width, 6e6),
        name="norm_one_back",
    )(keep, core_got, near_got, tokens, grad_res, mod, gain, sums)


def feed_forward(core, mixes, tokens, pulls, mod, gain, w_out, b_down, w_up, b_up, w_down, dp_size):
    parts, rows, width = tokens.shape
    hidden = w_up.shape[1]
    tile = width
    tiles = hidden // tile
    total = parts * rows
    blocks, piece = dp_size // 2, width // dp_size
    tall_piece = hidden // dp_size
    per_tile = tile // (2 * tall_piece)
    late = lambda i: jnp.maximum(i - tiles, 0)
    last = lambda i: jnp.minimum(late(i), tiles - 1)
    turn = lambda i: jnp.minimum(jnp.where(i < tiles, i, i - tiles), tiles - 1)
    wide = pl.BlockSpec((width, tile), lambda i, c: (0, turn(i)))
    bias = pl.BlockSpec((1, tile), lambda i, c: (0, turn(i)))
    tall = pl.BlockSpec((tile, width), lambda i, c: (turn(i), 0))
    out_wide = pl.BlockSpec((blocks, piece, tile), lambda i, c: (0, 0, late(i)))
    out_tall = pl.BlockSpec((per_tile, tall_piece, width), lambda i, c: (last(i), 0, 0))
    outs = [
        jax.ShapeDtypeStruct(tokens.shape, BF),
        jax.ShapeDtypeStruct(tokens.shape, F32),
        jax.ShapeDtypeStruct(tokens.shape, BF),
        jax.ShapeDtypeStruct((6 * parts + 2 + hidden // width + 8, width), F32),
        jax.ShapeDtypeStruct((blocks, piece, hidden + width), BF),
        jax.ShapeDtypeStruct((blocks, piece, hidden + width), BF),
        jax.ShapeDtypeStruct((blocks, tall_piece, width), BF),
        jax.ShapeDtypeStruct((blocks, tall_piece, width), BF),
    ]
    return pl.pallas_call(
        mlp_kernel,
        grid_spec=pltpu.PrefetchScalarGridSpec(
            num_scalar_prefetch=1,
            grid=(2 * tiles + 1,),
            in_specs=[whole(m) for m in mixes]
            + [whole(a) for a in (tokens, pulls, mod, gain, w_out, b_down)]
            + [wide, bias, tall],
            out_specs=[whole(o) for o in outs[:4]]
            + [out_wide, out_wide, out_tall, out_tall],
            scratch_shapes=[
                pltpu.VMEM((total, width), F32),
                pltpu.VMEM((total, width), F32),
                pltpu.VMEM((total, width), BF),
                pltpu.VMEM((width, total), BF),
                pltpu.VMEM((tiles, total, tile), F32),
                pltpu.VMEM((tiles, total, tile), BF),
                pltpu.VMEM((total, width), F32),
                pltpu.VMEM((total, width), BF),
                pltpu.VMEM((total, width), F32),
                pltpu.VMEM((total, tile), BF),
            ],
        ),
        out_shape=outs,
        compiler_params=limits(),
        cost_estimate=cost(2 * total * width * (6 * hidden + 3 * width), 50e6),
        name="feed_forward",
    )(core, *mixes, tokens, pulls, mod, gain, w_out, b_down, w_up, b_up, w_down)


def combine(index, streams, turns, kept):
    in_specs, out_specs, shapes, inputs = [], [], [], []
    for which, (keep, got) in enumerate(streams):
        above, _, below, rows, columns = keep.shape
        tile = columns // turns
        block = (None, None, None, rows, tile)

        def place(i, c, p, flip, which=which, below=below):
            return (i // below, 1 - p[which] if flip else p[which], i % below, 0, c)

        mine = pl.BlockSpec(block, functools.partial(place, flip=False))
        other = pl.BlockSpec(block, functools.partial(place, flip=True))
        out = pl.BlockSpec((None, rows, tile), lambda i, c, p: (i, 0, c))
        in_specs += [mine, mine, other, other]
        inputs += [keep, got, keep, got]
        out_specs += [out, out]
        shape = (above * below, rows, columns)
        shapes += [jax.ShapeDtypeStruct(shape, kept), jax.ShapeDtypeStruct(shape, BF)]
        steps = above * below
    return pl.pallas_call(
        combine_kernel,
        grid_spec=pltpu.PrefetchScalarGridSpec(
            num_scalar_prefetch=1, grid=(steps, turns), in_specs=in_specs, out_specs=out_specs
        ),
        out_shape=shapes,
        compiler_params=limits(),
        cost_estimate=cost(inputs[0].size * 4, inputs[0].size * 18),
        name="combine",
    )(index, *inputs)


def spread(place, keep_a, got_a, keep_b, got_b, paired):
    _, rows, wide = keep_a.shape
    columns = wide + keep_b[0].size // rows
    if paired:
        shapes = [jax.ShapeDtypeStruct((2, rows, columns), t) for t in (F32, BF)]
    else:
        shapes = [jax.ShapeDtypeStruct((rows, columns), t) for t in (F32, BF, BF, BF)]
    arrays = (keep_a, got_a, keep_b, got_b)
    return pl.pallas_call(
        spread_kernel,
        grid_spec=pltpu.PrefetchScalarGridSpec(
            num_scalar_prefetch=1,
            grid=(1,),
            in_specs=[whole(v) for v in arrays],
            out_specs=[whole(v) for v in shapes],
        ),
        out_shape=shapes,
        compiler_params=limits(),
        cost_estimate=cost(columns * rows * 8, columns * rows * 40),
        name="spread",
    )(place, *arrays)


def after(value, *others):
    return lax.optimization_barrier((value,) + others)[0]


def body(
    dp_size, seq_size,
    tokens, cond, lengths, gain_one, gain_two, w_ada, b_ada, w_qkv, w_out, w_up, b_up, w_down,
    b_down, cotangent,
):
    parts, rows, width = tokens.shape
    hidden = w_up.shape[1]
    slots = rows * seq_size
    dp_bits = dp_size.bit_length() - 1
    dp, seq = lax.axis_index("dp").astype(jnp.int32), lax.axis_index("seq").astype(jnp.int32)
    core, side = dp & 1, lax.shift_right_logical(seq, jnp.int32(seq_size.bit_length() - 2))
    stays = core == side
    own = jnp.where(stays, seq, seq ^ 2).astype(jnp.int32)

    def dp_swap(value, bit):
        return lax.ppermute(value, "dp", [(i, i ^ (1 << bit)) for i in range(dp_size)])

    def seq_swap(value, bit):
        return lax.ppermute(value, "seq", [(i, i ^ (1 << bit)) for i in range(seq_size)])

    def swap(value, axis, bit):
        return dp_swap(value, bit) if axis == "dp" else seq_swap(value, bit)

    def bit_of(axis, bit):
        return ((dp if axis == "dp" else seq) >> bit) & 1

    pairs = []
    for i in range(dp_size):
        for j in range(seq_size):
            if (i & 1) != j // (seq_size // 2):
                pairs.append((i * seq_size + j, (i ^ 1) * seq_size + (j ^ 2)))

    def send_across(value):
        return lax.ppermute(value, ("dp", "seq"), pairs)

    def settle(value, moved, *others):
        return jnp.where(stays, value, after(moved, *others).astype(value.dtype))

    def regroup(value, moving=None):
        return settle(value, send_across(value if moving is None else moving))

    *sorted_tokens, both, order = arrange(lengths, tokens, cond.astype(F32))

    puts = jnp.concatenate([order[:parts], stays.astype(jnp.int32)[None]])

    mine = [None] * parts
    mine[0] = regroup(sorted_tokens[0])
    both = jnp.where(stays, both, dp_swap(both, 0))
    cond_here, lengths_here = both[:parts, :-LANES].astype(BF), both[:, -1].astype(jnp.int32)
    mod = jnp.dot(cond_here, w_ada, preferred_element_type=F32) + b_ada
    mod = mod.reshape(parts, 6, width)
    places = [jnp.stack([own, lengths_here[s], core]).astype(jnp.int32) for s in range(parts)]
    core_index = core.astype(jnp.int32)[None]
    frequency = np.power(10000.0, -np.arange(HD // 2) * 2.0 / HD).astype(np.float32)
    angles = np.arange(slots).astype(np.float32)[:, None] * frequency[None, :]
    angles = angles.astype(np.float64)
    cosine = jnp.asarray(np.tile(np.cos(angles), (1, LANES // (HD // 2))).astype(np.float32))
    sine = np.sin(angles)
    sine = jnp.asarray(np.tile(np.concatenate([-sine, sine], 1), (1, LANES // HD)).astype(np.float32))
    gain_one_row, gain_two_row = gain_one[None, :], gain_two[None, :]

    saved, mixes = [], []
    tie = lax.optimization_barrier
    mine[0] = after(mine[0], mod, *places)
    nears = [seq_swap(mine[0], 0)]
    moving = send_across(after(sorted_tokens[1], mine[0]))
    fars = [dp_swap(mine[0], 0)]
    pulls, pulled = arrange_pulls(order, after(cotangent, mine[0])), []
    for s in range(parts):
        group = (mine[s], nears[s], fars[s], dp_swap(nears[s], 0))
        if s:
            group = tie((group, mixes[-1]))[0]
        if s > 1:
            pulled.append(send_across(after(pulls[s], pulled[-1], nears[s])))
        act_t, queries, keys, values = prepare(
            places[s], group, mod, s, gain_one_row, w_qkv, cosine, sine
        )
        if s == 0:
            mine[1] = settle(sorted_tokens[1], moving, act_t)
            nears.append(seq_swap(mine[1], 0))
            fars.append(dp_swap(mine[1], 0))
            if parts > 2:
                moving = send_across(after(sorted_tokens[2], mine[1]))
        elif s == 1:
            pulled.append(send_across(after(pulls[1], pulled[-1], act_t)))
        mixture, logs = attend(places[s], queries, keys, values)
        saved.append((act_t, queries, keys, values, logs))
        mixes.append(mixture)
        if s + 1 < parts:
            nears[s + 1] = after(nears[s + 1], mixture)
        if s + 2 < parts:
            mine[s + 2] = settle(sorted_tokens[s + 2], moving, mixture)
            nears.append(seq_swap(mine[s + 2], 0))
            fars.append(dp_swap(after(mine[s + 2], nears[s + 1]), 0))
            if s == 0:
                pulled.append(send_across(after(pulls[0], mine[2])))
            if s + 3 < parts:
                moving = send_across(after(sorted_tokens[s + 3], mine[s + 2]))
    pulls = [settle(v, m, mixes[-1]) for v, m in zip(pulls, pulled)]

    output, grad_res, grad_mix, sums, keep_up, send_up, keep_down, send_down = feed_forward(
        core_index, mixes, jnp.stack(mine), jnp.stack(pulls), mod, gain_two_row, w_out,
        b_down[None, :], w_up, b_up[None, :], w_down, dp_size,
    )
    output_moved = send_across(output)

    forth = list(range(1, dp_bits))
    back = forth[::-1]

    class Halving:
        def __init__(self, arrays, sends, turns):
            self.arrays, self.sends, self.turns, self.at = arrays, sends, turns, [0, 0]
            self.orders = [list(forth), list(back)]
            self.names = [forth[::-1], forth[::-1]]
            self.move()

        def merge(self, kept=F32):
            streams, index, self.at = [], [], []
            for which in range(2):
                bit = self.orders[which].pop(0)
                names = self.names[which]
                place = names.index(bit)
                names.pop(place)
                keep = self.arrays[which]
                shape = (2**place, 2, 2 ** (len(names) - place)) + keep.shape[1:]
                streams.append((keep.reshape(shape), self.got[which].reshape(shape)))
                index.append(bit_of("dp", bit))
                self.at.append(bit)
            index = jnp.stack(index).astype(jnp.int32)
            keep_a, send_a, keep_b, send_b = combine(index, streams, self.turns, kept)
            self.arrays, self.sends, self.turns = [keep_a, keep_b], [send_a, send_b], 1
            return self.sends

        def move(self):
            self.got = [dp_swap(v, bit) for v, bit in zip(self.sends, self.at)]

        def spread(self, paired):
            pieces = [
                v.reshape(seq_size, v.shape[1] // seq_size, v.shape[2]) for v in self.arrays + self.got
            ]
            self.own, *self.sends = spread(
                own_seq, pieces[0], pieces[2], pieces[1], pieces[3], paired
            )
            return self.sends

        def send(self):
            self.got = [
                lax.ppermute(v, "seq", [(i, i ^ k) for i in range(seq_size)])
                for k, v in enumerate(self.sends, 1)
            ]

    own_seq = seq.astype(jnp.int32)[None]
    mlp = Halving([keep_up, keep_down], [send_up, send_down], 3)

    shares, cores, nears, grad_tokens, moved, g_tokens = [], [], [], [], [], None

    def pass_on(s):
        there = (shares[s][0][1] + cores[s][1].astype(F32)).astype(BF)
        nears.append(seq_swap(there, 0))
        return there

    def finish(s, sums):
        grad, rounded, sums = norm_one_back(
            shares[s][0], cores[s], nears[s], mine[s], grad_res, s, mod, gain_one_row, sums
        )
        grad_tokens.append(grad)
        return rounded, sums

    def give_back(s, rounded):
        moved.append(send_across(rounded))

    def put(s, *others):
        held = after(moved[s], *others)
        return put_grad(puts, s, grad_tokens[s], held, parts, g_tokens)

    waits, weights = [], [None]
    for s in range(parts):
        act_t, queries, keys, values, logs = saved[s]
        keep, send, *weights = attend_back(
            places[s], after(queries, *waits), keys, values, grad_mix, s, logs, cosine, sine, w_qkv,
            act_t, weights[0], s == parts - 1, dp_size,
        )
        if s == 0:
            send, weights, mlp.got = tie((send, weights, mlp.got))
        elif s == 1:
            send, weights, mlp.got, nears[0], output_moved = tie(
                (send, weights, mlp.got, nears[0], output_moved)
            )
        else:
            send, weights, mlp.got, nears[1], moved[0] = tie(
                (send, weights, mlp.got, nears[1], moved[0])
            )
        shares.append((keep, send))
        cores.append(dp_swap(send, 0))
        if s == parts - 1:
            break
        if mlp.orders[0]:
            waits = list(mlp.merge(BF if s == 0 else F32))
            mlp.move()
        if s:
            rounded, sums = finish(s - 1, sums)
            give_back(s - 1, rounded)
            waits.append(rounded)
        waits.append(pass_on(s))

    while mlp.orders[0]:
        mlp.merge()
        mlp.move()
    waits = mlp.spread(True)
    mlp.send()
    cores[-1] = after(cores[-1], *waits)
    passed = pass_on(parts - 1)
    att = Halving([weights[0], weights[2]], [weights[1], weights[3]], 1)
    nears[-2] = after(nears[-2], passed)
    rounded, sums = finish(parts - 2, sums)
    give_back(parts - 2, rounded)
    att.got = tie((att.got, rounded))[0]
    waits = att.merge()
    att.move()
    output = put_output(puts, output, after(output_moved, *waits))
    g_tokens = put(0, output)
    nears[-1], g_tokens = tie((nears[-1], g_tokens))
    rounded, sums = finish(parts - 1, sums)
    give_back(parts - 1, rounded)
    across = dp_swap(sums, 0)
    waits = [rounded]
    while att.orders[0]:
        att.got = tie((att.got, *waits))[0]
        waits = att.merge()
        att.move()
    held = sums + after(across, *waits)
    across = seq_swap(held, 0)
    mlp.got, mlp.own = tie((mlp.got, mlp.own, held))[:2]
    further = (mlp.own[1] + mlp.got[0][1].astype(F32)).astype(BF)
    g_mlp = mlp.own[0] + mlp.got[0][0].astype(F32)
    held = held + after(across, further, g_mlp)
    further = seq_swap(further, 1)
    count, kept = 6 * parts, held.shape[0] - 7
    conds = cond_here.astype(F32).reshape(1, -1)
    conds = jnp.pad(conds, ((0, 0), (0, width - conds.shape[1])))
    ours = jnp.concatenate([held[:kept], conds]).astype(BF)[None]
    for axis, bit in [("seq", 1)] + [("dp", b) for b in forth]:
        got = swap(ours, axis, bit)
        if axis == "seq":
            att.got = tie((att.got, ours))[0]
            waits = att.spread(False)
            att.send()
            g_tokens = put(1, *waits)
            got = after(got, g_tokens)
            mod_here = jnp.where(stays, held[:count], got[0, :count].astype(F32))
        ours = jnp.concatenate([ours, got])
    ours = ours.astype(F32)
    totals = jnp.sum(ours[:, count:kept], axis=0)
    g_tokens = put(2, ours)
    att.got, further = tie((att.got, further, ours))[:2]
    g_att = att.own + sum(v.astype(F32) for v in att.got)
    g_mlp = g_mlp + further.astype(F32)

    piece = width // (dp_size * seq_size)
    g_w_up, g_w_out = g_mlp[:, :hidden], g_mlp[:, hidden : hidden + width]
    tall = g_mlp[:, hidden + width :].reshape(piece, hidden // width, width)
    g_w_down = tall.transpose(1, 0, 2).reshape(hidden // (dp_size * seq_size), width)
    parted = g_att.reshape(piece, 2, width // BLOCK, BLOCK + LANES)
    sides = [parted[:, k, :, :BLOCK].reshape(piece, width) for k in range(2)]
    sides.append(parted[..., BLOCK:].transpose(0, 2, 1, 3).reshape(piece, width))
    g_w_qkv = jnp.concatenate(sides, axis=1)

    w_ada_f = w_ada.astype(F32)
    g_cond = sum(
        jnp.dot(
            mod_here[k * parts : (k + 1) * parts],
            w_ada_f[:, k * width : (k + 1) * width].T,
            precision=HIGH,
        )
        for k in range(6)
    )
    chosen = order[:parts, None] == jnp.arange(parts)[None, :]
    g_cond = jnp.sum(jnp.where(chosen[:, :, None], g_cond[:, None], 0.0), axis=0)
    groups = ours.shape[0]
    conds = ours[:, kept, : cond_here.size].reshape(groups * parts, -1)
    lanes = ours[:, :count].reshape(groups, 6, parts, width).transpose(0, 2, 1, 3)
    lanes = lanes.reshape(groups * parts, 6 * width)
    shards = dp_size * seq_size
    index = dp * seq_size + seq

    def mine_of(value):
        size = value.shape[-1] // shards
        starts = (jnp.int32(0),) * (value.ndim - 1) + (index * size,)
        sizes = value.shape[:-1] + (size,)
        return lax.dynamic_slice(value, starts, sizes, allow_negative_indices=False)

    lanes = mine_of(lanes)
    g_w_ada = jnp.dot(conds.T, lanes, precision=HIGH)
    g_b_ada = jnp.sum(lanes, axis=0)
    g_b_down, g_gain_two, g_gain_one = mine_of(totals[0]), mine_of(totals[1]), mine_of(totals[-1])
    g_b_up = mine_of(totals[2:-1].reshape(-1))
    return (
        output,
        g_tokens,
        g_cond,
        g_gain_one,
        g_gain_two,
        g_w_ada,
        g_b_ada,
        g_w_qkv,
        g_w_out,
        g_w_up,
        g_b_up,
        g_w_down,
        g_b_down,
    )


def solution(mesh):
    shards = ("dp", "seq")
    placed = (
        (P("dp", "seq", None), P("dp", None), P("dp"))
        + (P(),) * 10
        + (P("dp", "seq", None),)
    )
    return jax.shard_map(
        functools.partial(body, mesh.shape["dp"], mesh.shape["seq"]),
        mesh=mesh,
        in_specs=placed,
        out_specs=(
            P("dp", "seq", None),
            P("dp", "seq", None),
            P("dp", None),
            P(shards),
            P(shards),
            P(None, shards),
            P(shards),
            P(shards, None),
            P(shards, None),
            P(shards, None),
            P(shards),
            P(shards, None),
            P(shards),
        ),
        check_vma=False,
    )
```

```python
import functools

import jax
import jax.numpy as jnp
import numpy as np
from jax import lax
from jax.experimental import pallas as pl
from jax.experimental.pallas import tpu as pltpu
from jax.sharding import PartitionSpec as P

HEADS = 12
HD = 64
EPS = 1e-05
HIGH = lax.Precision.HIGHEST
BF = jnp.bfloat16
F32 = jnp.float32
PACK = 4
BLOCK = PACK * HD
LANES = 128
SPANS = (128, 512, 1024)
SCALE = 1000
GELU_C = float(np.sqrt(2.0 / np.pi))


def nn(left, right):
    return lax.dot_general(left, right, (((1,), (0,)), ((), ())), preferred_element_type=F32)


def nt(left, right):
    return lax.dot_general(left, right, (((1,), (1,)), ((), ())), preferred_element_type=F32)


def normalize(vector):
    average = jnp.mean(vector, axis=-1, keepdims=True)
    centred = vector - average
    inverse = lax.rsqrt(jnp.mean(centred * centred, axis=-1, keepdims=True) + EPS)
    return centred * inverse, inverse


def norm_back(grad_normed, normed, inverse):
    return inverse * (
        grad_normed
        - jnp.mean(grad_normed, axis=-1, keepdims=True)
        - normed * jnp.mean(grad_normed * normed, axis=-1, keepdims=True)
    )


def rows_sum(value):
    return jnp.sum(value, axis=0, keepdims=True)


def head_masks():
    lane = lax.broadcasted_iota(jnp.int32, (1, BLOCK), 1)
    return [(lane // HD == h).astype(F32).astype(BF) for h in range(PACK)]


def swap_halves(value):
    half = HD // 2
    lane = lax.broadcasted_iota(jnp.int32, value.shape, 1)
    ahead = pltpu.roll(value, LANES - half, 1)
    behind = pltpu.roll(value, half, 1)
    return jnp.where(lane % HD < half, ahead, behind)


def arrange_kernel(lengths, tok_ref, cond_ref, *refs):
    parts = tok_ref.shape[0]
    tok_refs, both_ref, order_ref = refs[:parts], refs[parts], refs[parts + 1]
    rank = []
    for s in range(parts):
        ahead = jnp.int32(0)
        for k in range(parts):
            if k < s:
                ahead = ahead + (lengths[k] >= lengths[s]).astype(jnp.int32)
            elif k > s:
                ahead = ahead + (lengths[k] > lengths[s]).astype(jnp.int32)
        rank.append(ahead)
    both_ref[...] = jnp.zeros_like(both_ref)
    for r in range(parts):
        at = jnp.int32(0)
        for k in range(1, parts):
            at = jnp.where(rank[k] == r, k, at)
        tok_refs[r][...] = tok_ref[at]
        width = cond_ref.shape[1]
        both_ref[r : r + 1, :width] = cond_ref[pl.ds(at, 1), :]
        both_ref[r : r + 1, width:] = jnp.full((1, LANES), lengths[at]).astype(F32)
        order_ref[r] = at
        order_ref[parts + r] = rank[r]


def arrange_pulls_kernel(order, pull_ref, *refs):
    for r, ref in enumerate(refs):
        ref[...] = pull_ref[order[r]]


def put_kernel(order, *refs):
    parts = (order.shape[0] - 1)
    step = pl.program_id(0)
    value_ref, moved_ref = refs[:2]
    grads, moves = refs[2 : 2 + parts], refs[2 + parts : 2 + 2 * parts]
    out_ref, grad_ref = refs[2 + 2 * parts :]
    stays = order[parts] == 1
    out_ref[...] = jnp.where(stays, value_ref[...], moved_ref[...])
    for s in range(parts):

        @pl.when((step == s) & stays)
        def _():
            grad_ref[0] = grads[s][...]

        @pl.when((step == s) & ~stays)
        def _():
            grad_ref[0] = moves[s][...].astype(F32)


def prep_kernel(
    place, a_ref, b_ref, c_ref, d_ref, mod_ref, gain_ref, w_ref, cos_ref, sin_ref,
    actt_ref, q_ref, k_ref, v_ref,
):
    step = pl.program_id(0)
    rows, width = a_ref.shape
    source = jnp.where(
        step < 2,
        jnp.where(step == 0, a_ref[...], b_ref[...]),
        jnp.where(step == 2, c_ref[...], d_ref[...]),
    ).astype(F32)
    normed, _ = normalize(source)
    act = (normed * gain_ref[...] * (1.0 + mod_ref[0, 1:2, :]) + mod_ref[0, 0:1, :]).astype(BF)
    actt_ref[...] = act.T
    cosine, sine = cos_ref[...], sin_ref[...]

    def turned(start, out_ref, factor):
        for at in range(0, width, BLOCK):
            both = nn(act, w_ref[:, start + at : start + at + BLOCK])
            for lane in range(0, BLOCK, LANES):
                part = both[:, lane : lane + LANES]
                out_ref[:, at + lane : at + lane + LANES] = (
                    part * cosine + swap_halves(part) * sine
                ).astype(BF) * factor

    @pl.when((place[0] ^ step) * rows < place[1])
    def _():
        turned(width, k_ref, BF(1.0))
        v_ref[...] = nn(act, w_ref[:, 2 * width :]).astype(BF)

    @pl.when(step == 0)
    def _():
        turned(0, q_ref, BF(HD**-0.5))


def attend_kernel(place, q_ref, k_ref, v_ref, mix_ref, lse_ref):
    masks = head_masks()
    lane = lax.broadcasted_iota(jnp.int32, (1, BLOCK), 1)
    narrow = lax.broadcasted_iota(jnp.int32, (1, LANES), 1)

    def work(span):
        queries, keys, values = q_ref[...], k_ref[:span, :], v_ref[:span, :]
        mixed = jnp.zeros(q_ref.shape, F32)
        logs = jnp.zeros((q_ref.shape[0], LANES), F32)
        for head in range(PACK):
            scores = nt(queries * masks[head], keys)
            top = jnp.max(scores, axis=-1, keepdims=True)
            raised = jnp.exp(scores - top)
            total = jnp.sum(raised, axis=-1, keepdims=True)
            probs = (raised * (1.0 / total)).astype(BF)
            mixed = jnp.where(lane // HD == head, nn(probs, values), mixed)
            logs = jnp.where(narrow == head, top + jnp.log(total), logs)
        mix_ref[...] = mixed.astype(BF)
        lse_ref[0] = logs.T[:8, :]

    for span in SPANS:
        pl.when(place[1] == span)(functools.partial(work, span))


def attend_back_kernel(
    more, last, place, q_ref, k_ref, v_ref, g_ref, lse_ref, cosq_ref, sinq_ref, cosk_ref, sink_ref,
    wq_ref, wk_ref, wv_ref, actt_ref, owns_ref, *refs,
):
    refs = list(refs)
    before_ref = refs.pop(0) if more else None
    keep_ref, send_ref = refs.pop(0), refs.pop(0)
    outs = [refs.pop(0) for _ in range(4 if last else 1)]
    share, own_share, grad_q, grad_k, grad_v, weights = refs
    masks = head_masks()
    group = pl.program_id(0)
    rows = q_ref.shape[0]

    def unturn(value, cosine, sine, out_ref):
        for lane in range(0, BLOCK, LANES):
            part = value[:, lane : lane + LANES]
            out_ref[: value.shape[0], lane : lane + LANES] = (
                part * cosine - swap_halves(part) * sine
            ).astype(BF)

    @pl.when(group == 0)
    def _():
        share[...] = jnp.zeros_like(share)
        own_share[...] = jnp.zeros_like(own_share)

    def work(span):
        queries, grads = q_ref[...], g_ref[...]
        query_all = jnp.concatenate([queries * masks[h] for h in range(PACK)], axis=0)
        grad_all = jnp.concatenate([grads * masks[h] for h in range(PACK)], axis=0)
        head = lax.broadcasted_iota(jnp.int32, (BLOCK, 1), 0) // HD
        sides = [(head == h).astype(F32).astype(BF) for h in range(PACK)]
        queries_t, grads_t = queries.T, grads.T
        query_t = jnp.concatenate([queries_t * sides[h] for h in range(PACK)], axis=1)
        grad_t = jnp.concatenate([grads_t * sides[h] for h in range(PACK)], axis=1)
        keys, values = k_ref[:span, :], v_ref[:span, :]
        keys_t = keys.T
        raw_all, pull_all = nn(keys, query_t), nn(values, grad_t)
        turned, probs_all, scores_all = [], [], []
        for h in range(PACK):
            part = slice(h * rows, (h + 1) * rows)
            probs = jnp.exp(raw_all[:, part] - lse_ref[0, h : h + 1, :])
            pull = pull_all[:, part]
            scores = (probs * (pull - rows_sum(probs * pull))).astype(BF)
            probs_all.append(probs.astype(BF))
            scores_all.append(scores)
            turned.append(nn(keys_t[h * HD : (h + 1) * HD], scores))
        grad_v[:span, :] = nn(jnp.concatenate(probs_all, axis=1), grad_all).astype(BF)
        grad_keys = nn(jnp.concatenate(scores_all, axis=1), query_all)
        unturn(grad_keys, cosk_ref[:span, :], sink_ref[:span, :], grad_k)
        grad_queries = jnp.concatenate(turned, axis=0).T * HD**-0.5
        unturn(grad_queries, cosq_ref[...], sinq_ref[...], grad_q)
        share[:span, :] += nt(grad_k[:span, :], wk_ref[...]) + nt(grad_v[:span, :], wv_ref[...])
        act = actt_ref[:, :span]
        products = (
            nn(owns_ref[...], grad_q[...]),
            nn(act, grad_k[:span, :]),
            nn(act, grad_v[:span, :]),
        )
        for which, product in enumerate(products):
            lanes = slice(which * BLOCK, (which + 1) * BLOCK)
            if more:
                product = product + before_ref[0, :, lanes]
            if last:
                weights[:, lanes] = product
            else:
                outs[0][0, :, lanes] = product

    for span in SPANS:
        pl.when(place[1] == span)(functools.partial(work, span))
    own_share[...] += nt(grad_q[...], wq_ref[...])
    if last:
        cut = 2 * BLOCK + LANES
        first = jnp.concatenate([weights[:, :BLOCK], weights[:, 2 * BLOCK : cut]], axis=1)
        other = jnp.concatenate([weights[:, BLOCK : 2 * BLOCK], weights[:, cut:]], axis=1)
        part_rows(first, place[2], outs[0], outs[1])
        part_rows(other, place[2], outs[2], outs[3])

    @pl.when(group == pl.num_programs(0) - 1)
    def _():
        def piece(k):
            return share[pl.ds(pl.multiple_of((place[0] ^ k) * rows, rows), rows), :]

        keep_ref[0] = piece(0) + own_share[...]
        keep_ref[1] = piece(1)
        send_ref[0] = piece(2).astype(BF)
        send_ref[1] = piece(3).astype(BF)


def norm_back_kernel(
    s, parts, keep_ref, core_ref, near_ref, tok_ref, gres_ref, mod_ref, gain_ref, before_ref,
    grad_ref, send_ref, sums_ref,
):
    def add(row, value):
        sums_ref[row : row + 1, :] = before_ref[row : row + 1, :] + rows_sum(value)

    pull = keep_ref[0] + core_ref[0].astype(F32) + near_ref[...].astype(F32)
    normed, inverse = normalize(tok_ref[...].astype(F32))
    gain = gain_ref[...]
    sums_ref[...] = before_ref[...]
    add(s, pull)
    add(parts + s, pull * (normed * gain))
    scaled = pull * (1.0 + mod_ref[0, 1:2, :])
    add(sums_ref.shape[0] - 8, scaled * normed)
    grad = gres_ref[0] + norm_back(scaled * gain, normed, inverse)
    grad_ref[...] = grad
    send_ref[...] = grad.astype(BF)


def part_rows(value, core, keep_ref, send_ref):
    blocks, piece, columns = keep_ref.shape
    both = value.reshape(blocks, 2, piece, columns)
    keep_ref[...] = jnp.where(core == 0, both[:, 0], both[:, 1]).astype(keep_ref.dtype)
    send_ref[...] = jnp.where(core == 0, both[:, 1], both[:, 0]).astype(BF)


def combine_kernel(index, *refs):
    for which in range(2):
        mine, got, other, other_got = refs[4 * which : 4 * which + 4]
        keep_ref, send_ref = refs[8 + 2 * which : 10 + 2 * which]
        keep_ref[...] = (mine[...].astype(F32) + got[...].astype(F32)).astype(keep_ref.dtype)
        send_ref[...] = (other[...].astype(F32) + other_got[...].astype(F32)).astype(BF)


def spread_kernel(place, keep_a, got_a, keep_b, got_b, *out_refs):
    rows, wide = keep_a.shape[1:]
    columns = keep_b.shape[2]
    if len(out_refs) == 2:
        out_refs = (out_refs[0].at[0], out_refs[1].at[0], out_refs[0].at[1], out_refs[1].at[1])
    for turn, out_ref in enumerate(out_refs):
        at = place[0] ^ turn
        out_ref[:, :wide] = (keep_a[at].astype(F32) + got_a[at].astype(F32)).astype(out_ref.dtype)
        below = keep_b[at].astype(F32) + got_b[at].astype(F32)
        for k in range(keep_b.shape[1] // rows):
            lanes = slice(wide + k * columns, wide + (k + 1) * columns)
            out_ref[:, lanes] = below[k * rows : (k + 1) * rows].astype(out_ref.dtype)


def place_mlp_kernel(own_ref, near_ref, far_ref, up_ref, out_ref, down_ref):
    total = own_ref[0] + near_ref[0].astype(F32) + far_ref[...].astype(F32)
    rows, hidden = up_ref.shape
    width = out_ref.shape[1]
    up_ref[...] = total[:, :hidden]
    out_ref[...] = total[:, hidden : hidden + width]
    for k in range(down_ref.shape[0] // rows):
        at = hidden + (k + 1) * width
        down_ref[k * rows : (k + 1) * rows, :] = total[:, at : at + width]


def place_att_kernel(own_ref, near_ref, far_ref, qkv_ref):
    total = own_ref[0] + near_ref[0].astype(F32) + far_ref[...].astype(F32)
    width = qkv_ref.shape[1] // 3
    step, side = BLOCK + LANES, width // BLOCK * (BLOCK + LANES)
    for j in range(width // BLOCK):
        for which in range(2):
            at = which * side + j * step
            to = which * width + j * BLOCK
            qkv_ref[:, to : to + BLOCK] = total[:, at : at + BLOCK]
            to = 2 * width + j * BLOCK + which * LANES
            qkv_ref[:, to : to + LANES] = total[:, at + BLOCK : at + step]


def mlp_kernel(
    core, mix0_ref, mix1_ref, mix2_ref, tok_ref, cot_ref, mod_ref, gain_ref, wout_ref, bdown_ref,
    wup_ref, bup_ref, wdown_ref,
    out_ref, gres_ref, gmix_ref, sums_ref,
    keepup_ref, sendup_ref, keepdown_ref, senddown_ref,
    resid, branch, act, act_t, slope, active, second, gsecond, gact, gpre,
):
    step = pl.program_id(0)
    tiles = pl.num_programs(0) // 2
    parts, rows, _ = tok_ref.shape
    mixes = (mix0_ref, mix1_ref, mix2_ref)

    def span(s):
        return slice(s * rows, (s + 1) * rows)

    def mod(s, which):
        return mod_ref[s, which : which + 1, :]

    @pl.when(step == 0)
    def _():
        sums_ref[...] = jnp.zeros_like(sums_ref)
        for s in range(parts):
            one = nn(mixes[s][...], wout_ref[...])
            res = tok_ref[s].astype(F32) + mod(s, 2) * one
            branch[span(s), :] = one
            resid[span(s), :] = res
            normed, _ = normalize(res)
            value = (normed * gain_ref[...] * (1.0 + mod(s, 4)) + mod(s, 3)).astype(BF)
            act[span(s), :] = value
            act_t[:, span(s)] = value.T
            second[span(s), :] = jnp.zeros_like(res)
            gact[span(s), :] = jnp.zeros_like(res)

    @pl.when(step < tiles)
    def _():
        for s in range(parts):
            u = nn(act[span(s), :], wup_ref[...]) + bup_ref[...]
            square = u * u
            bent = jnp.tanh(GELU_C * (u + 0.044715 * (square * u)))
            value = (0.5 * u * (1.0 + bent)).astype(BF)
            slope[step, span(s), :] = 0.5 * (1.0 + bent) + 0.5 * u * (1.0 - bent * bent) * (
                GELU_C * (1.0 + 3 * 0.044715 * square)
            )
            active[step, span(s), :] = value
            second[span(s), :] += nn(value, wdown_ref[...])

    @pl.when(step == tiles - 1)
    def _():
        total = jnp.zeros(bdown_ref.shape, F32)
        for s in range(parts):
            two = second[span(s), :] + bdown_ref[...]
            out_ref[s] = (resid[span(s), :] + mod(s, 5) * two).astype(BF)
            pull = cot_ref[s].astype(F32)
            sums_ref[5 * parts + s : 5 * parts + s + 1, :] = rows_sum(pull * two)
            down = (pull * mod(s, 5)).astype(BF)
            gsecond[span(s), :] = down
            total = total + rows_sum(down.astype(F32))
        sums_ref[6 * parts : 6 * parts + 1, :] = total

    @pl.when((step >= tiles) & (step < 2 * tiles))
    def _():
        at = step - tiles
        total = jnp.zeros(bup_ref.shape, F32)
        for s in range(parts):
            pulled = nt(gsecond[span(s), :], wdown_ref[...])
            value = (pulled * slope[at, span(s), :]).astype(BF)
            gpre[span(s), :] = value
            total = total + rows_sum(value.astype(F32))
            gact[span(s), :] += nt(value, wup_ref[...])
        sums_ref[pl.ds(6 * parts + 2 + at, 1), :] = total
        part_rows(nn(active[at].T, gsecond[...]), core[0], keepdown_ref, senddown_ref)
        part_rows(nn(act_t[...], gpre[...]), core[0], keepup_ref, sendup_ref)

    @pl.when(step == 2 * tiles)
    def _():
        total = jnp.zeros(bdown_ref.shape, F32)
        outer = jnp.zeros(resid.shape[1:] * 2, F32)
        for s in range(parts):
            normed, inverse = normalize(resid[span(s), :])
            pull = gact[span(s), :]
            sums_ref[3 * parts + s : 3 * parts + s + 1, :] = rows_sum(pull)
            sums_ref[4 * parts + s : 4 * parts + s + 1, :] = rows_sum(
                pull * (normed * gain_ref[...])
            )
            scaled = pull * (1.0 + mod(s, 4))
            total = total + rows_sum(scaled * normed)
            grad = cot_ref[s].astype(F32) + norm_back(scaled * gain_ref[...], normed, inverse)
            gres_ref[s] = grad
            sums_ref[2 * parts + s : 2 * parts + s + 1, :] = rows_sum(grad * branch[span(s), :])
            one = (grad * mod(s, 2)).astype(BF)
            gmix_ref[s] = nt(one, wout_ref[...]).astype(BF)
            outer = outer + nn(mixes[s][...].T, one)
        part_rows(outer, core[0], keepup_ref, sendup_ref)
        sums_ref[6 * parts + 1 : 6 * parts + 2, :] = total


def whole(array):
    rank = array.ndim
    return pl.BlockSpec(array.shape, lambda *_: (0,) * rank, pipeline_mode=pl.Buffered(1))


def limits(mib=60):
    return pltpu.CompilerParams(vmem_limit_bytes=mib * 2**20)


def cost(flops, bytes_accessed):
    return pl.CostEstimate(
        flops=int(flops) // SCALE, bytes_accessed=int(bytes_accessed) // SCALE, transcendentals=0
    )


def arrange(lengths, tokens, cond):
    parts, rows, width = tokens.shape
    shapes = [jax.ShapeDtypeStruct((rows, width), BF)] * parts
    shapes.append(jax.ShapeDtypeStruct((8, cond.shape[1] + LANES), F32))
    return pl.pallas_call(
        arrange_kernel,
        grid_spec=pltpu.PrefetchScalarGridSpec(
            num_scalar_prefetch=1,
            grid=(1,),
            in_specs=[whole(tokens), whole(cond)],
            out_specs=[whole(v) for v in shapes] + [pl.BlockSpec(memory_space=pltpu.SMEM)],
        ),
        out_shape=shapes + [jax.ShapeDtypeStruct((2 * parts,), jnp.int32)],
        compiler_params=limits(32),
        cost_estimate=cost(1e6, 3e6),
        name="arrange",
    )(lengths, tokens, cond)


def arrange_pulls(order, pulls):
    parts, rows, width = pulls.shape
    shapes = [jax.ShapeDtypeStruct((rows, width), BF)] * parts
    return pl.pallas_call(
        arrange_pulls_kernel,
        grid_spec=pltpu.PrefetchScalarGridSpec(
            num_scalar_prefetch=1,
            grid=(1,),
            in_specs=[whole(pulls)],
            out_specs=[whole(v) for v in shapes],
        ),
        out_shape=shapes,
        compiler_params=limits(32),
        cost_estimate=cost(1e6, 3e6),
        name="arrange_pulls",
    )(order, pulls)


def put(order, value, moved, grads, moves):
    parts, rows, width = value.shape
    block = pl.BlockSpec((1, rows, width), lambda i, p: (i, 0, 0))
    placed = pl.BlockSpec((1, rows, width), lambda i, p: (p[i], 0, 0))
    return pl.pallas_call(
        put_kernel,
        grid_spec=pltpu.PrefetchScalarGridSpec(
            num_scalar_prefetch=1,
            grid=(parts,),
            in_specs=[block, block] + [whole(v) for v in list(grads) + list(moves)],
            out_specs=[placed, placed],
        ),
        out_shape=[
            jax.ShapeDtypeStruct(value.shape, BF),
            jax.ShapeDtypeStruct(value.shape, F32),
        ],
        compiler_params=limits(),
        cost_estimate=cost(1e6, 1e7),
        name="put",
    )(order, value, moved, *grads, *moves)


def prepare(place, pieces, mod, s, gain, w_qkv, cosine, sine):
    rows, width = pieces[0].shape
    slots = 4 * rows
    table = pl.BlockSpec((rows, LANES), lambda i, p: (p[0] ^ i, 0))
    piece = pl.BlockSpec((rows, width), lambda i, p: (p[0] ^ i, 0))
    return pl.pallas_call(
        prep_kernel,
        grid_spec=pltpu.PrefetchScalarGridSpec(
            num_scalar_prefetch=1,
            grid=(4,),
            in_specs=[whole(a) for a in pieces]
            + [pl.BlockSpec((1,) + mod.shape[1:], lambda i, p: (s, 0, 0))]
            + [whole(gain), whole(w_qkv), table, table],
            out_specs=[
                pl.BlockSpec((width, rows), lambda i, p: (0, p[0] ^ i)),
                pl.BlockSpec((rows, width), lambda i, p: (0, 0)),
                piece, piece,
            ],
        ),
        out_shape=[
            jax.ShapeDtypeStruct((width, slots), BF),
            jax.ShapeDtypeStruct((rows, width), BF),
            jax.ShapeDtypeStruct((slots, width), BF),
            jax.ShapeDtypeStruct((slots, width), BF),
        ],
        compiler_params=limits(32),
        cost_estimate=cost(2 * slots * width * width * 2.25, 10e6),
        name="prepare",
    )(place, *pieces, mod, gain, w_qkv, cosine, sine)


def attend(place, queries, keys, values):
    rows, width = queries.shape
    slots = keys.shape[0]
    groups = width // BLOCK
    own = pl.BlockSpec((rows, BLOCK), lambda j, p: (0, j))
    full = pl.BlockSpec((slots, BLOCK), lambda j, p: (0, j))
    return pl.pallas_call(
        attend_kernel,
        grid_spec=pltpu.PrefetchScalarGridSpec(
            num_scalar_prefetch=1,
            grid=(groups,),
            in_specs=[own, full, full],
            out_specs=[own, pl.BlockSpec((1, 8, rows), lambda j, p: (j, 0, 0))],
        ),
        out_shape=[
            jax.ShapeDtypeStruct((rows, width), BF),
            jax.ShapeDtypeStruct((groups, 8, rows), F32),
        ],
        compiler_params=limits(32),
        cost_estimate=cost(16 * rows * slots * width, 5e6),
        name="attend",
    )(place, queries, keys, values)


def attend_back(
    place, queries, keys, values, grads, s, logs, cosine, sine, w_qkv, act_t, before, last, dp_size
):
    rows, width = queries.shape
    slots = keys.shape[0]
    groups = width // BLOCK
    own = pl.BlockSpec((rows, BLOCK), lambda j, p: (0, j))
    full = pl.BlockSpec((slots, BLOCK), lambda j, p: (0, j))
    own_table = pl.BlockSpec((rows, LANES), lambda j, p: (p[0], 0))
    full_table = pl.BlockSpec((slots, LANES), lambda j, p: (0, 0))
    every = pl.BlockSpec((1, width, 3 * BLOCK), lambda j, p: (j, 0, 0))
    blocks, piece, columns = dp_size // 2, width // dp_size, BLOCK + LANES
    more = before is not None
    if last:
        part = (blocks, piece, groups * columns)
        weight_specs = [pl.BlockSpec((blocks, piece, columns), lambda j, p: (0, 0, j))] * 4
        weight_shapes = [jax.ShapeDtypeStruct(part, F32), jax.ShapeDtypeStruct(part, BF)] * 2
    else:
        weight_specs = [every]
        weight_shapes = [jax.ShapeDtypeStruct((groups, width, 3 * BLOCK), F32)]
    return pl.pallas_call(
        functools.partial(attend_back_kernel, more, last),
        grid_spec=pltpu.PrefetchScalarGridSpec(
            num_scalar_prefetch=1,
            grid=(groups,),
            in_specs=[
                own, full, full,
                pl.BlockSpec((None, rows, BLOCK), lambda j, p: (s, 0, j)),
                pl.BlockSpec((1, 8, rows), lambda j, p: (j, 0, 0)),
                own_table, own_table, full_table, full_table,
                pl.BlockSpec((width, BLOCK), lambda j, p: (0, j)),
                pl.BlockSpec((width, BLOCK), lambda j, p: (0, groups + j)),
                pl.BlockSpec((width, BLOCK), lambda j, p: (0, 2 * groups + j)),
                whole(act_t),
                pl.BlockSpec((width, rows), lambda j, p: (0, p[0])),
            ]
            + [every] * more,
            out_specs=[pl.BlockSpec((2, rows, width), lambda j, p: (0, 0, 0))] * 2 + weight_specs,
            scratch_shapes=[
                pltpu.VMEM((slots, width), F32),
                pltpu.VMEM((rows, width), F32),
                pltpu.VMEM((rows, BLOCK), BF),
                pltpu.VMEM((slots, BLOCK), BF),
                pltpu.VMEM((slots, BLOCK), BF),
                pltpu.VMEM((width, 3 * BLOCK), F32),
            ],
        ),
        out_shape=[
            jax.ShapeDtypeStruct((2, rows, width), F32),
            jax.ShapeDtypeStruct((2, rows, width), BF),
        ]
        + weight_shapes,
        compiler_params=limits(),
        cost_estimate=cost(60 * rows * slots * width, 12e6),
        name="attend_back",
    )(
        place, queries, keys, values, grads, logs, cosine, sine, cosine, sine, w_qkv, w_qkv,
        w_qkv, act_t, act_t, *([before] if more else []),
    )


def norm_one_back(keep, core_got, near_got, tokens, grad_res, s, mod, gain, sums):
    rows, width = tokens.shape
    first = pl.BlockSpec((1, rows, width), lambda i: (0, 0, 0))
    return pl.pallas_call(
        functools.partial(norm_back_kernel, s, mod.shape[0]),
        grid=(1,),
        in_specs=[
            first, first, whole(near_got), whole(tokens),
            pl.BlockSpec((1, rows, width), lambda i: (s, 0, 0)),
            pl.BlockSpec((1,) + mod.shape[1:], lambda i: (s, 0, 0)),
            whole(gain), whole(sums),
        ],
        out_specs=[pl.BlockSpec((rows, width), lambda i: (0, 0))] * 2
        + [pl.BlockSpec(sums.shape, lambda i: (0, 0))],
        out_shape=[
            jax.ShapeDtypeStruct((rows, width), F32),
            jax.ShapeDtypeStruct((rows, width), BF),
            jax.ShapeDtypeStruct(sums.shape, F32),
        ],
        compiler_params=limits(),
        cost_estimate=cost(40 * rows * width, 6e6),
        name="norm_one_back",
    )(keep, core_got, near_got, tokens, grad_res, mod, gain, sums)


def feed_forward(core, mixes, tokens, pulls, mod, gain, w_out, b_down, w_up, b_up, w_down, dp_size):
    parts, rows, width = tokens.shape
    hidden = w_up.shape[1]
    tile = width
    tiles = hidden // tile
    total = parts * rows
    blocks, piece = dp_size // 2, width // dp_size
    tall_piece = hidden // dp_size
    per_tile = tile // (2 * tall_piece)
    late = lambda i: jnp.maximum(i - tiles, 0)
    last = lambda i: jnp.minimum(late(i), tiles - 1)
    turn = lambda i: jnp.minimum(jnp.where(i < tiles, i, i - tiles), tiles - 1)
    wide = pl.BlockSpec((width, tile), lambda i, c: (0, turn(i)))
    bias = pl.BlockSpec((1, tile), lambda i, c: (0, turn(i)))
    tall = pl.BlockSpec((tile, width), lambda i, c: (turn(i), 0))
    out_wide = pl.BlockSpec((blocks, piece, tile), lambda i, c: (0, 0, late(i)))
    out_tall = pl.BlockSpec((per_tile, tall_piece, width), lambda i, c: (last(i), 0, 0))
    outs = [
        jax.ShapeDtypeStruct(tokens.shape, BF),
        jax.ShapeDtypeStruct(tokens.shape, F32),
        jax.ShapeDtypeStruct(tokens.shape, BF),
        jax.ShapeDtypeStruct((6 * parts + 2 + hidden // width + 8, width), F32),
        jax.ShapeDtypeStruct((blocks, piece, hidden + width), BF),
        jax.ShapeDtypeStruct((blocks, piece, hidden + width), BF),
        jax.ShapeDtypeStruct((blocks, tall_piece, width), BF),
        jax.ShapeDtypeStruct((blocks, tall_piece, width), BF),
    ]
    return pl.pallas_call(
        mlp_kernel,
        grid_spec=pltpu.PrefetchScalarGridSpec(
            num_scalar_prefetch=1,
            grid=(2 * tiles + 1,),
            in_specs=[whole(m) for m in mixes]
            + [whole(a) for a in (tokens, pulls, mod, gain, w_out, b_down)]
            + [wide, bias, tall],
            out_specs=[whole(o) for o in outs[:4]]
            + [out_wide, out_wide, out_tall, out_tall],
            scratch_shapes=[
                pltpu.VMEM((total, width), F32),
                pltpu.VMEM((total, width), F32),
                pltpu.VMEM((total, width), BF),
                pltpu.VMEM((width, total), BF),
                pltpu.VMEM((tiles, total, tile), F32),
                pltpu.VMEM((tiles, total, tile), BF),
                pltpu.VMEM((total, width), F32),
                pltpu.VMEM((total, width), BF),
                pltpu.VMEM((total, width), F32),
                pltpu.VMEM((total, tile), BF),
            ],
        ),
        out_shape=outs,
        compiler_params=limits(),
        cost_estimate=cost(2 * total * width * (6 * hidden + 3 * width), 50e6),
        name="feed_forward",
    )(core, *mixes, tokens, pulls, mod, gain, w_out, b_down, w_up, b_up, w_down)


def combine(index, streams, turns, kept):
    in_specs, out_specs, shapes, inputs = [], [], [], []
    for which, (keep, got) in enumerate(streams):
        above, _, below, rows, columns = keep.shape
        tile = columns // turns
        block = (None, None, None, rows, tile)

        def place(i, c, p, flip, which=which, below=below):
            return (i // below, 1 - p[which] if flip else p[which], i % below, 0, c)

        mine = pl.BlockSpec(block, functools.partial(place, flip=False))
        other = pl.BlockSpec(block, functools.partial(place, flip=True))
        out = pl.BlockSpec((None, rows, tile), lambda i, c, p: (i, 0, c))
        in_specs += [mine, mine, other, other]
        inputs += [keep, got, keep, got]
        out_specs += [out, out]
        shape = (above * below, rows, columns)
        shapes += [jax.ShapeDtypeStruct(shape, kept), jax.ShapeDtypeStruct(shape, BF)]
        steps = above * below
    return pl.pallas_call(
        combine_kernel,
        grid_spec=pltpu.PrefetchScalarGridSpec(
            num_scalar_prefetch=1, grid=(steps, turns), in_specs=in_specs, out_specs=out_specs
        ),
        out_shape=shapes,
        compiler_params=limits(),
        cost_estimate=cost(inputs[0].size * 4, inputs[0].size * 18),
        name="combine",
    )(index, *inputs)


def spread(place, keep_a, got_a, keep_b, got_b, paired):
    _, rows, wide = keep_a.shape
    columns = wide + keep_b[0].size // rows
    if paired:
        shapes = [jax.ShapeDtypeStruct((2, rows, columns), t) for t in (F32, BF)]
    else:
        shapes = [jax.ShapeDtypeStruct((rows, columns), t) for t in (F32, BF, BF, BF)]
    arrays = (keep_a, got_a, keep_b, got_b)
    return pl.pallas_call(
        spread_kernel,
        grid_spec=pltpu.PrefetchScalarGridSpec(
            num_scalar_prefetch=1,
            grid=(1,),
            in_specs=[whole(v) for v in arrays],
            out_specs=[whole(v) for v in shapes],
        ),
        out_shape=shapes,
        compiler_params=limits(),
        cost_estimate=cost(columns * rows * 8, columns * rows * 40),
        name="spread",
    )(place, *arrays)


def place_weights(kernel, own, near, far, shapes):
    return pl.pallas_call(
        kernel,
        grid=(1,),
        in_specs=[pl.BlockSpec((1,) + far.shape, lambda i: (0, 0, 0))] * 2 + [whole(far)],
        out_specs=[whole(v) for v in shapes],
        out_shape=shapes,
        compiler_params=limits(),
        cost_estimate=cost(far.size * 2, far.size * 12),
        name="place_weights",
    )(own, near, far)


def after(value, *others):
    return lax.optimization_barrier((value,) + others)[0]


def body(
    dp_size, seq_size,
    tokens, cond, lengths, gain_one, gain_two, w_ada, b_ada, w_qkv, w_out, w_up, b_up, w_down,
    b_down, cotangent,
):
    parts, rows, width = tokens.shape
    hidden = w_up.shape[1]
    slots = rows * seq_size
    dp_bits = dp_size.bit_length() - 1
    dp, seq = lax.axis_index("dp").astype(jnp.int32), lax.axis_index("seq").astype(jnp.int32)
    core, side = dp & 1, lax.shift_right_logical(seq, jnp.int32(seq_size.bit_length() - 2))
    stays = core == side
    own = jnp.where(stays, seq, seq ^ 2).astype(jnp.int32)

    def dp_swap(value, bit):
        return lax.ppermute(value, "dp", [(i, i ^ (1 << bit)) for i in range(dp_size)])

    def seq_swap(value, bit):
        return lax.ppermute(value, "seq", [(i, i ^ (1 << bit)) for i in range(seq_size)])

    def swap(value, axis, bit):
        return dp_swap(value, bit) if axis == "dp" else seq_swap(value, bit)

    def bit_of(axis, bit):
        return ((dp if axis == "dp" else seq) >> bit) & 1

    pairs = []
    for i in range(dp_size):
        for j in range(seq_size):
            if (i & 1) != j // (seq_size // 2):
                pairs.append((i * seq_size + j, (i ^ 1) * seq_size + (j ^ 2)))

    def send_across(value):
        return lax.ppermute(value, ("dp", "seq"), pairs)

    def settle(value, moved, *others):
        return jnp.where(stays, value, after(moved, *others).astype(value.dtype))

    def regroup(value, moving=None):
        return settle(value, send_across(value if moving is None else moving))

    *sorted_tokens, both, order = arrange(lengths, tokens, cond.astype(F32))

    puts = jnp.concatenate([order[:parts], stays.astype(jnp.int32)[None]])

    mine = [None] * parts
    mine[0] = regroup(sorted_tokens[0])
    both = jnp.where(stays, both, dp_swap(both, 0))
    cond_here, lengths_here = both[:parts, :-LANES].astype(BF), both[:, -1].astype(jnp.int32)
    mod = jnp.dot(cond_here, w_ada, preferred_element_type=F32) + b_ada
    mod = mod.reshape(parts, 6, width)
    places = [jnp.stack([own, lengths_here[s], core]).astype(jnp.int32) for s in range(parts)]
    core_index = core.astype(jnp.int32)[None]
    frequency = np.power(10000.0, -np.arange(HD // 2) * 2.0 / HD).astype(np.float32)
    angles = np.arange(slots).astype(np.float32)[:, None] * frequency[None, :]
    angles = angles.astype(np.float64)
    cosine = jnp.asarray(np.tile(np.cos(angles), (1, LANES // (HD // 2))).astype(np.float32))
    sine = np.sin(angles)
    sine = jnp.asarray(np.tile(np.concatenate([-sine, sine], 1), (1, LANES // HD)).astype(np.float32))
    gain_one_row, gain_two_row = gain_one[None, :], gain_two[None, :]

    saved, mixes = [], []
    tie = lax.optimization_barrier
    forth = list(range(1, dp_bits))
    back = forth[::-1]
    halves = [jnp.stack([bit_of("dp", i), bit_of("dp", j)]) for i, j in zip(forth, back)]
    own_seq = seq[None]
    mine[0] = after(mine[0], mod, *places, *halves, own_seq, puts, core_index)
    nears = [seq_swap(mine[0], 0)]
    moving = send_across(after(sorted_tokens[1], mine[0]))
    fars = [dp_swap(mine[0], 0)]
    mine[1] = settle(sorted_tokens[1], moving)
    nears.append(seq_swap(mine[1], 0))
    if parts > 2:
        moving = send_across(after(sorted_tokens[2], mine[1]))
    pulls, pulled = arrange_pulls(order, after(cotangent, mine[0])), []
    for s in range(parts):
        group = (mine[s], nears[s], fars[s], dp_swap(nears[s], 0))
        group = tie((group, mixes[-1] if s else mine[1], tuple(pulled) if s > 1 else ()))[0]
        if s == parts - 1:
            pulled += [send_across(after(pulls[k], nears[s])) for k in range(len(pulled), parts)]
        act_t, queries, keys, values = prepare(
            places[s], group, mod, s, gain_one_row, w_qkv, cosine, sine
        )
        if s == parts - 1:
            queries = after(queries, *pulled)
        mixture, logs = attend(places[s], queries, keys, values)
        saved.append((act_t, queries, keys, values, logs))
        mixes.append(mixture)
        if s + 1 < parts:
            nears[s + 1] = after(nears[s + 1], mixture)
            fars.append(dp_swap(after(mine[s + 1], mixture), 0))
        if s + 2 < parts:
            mine[s + 2] = settle(sorted_tokens[s + 2], moving, mixture)
            nears.append(seq_swap(mine[s + 2], 0))
            if s == 0:
                pulled += [send_across(after(pulls[k], mine[2])) for k in range(parts - 1)]
            if s + 3 < parts:
                moving = send_across(after(sorted_tokens[s + 3], mine[s + 2]))
    pulls = [settle(v, m, mixes[-1]) for v, m in zip(pulls, pulled)]

    output, grad_res, grad_mix, sums, keep_up, send_up, keep_down, send_down = feed_forward(
        core_index, mixes, jnp.stack(mine), jnp.stack(pulls), mod, gain_two_row, w_out,
        b_down[None, :], w_up, b_up[None, :], w_down, dp_size,
    )
    output_moved = send_across(output)

    class Halving:
        def __init__(self, arrays, sends, turns):
            self.arrays, self.sends, self.turns, self.at = arrays, sends, turns, [0, 0]
            self.orders = [list(forth), list(back)]
            self.names = [forth[::-1], forth[::-1]]
            self.move()

        def merge(self, kept=F32):
            streams, self.at = [], []
            index = halves[len(forth) - len(self.orders[0])]
            for which in range(2):
                bit = self.orders[which].pop(0)
                names = self.names[which]
                place = names.index(bit)
                names.pop(place)
                keep = self.arrays[which]
                shape = (2**place, 2, 2 ** (len(names) - place)) + keep.shape[1:]
                streams.append((keep.reshape(shape), self.got[which].reshape(shape)))
                self.at.append(bit)
            keep_a, send_a, keep_b, send_b = combine(index, streams, self.turns, kept)
            self.arrays, self.sends, self.turns = [keep_a, keep_b], [send_a, send_b], 1
            return self.sends

        def move(self):
            self.got = [dp_swap(v, bit) for v, bit in zip(self.sends, self.at)]

        def spread(self, paired):
            pieces = [
                v.reshape(seq_size, v.shape[1] // seq_size, v.shape[2]) for v in self.arrays + self.got
            ]
            self.own, *self.sends = spread(
                own_seq, pieces[0], pieces[2], pieces[1], pieces[3], paired
            )
            return self.sends

        def send(self):
            self.got = [
                lax.ppermute(v, "seq", [(i, i ^ k) for i in range(seq_size)])
                for k, v in enumerate(self.sends, 1)
            ]

    mlp = Halving([keep_up, keep_down], [send_up, send_down], 3)

    shares, cores, nears, grad_tokens, moved = [], [], [], [], []

    def pass_on(s):
        there = (shares[s][0][1] + cores[s][1].astype(F32)).astype(BF)
        nears.append(seq_swap(there, 0))
        return there

    def finish(s, sums):
        grad, rounded, sums = norm_one_back(
            shares[s][0], cores[s], nears[s], mine[s], grad_res, s, mod, gain_one_row, sums
        )
        grad_tokens.append(grad)
        return rounded, sums

    def give_back(s, rounded):
        moved.append(send_across(rounded))

    waits, weights = [], [None]
    for s in range(parts):
        act_t, queries, keys, values, logs = saved[s]
        keep, send, *weights = attend_back(
            places[s], after(queries, *waits), keys, values, grad_mix, s, logs, cosine,
            sine, w_qkv, act_t, weights[0], s == parts - 1, dp_size,
        )
        if s == 0:
            send, weights, mlp.got = tie((send, weights, mlp.got))
        elif s == 1:
            send, weights, mlp.got, nears[0], output_moved = tie(
                (send, weights, mlp.got, nears[0], output_moved)
            )
        else:
            send, weights, mlp.got, nears[1], moved[0] = tie(
                (send, weights, mlp.got, nears[1], moved[0])
            )
        shares.append((keep, send))
        cores.append(dp_swap(send, 0))
        if s == parts - 1:
            break
        if mlp.orders[0]:
            waits = list(mlp.merge(BF if s == 0 else F32))
            mlp.move()
        if s:
            rounded, sums = finish(s - 1, sums)
            give_back(s - 1, rounded)
            waits.append(rounded)
        waits.append(pass_on(s))

    while mlp.orders[0]:
        mlp.merge()
        mlp.move()
    att = Halving([weights[0], weights[2]], [weights[1], weights[3]], 1)
    rounded, sums = finish(parts - 2, sums)
    cores[-1] = after(cores[-1], rounded)
    passed = pass_on(parts - 1)
    give_back(parts - 2, after(rounded, passed))
    att.got = tie((att.got, passed))[0]
    waits = att.merge()
    att.move()
    mlp.got = tie((mlp.got, *waits))[0]
    waits = mlp.spread(True)
    nears[-1], mlp.sends = tie((nears[-1], mlp.sends, *waits))[:2]
    mlp.send()
    rounded, sums = finish(parts - 1, sums)
    across = dp_swap(sums, 0)
    give_back(parts - 1, rounded)
    waits = [rounded]
    while att.orders[0]:
        att.got = tie((att.got, *waits))[0]
        waits = att.merge()
        att.move()
    held = sums + after(across, *waits)
    across = seq_swap(held, 0)
    mlp.got, moved[-2] = tie((mlp.got, moved[-2], held))[:2]
    further = (mlp.own[1] + mlp.got[0][1].astype(F32)).astype(BF)
    att.got = tie((att.got, further))[0]
    waits = att.spread(True)
    held = held + after(across, *waits)
    att.send()
    further = seq_swap(further, 1)
    count, kept = 6 * parts, held.shape[0] - 7
    conds = cond_here.astype(F32).reshape(1, -1)
    conds = jnp.pad(conds, ((0, 0), (0, width - conds.shape[1])))
    ours = jnp.concatenate([held[:kept], conds]).astype(BF)[None]
    got = swap(ours, "seq", 1)
    mod_here = jnp.where(stays, held[:count], got[0, :count].astype(F32))
    ours = jnp.concatenate([ours, got])
    for bit in forth:
        got = swap(ours, "dp", bit)
        if bit == forth[0]:
            att.got = tie((att.got, ours))[0]
            later = (att.own[1] + att.got[0][1].astype(F32)).astype(BF)
            got = after(got, later)
            later = seq_swap(later, 1)
        ours = jnp.concatenate([ours, got])
    ours = ours.astype(F32)
    totals = jnp.sum(ours[:, count:kept], axis=0)
    output, g_tokens = put(puts, output, output_moved, grad_tokens, tie((tuple(moved), ours))[0])
    piece = width // (dp_size * seq_size)
    tall = hidden // (dp_size * seq_size)
    shapes = [
        jax.ShapeDtypeStruct((piece, hidden), F32),
        jax.ShapeDtypeStruct((piece, width), F32),
        jax.ShapeDtypeStruct((tall, width), F32),
    ]
    g_w_up, g_w_out, g_w_down = place_weights(
        place_mlp_kernel, mlp.own, mlp.got[0], after(further, g_tokens), shapes
    )
    shapes = [jax.ShapeDtypeStruct((piece, 3 * width), F32)]
    (g_w_qkv,) = place_weights(
        place_att_kernel, att.own, att.got[0], after(later, g_w_out), shapes
    )

    w_ada_f = w_ada.astype(F32)
    g_cond = sum(
        jnp.dot(
            mod_here[k * parts : (k + 1) * parts],
            w_ada_f[:, k * width : (k + 1) * width].T,
            precision=HIGH,
        )
        for k in range(6)
    )
    chosen = order[:parts, None] == jnp.arange(parts)[None, :]
    g_cond = jnp.sum(jnp.where(chosen[:, :, None], g_cond[:, None], 0.0), axis=0)
    groups = ours.shape[0]
    conds = ours[:, kept, : cond_here.size].reshape(groups * parts, -1)
    lanes = ours[:, :count].reshape(groups, 6, parts, width).transpose(0, 2, 1, 3)
    lanes = lanes.reshape(groups * parts, 6 * width)
    shards = dp_size * seq_size
    index = dp * seq_size + seq

    def mine_of(value):
        size = value.shape[-1] // shards
        starts = (jnp.int32(0),) * (value.ndim - 1) + (index * size,)
        sizes = value.shape[:-1] + (size,)
        return lax.dynamic_slice(value, starts, sizes, allow_negative_indices=False)

    lanes = mine_of(lanes)
    g_w_ada = jnp.dot(conds.T, lanes, precision=HIGH)
    g_b_ada = jnp.sum(lanes, axis=0)
    g_b_down, g_gain_two, g_gain_one = mine_of(totals[0]), mine_of(totals[1]), mine_of(totals[-1])
    g_b_up = mine_of(totals[2:-1].reshape(-1))
    return (
        output,
        g_tokens,
        g_cond,
        g_gain_one,
        g_gain_two,
        g_w_ada,
        g_b_ada,
        g_w_qkv,
        g_w_out,
        g_w_up,
        g_b_up,
        g_w_down,
        g_b_down,
    )


def solution(mesh):
    shards = ("dp", "seq")
    placed = (
        (P("dp", "seq", None), P("dp", None), P("dp"))
        + (P(),) * 10
        + (P("dp", "seq", None),)
    )
    return jax.shard_map(
        functools.partial(body, mesh.shape["dp"], mesh.shape["seq"]),
        mesh=mesh,
        in_specs=placed,
        out_specs=(
            P("dp", "seq", None),
            P("dp", "seq", None),
            P("dp", None),
            P(shards),
            P(shards),
            P(None, shards),
            P(shards),
            P(shards, None),
            P(shards, None),
            P(shards, None),
            P(shards),
            P(shards, None),
            P(shards),
        ),
        check_vma=False,
    )
```

```python
import functools

import jax
import jax.numpy as jnp
import numpy as np
from jax import lax
from jax.experimental import pallas as pl
from jax.experimental.pallas import tpu as pltpu
from jax.sharding import PartitionSpec as P

HEADS = 12
HD = 64
EPS = 1e-05
HIGH = lax.Precision.HIGHEST
BF = jnp.bfloat16
F32 = jnp.float32
PACK = 4
BLOCK = PACK * HD
LANES = 128
SPANS = (128, 512, 1024)
SCALE = 1000
GELU_C = float(np.sqrt(2.0 / np.pi))


def nn(left, right):
    return lax.dot_general(left, right, (((1,), (0,)), ((), ())), preferred_element_type=F32)


def nt(left, right):
    return lax.dot_general(left, right, (((1,), (1,)), ((), ())), preferred_element_type=F32)


def normalize(vector):
    average = jnp.mean(vector, axis=-1, keepdims=True)
    centred = vector - average
    inverse = lax.rsqrt(jnp.mean(centred * centred, axis=-1, keepdims=True) + EPS)
    return centred * inverse, inverse


def norm_back(grad_normed, normed, inverse):
    return inverse * (
        grad_normed
        - jnp.mean(grad_normed, axis=-1, keepdims=True)
        - normed * jnp.mean(grad_normed * normed, axis=-1, keepdims=True)
    )


def rows_sum(value):
    return jnp.sum(value, axis=0, keepdims=True)


def head_masks():
    lane = lax.broadcasted_iota(jnp.int32, (1, BLOCK), 1)
    return [(lane // HD == h).astype(F32).astype(BF) for h in range(PACK)]


def swap_halves(value):
    half = HD // 2
    lane = lax.broadcasted_iota(jnp.int32, value.shape, 1)
    ahead = pltpu.roll(value, LANES - half, 1)
    behind = pltpu.roll(value, half, 1)
    return jnp.where(lane % HD < half, ahead, behind)


def arrange_kernel(lengths, tok_ref, cond_ref, *refs):
    parts = tok_ref.shape[0]
    first_ref, rest_ref, both_ref, order_ref = refs
    rank = []
    for s in range(parts):
        ahead = jnp.int32(0)
        for k in range(parts):
            if k < s:
                ahead = ahead + (lengths[k] >= lengths[s]).astype(jnp.int32)
            elif k > s:
                ahead = ahead + (lengths[k] > lengths[s]).astype(jnp.int32)
        rank.append(ahead)
    both_ref[...] = jnp.zeros_like(both_ref)
    for r in range(parts):
        at = jnp.int32(0)
        for k in range(1, parts):
            at = jnp.where(rank[k] == r, k, at)
        if r == 0:
            first_ref[0] = tok_ref[at]
        else:
            rest_ref[r - 1] = tok_ref[at]
        width = cond_ref.shape[1]
        both_ref[r : r + 1, :width] = cond_ref[pl.ds(at, 1), :]
        both_ref[r : r + 1, width:] = jnp.full((1, LANES), lengths[at]).astype(F32)
        order_ref[r] = at
        order_ref[parts + r] = rank[r]


def arrange_pulls_kernel(order, pull_ref, out_ref):
    for r in range(pull_ref.shape[0]):
        out_ref[r] = pull_ref[order[r]]


def put_kernel(order, *refs):
    parts = (order.shape[0] - 1)
    step = pl.program_id(0)
    value_ref, moved_ref = refs[:2]
    grads, moves = refs[2 : 2 + parts], refs[2 + parts : 2 + 2 * parts]
    out_ref, grad_ref = refs[2 + 2 * parts :]
    stays = order[parts] == 1
    out_ref[...] = jnp.where(stays, value_ref[...], moved_ref[...])
    for s in range(parts):

        @pl.when((step == s) & stays)
        def _():
            grad_ref[0] = grads[s][...]

        @pl.when((step == s) & ~stays)
        def _():
            grad_ref[0] = moves[s][...].astype(F32)


def front_kernel(
    place, a_ref, b_ref, c_ref, d_ref, mod_ref, gain_ref, w_ref, cos_ref, sin_ref,
    actt_ref, q_ref, k_ref, v_ref, mix_ref, lse_ref, queries, keys, values,
):
    step, length = pl.program_id(1), place[1 + pl.program_id(0)]
    rows, width = a_ref.shape
    groups = width // BLOCK
    chunk = place[0] ^ jnp.minimum(step, 3)
    here = pl.ds(pl.multiple_of(chunk * rows, rows), rows)

    def turned(act, start, group):
        at = start + group * BLOCK
        both = nn(act, w_ref[:, at : at + BLOCK])
        cosine, sine = cos_ref[...], sin_ref[...]
        parts = []
        for lane in range(0, BLOCK, LANES):
            part = both[:, lane : lane + LANES]
            parts.append((part * cosine + swap_halves(part) * sine).astype(BF))
        return jnp.concatenate(parts, axis=1)

    @pl.when(step < 4)
    def _():
        source = jnp.where(
            step < 2,
            jnp.where(step == 0, a_ref[...], b_ref[...]),
            jnp.where(step == 2, c_ref[...], d_ref[...]),
        ).astype(F32)
        normed, _ = normalize(source)
        act = (normed * gain_ref[...] * (1.0 + mod_ref[0, 1:2, :]) + mod_ref[0, 0:1, :]).astype(BF)
        actt_ref[...] = act.T

        @pl.when(chunk * rows < length)
        def _():
            for group in range(groups):
                lanes = slice(group * BLOCK, (group + 1) * BLOCK)
                key = turned(act, width, group)
                k_ref[:, lanes] = key
                keys[group, here, :] = key
                at = 2 * width + group * BLOCK
                value = nn(act, w_ref[:, at : at + BLOCK]).astype(BF)
                v_ref[:, lanes] = value
                values[group, here, :] = value

        @pl.when(step == 0)
        def _():
            for group in range(groups):
                query = turned(act, 0, group) * BF(HD**-0.5)
                q_ref[:, group * BLOCK : (group + 1) * BLOCK] = query
                queries[group] = query

    masks = head_masks()
    lane = lax.broadcasted_iota(jnp.int32, (1, BLOCK), 1)
    narrow = lax.broadcasted_iota(jnp.int32, (1, LANES), 1)

    def work(span):
        group = step - 4
        query = queries[group]
        stacked = jnp.concatenate([query * masks[h] for h in range(PACK)], axis=0)
        scores = nt(stacked, keys[group, :span, :])
        top = jnp.max(scores, axis=-1, keepdims=True)
        raised = jnp.exp(scores - top)
        total = jnp.sum(raised, axis=-1, keepdims=True)
        probs = (raised * (1.0 / total)).astype(BF)
        level = top + jnp.log(total)
        logs = jnp.zeros((rows, LANES), F32)
        result = jnp.zeros((rows, BLOCK), F32)
        for head in range(PACK):
            part = slice(head * rows, (head + 1) * rows)
            result = jnp.where(lane // HD == head, nn(probs[part], values[group, :span, :]), result)
            logs = jnp.where(narrow == head, level[part], logs)
        mix_ref[...] = result.astype(BF)
        lse_ref[0] = logs.T[:8, :]

    for span in SPANS:
        pl.when((step >= 4) & (length == span))(functools.partial(work, span))


def attend_back_kernel(
    more, last, place, q_ref, k_ref, v_ref, g_ref, lse_ref, cosq_ref, sinq_ref, cosk_ref, sink_ref,
    wq_ref, wk_ref, wv_ref, actt_ref, owns_ref, *refs,
):
    refs = list(refs)
    before_ref = refs.pop(0) if more else None
    keep_ref, send_ref = refs.pop(0), refs.pop(0)
    outs = [refs.pop(0) for _ in range(4 if last else 1)]
    share, own_share, grad_q, grad_k, grad_v, weights = refs
    masks = head_masks()
    group = pl.program_id(0)
    rows = q_ref.shape[0]

    def unturn(value, cosine, sine, out_ref):
        for lane in range(0, BLOCK, LANES):
            part = value[:, lane : lane + LANES]
            out_ref[: value.shape[0], lane : lane + LANES] = (
                part * cosine - swap_halves(part) * sine
            ).astype(BF)

    @pl.when(group == 0)
    def _():
        share[...] = jnp.zeros_like(share)
        own_share[...] = jnp.zeros_like(own_share)

    def work(span):
        queries, grads = q_ref[...], g_ref[...]
        query_all = jnp.concatenate([queries * masks[h] for h in range(PACK)], axis=0)
        grad_all = jnp.concatenate([grads * masks[h] for h in range(PACK)], axis=0)
        head = lax.broadcasted_iota(jnp.int32, (BLOCK, 1), 0) // HD
        sides = [(head == h).astype(F32).astype(BF) for h in range(PACK)]
        queries_t, grads_t = queries.T, grads.T
        query_t = jnp.concatenate([queries_t * sides[h] for h in range(PACK)], axis=1)
        grad_t = jnp.concatenate([grads_t * sides[h] for h in range(PACK)], axis=1)
        keys, values = k_ref[:span, :], v_ref[:span, :]
        keys_t = keys.T
        raw_all, pull_all = nn(keys, query_t), nn(values, grad_t)
        turned, probs_all, scores_all = [], [], []
        for h in range(PACK):
            part = slice(h * rows, (h + 1) * rows)
            probs = jnp.exp(raw_all[:, part] - lse_ref[0, h : h + 1, :])
            pull = pull_all[:, part]
            scores = (probs * (pull - rows_sum(probs * pull))).astype(BF)
            probs_all.append(probs.astype(BF))
            scores_all.append(scores)
            turned.append(nn(keys_t[h * HD : (h + 1) * HD], scores))
        grad_v[:span, :] = nn(jnp.concatenate(probs_all, axis=1), grad_all).astype(BF)
        grad_keys = nn(jnp.concatenate(scores_all, axis=1), query_all)
        unturn(grad_keys, cosk_ref[:span, :], sink_ref[:span, :], grad_k)
        grad_queries = jnp.concatenate(turned, axis=0).T * HD**-0.5
        unturn(grad_queries, cosq_ref[...], sinq_ref[...], grad_q)
        share[:span, :] += nt(grad_k[:span, :], wk_ref[...]) + nt(grad_v[:span, :], wv_ref[...])
        act = actt_ref[:, :span]
        products = (
            nn(owns_ref[...], grad_q[...]),
            nn(act, grad_k[:span, :]),
            nn(act, grad_v[:span, :]),
        )
        for which, product in enumerate(products):
            lanes = slice(which * BLOCK, (which + 1) * BLOCK)
            if more:
                product = product + before_ref[0, :, lanes]
            if last:
                weights[:, lanes] = product
            else:
                outs[0][0, :, lanes] = product

    for span in SPANS:
        pl.when(place[1] == span)(functools.partial(work, span))
    own_share[...] += nt(grad_q[...], wq_ref[...])
    if last:
        cut = 2 * BLOCK + LANES
        first = jnp.concatenate([weights[:, :BLOCK], weights[:, 2 * BLOCK : cut]], axis=1)
        other = jnp.concatenate([weights[:, BLOCK : 2 * BLOCK], weights[:, cut:]], axis=1)
        part_rows(first, place[2], outs[0], outs[1])
        part_rows(other, place[2], outs[2], outs[3])

    @pl.when(group == pl.num_programs(0) - 1)
    def _():
        def piece(k):
            return share[pl.ds(pl.multiple_of((place[0] ^ k) * rows, rows), rows), :]

        keep_ref[0] = piece(0) + own_share[...]
        keep_ref[1] = piece(1)
        send_ref[0] = piece(2).astype(BF)
        send_ref[1] = piece(3).astype(BF)


def norm_back_kernel(
    s, parts, keep_ref, core_ref, near_ref, tok_ref, gres_ref, mod_ref, gain_ref, before_ref,
    grad_ref, send_ref, sums_ref,
):
    def add(row, value):
        sums_ref[row : row + 1, :] = before_ref[row : row + 1, :] + rows_sum(value)

    pull = keep_ref[0] + core_ref[0].astype(F32) + near_ref[...].astype(F32)
    normed, inverse = normalize(tok_ref[...].astype(F32))
    gain = gain_ref[...]
    sums_ref[...] = before_ref[...]
    add(s, pull)
    add(parts + s, pull * (normed * gain))
    scaled = pull * (1.0 + mod_ref[0, 1:2, :])
    add(sums_ref.shape[0] - 8, scaled * normed)
    grad = gres_ref[0] + norm_back(scaled * gain, normed, inverse)
    grad_ref[...] = grad
    send_ref[...] = grad.astype(BF)


def part_rows(value, core, keep_ref, send_ref):
    blocks, piece, columns = keep_ref.shape
    both = value.reshape(blocks, 2, piece, columns)
    keep_ref[...] = jnp.where(core == 0, both[:, 0], both[:, 1]).astype(keep_ref.dtype)
    send_ref[...] = jnp.where(core == 0, both[:, 1], both[:, 0]).astype(BF)


def combine_kernel(index, *refs):
    for which in range(2):
        mine, got, other, other_got = refs[4 * which : 4 * which + 4]
        keep_ref, send_ref = refs[8 + 2 * which : 10 + 2 * which]
        keep_ref[...] = (mine[...].astype(F32) + got[...].astype(F32)).astype(keep_ref.dtype)
        send_ref[...] = (other[...].astype(F32) + other_got[...].astype(F32)).astype(BF)


def spread_kernel(place, keep_a, got_a, keep_b, got_b, *out_refs):
    rows, wide = keep_a.shape[1:]
    columns = keep_b.shape[2]
    if len(out_refs) == 2:
        out_refs = (out_refs[0].at[0], out_refs[1].at[0], out_refs[0].at[1], out_refs[1].at[1])
    for turn, out_ref in enumerate(out_refs):
        at = place[0] ^ turn
        out_ref[:, :wide] = (keep_a[at].astype(F32) + got_a[at].astype(F32)).astype(out_ref.dtype)
        below = keep_b[at].astype(F32) + got_b[at].astype(F32)
        for k in range(keep_b.shape[1] // rows):
            lanes = slice(wide + k * columns, wide + (k + 1) * columns)
            out_ref[:, lanes] = below[k * rows : (k + 1) * rows].astype(out_ref.dtype)


def place_mlp_kernel(own_ref, near_ref, far_ref, up_ref, out_ref, down_ref):
    total = own_ref[0] + near_ref[0].astype(F32) + far_ref[...].astype(F32)
    rows, hidden = up_ref.shape
    width = out_ref.shape[1]
    up_ref[...] = total[:, :hidden]
    out_ref[...] = total[:, hidden : hidden + width]
    for k in range(down_ref.shape[0] // rows):
        at = hidden + (k + 1) * width
        down_ref[k * rows : (k + 1) * rows, :] = total[:, at : at + width]


def place_att_kernel(own_ref, near_ref, far_ref, qkv_ref):
    total = own_ref[0] + near_ref[0].astype(F32) + far_ref[...].astype(F32)
    width = qkv_ref.shape[1] // 3
    step, side = BLOCK + LANES, width // BLOCK * (BLOCK + LANES)
    for j in range(width // BLOCK):
        for which in range(2):
            at = which * side + j * step
            to = which * width + j * BLOCK
            qkv_ref[:, to : to + BLOCK] = total[:, at : at + BLOCK]
            to = 2 * width + j * BLOCK + which * LANES
            qkv_ref[:, to : to + LANES] = total[:, at + BLOCK : at + step]


def mlp_kernel(
    core, mix0_ref, mix1_ref, mix2_ref, tok0_ref, tok1_ref, tok2_ref, cot_ref, mod_ref, gain_ref, wout_ref, bdown_ref,
    wup_ref, bup_ref, wdown_ref,
    out_ref, gres_ref, gmix_ref, sums_ref,
    keepup_ref, sendup_ref, keepdown_ref, senddown_ref,
    resid, branch, act, act_t, slope, active, second, gsecond, gact, gpre,
):
    step = pl.program_id(0)
    tiles = pl.num_programs(0) // 2
    parts, rows, _ = cot_ref.shape
    mixes, tokens = (mix0_ref, mix1_ref, mix2_ref), (tok0_ref, tok1_ref, tok2_ref)

    def span(s):
        return slice(s * rows, (s + 1) * rows)

    def mod(s, which):
        return mod_ref[s, which : which + 1, :]

    @pl.when(step == 0)
    def _():
        sums_ref[...] = jnp.zeros_like(sums_ref)
        for s in range(parts):
            one = nn(mixes[s][...], wout_ref[...])
            res = tokens[s][...].astype(F32) + mod(s, 2) * one
            branch[span(s), :] = one
            resid[span(s), :] = res
            normed, _ = normalize(res)
            value = (normed * gain_ref[...] * (1.0 + mod(s, 4)) + mod(s, 3)).astype(BF)
            act[span(s), :] = value
            act_t[:, span(s)] = value.T
            second[span(s), :] = jnp.zeros_like(res)
            gact[span(s), :] = jnp.zeros_like(res)

    @pl.when(step < tiles)
    def _():
        for s in range(parts):
            u = nn(act[span(s), :], wup_ref[...]) + bup_ref[...]
            square = u * u
            bent = jnp.tanh(GELU_C * (u + 0.044715 * (square * u)))
            value = (0.5 * u * (1.0 + bent)).astype(BF)
            slope[step, span(s), :] = 0.5 * (1.0 + bent) + 0.5 * u * (1.0 - bent * bent) * (
                GELU_C * (1.0 + 3 * 0.044715 * square)
            )
            active[step, span(s), :] = value
            second[span(s), :] += nn(value, wdown_ref[...])

    @pl.when(step == tiles - 1)
    def _():
        total = jnp.zeros(bdown_ref.shape, F32)
        for s in range(parts):
            two = second[span(s), :] + bdown_ref[...]
            out_ref[s] = (resid[span(s), :] + mod(s, 5) * two).astype(BF)
            pull = cot_ref[s].astype(F32)
            sums_ref[5 * parts + s : 5 * parts + s + 1, :] = rows_sum(pull * two)
            down = (pull * mod(s, 5)).astype(BF)
            gsecond[span(s), :] = down
            total = total + rows_sum(down.astype(F32))
        sums_ref[6 * parts : 6 * parts + 1, :] = total

    @pl.when((step >= tiles) & (step < 2 * tiles))
    def _():
        at = step - tiles
        total = jnp.zeros(bup_ref.shape, F32)
        for s in range(parts):
            pulled = nt(gsecond[span(s), :], wdown_ref[...])
            value = (pulled * slope[at, span(s), :]).astype(BF)
            gpre[span(s), :] = value
            total = total + rows_sum(value.astype(F32))
            gact[span(s), :] += nt(value, wup_ref[...])
        sums_ref[pl.ds(6 * parts + 2 + at, 1), :] = total
        part_rows(nn(active[at].T, gsecond[...]), core[0], keepdown_ref, senddown_ref)
        part_rows(nn(act_t[...], gpre[...]), core[0], keepup_ref, sendup_ref)

    @pl.when(step == 2 * tiles)
    def _():
        total = jnp.zeros(bdown_ref.shape, F32)
        outer = jnp.zeros(resid.shape[1:] * 2, F32)
        for s in range(parts):
            normed, inverse = normalize(resid[span(s), :])
            pull = gact[span(s), :]
            sums_ref[3 * parts + s : 3 * parts + s + 1, :] = rows_sum(pull)
            sums_ref[4 * parts + s : 4 * parts + s + 1, :] = rows_sum(
                pull * (normed * gain_ref[...])
            )
            scaled = pull * (1.0 + mod(s, 4))
            total = total + rows_sum(scaled * normed)
            grad = cot_ref[s].astype(F32) + norm_back(scaled * gain_ref[...], normed, inverse)
            gres_ref[s] = grad
            sums_ref[2 * parts + s : 2 * parts + s + 1, :] = rows_sum(grad * branch[span(s), :])
            one = (grad * mod(s, 2)).astype(BF)
            gmix_ref[s] = nt(one, wout_ref[...]).astype(BF)
            outer = outer + nn(mixes[s][...].T, one)
        part_rows(outer, core[0], keepup_ref, sendup_ref)
        sums_ref[6 * parts + 1 : 6 * parts + 2, :] = total


def whole(array):
    rank = array.ndim
    return pl.BlockSpec(array.shape, lambda *_: (0,) * rank, pipeline_mode=pl.Buffered(1))


def limits(mib=60):
    return pltpu.CompilerParams(vmem_limit_bytes=mib * 2**20)


def cost(flops, bytes_accessed):
    return pl.CostEstimate(
        flops=int(flops) // SCALE, bytes_accessed=int(bytes_accessed) // SCALE, transcendentals=0
    )


def arrange(lengths, tokens, cond):
    parts, rows, width = tokens.shape
    shapes = [jax.ShapeDtypeStruct((n, rows, width), BF) for n in (1, parts - 1)]
    shapes.append(jax.ShapeDtypeStruct((8, cond.shape[1] + LANES), F32))
    return pl.pallas_call(
        arrange_kernel,
        grid_spec=pltpu.PrefetchScalarGridSpec(
            num_scalar_prefetch=1,
            grid=(1,),
            in_specs=[whole(tokens), whole(cond)],
            out_specs=[whole(v) for v in shapes] + [pl.BlockSpec(memory_space=pltpu.SMEM)],
        ),
        out_shape=shapes + [jax.ShapeDtypeStruct((2 * parts,), jnp.int32)],
        compiler_params=limits(32),
        cost_estimate=cost(1e6, 3e6),
        name="arrange",
    )(lengths, tokens, cond)


def arrange_pulls(order, pulls):
    return pl.pallas_call(
        arrange_pulls_kernel,
        grid_spec=pltpu.PrefetchScalarGridSpec(
            num_scalar_prefetch=1,
            grid=(1,),
            in_specs=[whole(pulls)],
            out_specs=whole(pulls),
        ),
        out_shape=jax.ShapeDtypeStruct(pulls.shape, BF),
        compiler_params=limits(32),
        cost_estimate=cost(1e6, 3e6),
        name="arrange_pulls",
    )(order, pulls)


def put(order, value, moved, grads, moves):
    parts, rows, width = value.shape
    block = pl.BlockSpec((1, rows, width), lambda i, p: (i, 0, 0))
    placed = pl.BlockSpec((1, rows, width), lambda i, p: (p[i], 0, 0))
    return pl.pallas_call(
        put_kernel,
        grid_spec=pltpu.PrefetchScalarGridSpec(
            num_scalar_prefetch=1,
            grid=(parts,),
            in_specs=[block, block] + [whole(v) for v in list(grads) + list(moves)],
            out_specs=[placed, placed],
        ),
        out_shape=[
            jax.ShapeDtypeStruct(value.shape, BF),
            jax.ShapeDtypeStruct(value.shape, F32),
        ],
        compiler_params=limits(),
        cost_estimate=cost(1e6, 1e7),
        name="put",
    )(order, value, moved, *grads, *moves)


def front(place, pieces, mod, first, gain, w_qkv, cosine, sine):
    count, rows, width = pieces[0].shape
    slots, groups = 4 * rows, width // BLOCK
    chunk = lambda i, p: p[0] ^ jnp.minimum(i, 3)
    group = lambda i: jnp.maximum(i - 4, 0)
    table = pl.BlockSpec((rows, LANES), lambda s, i, p: (chunk(i, p), 0))
    piece = pl.BlockSpec((None, rows, width), lambda s, i, p: (s, chunk(i, p), 0))
    return pl.pallas_call(
        front_kernel,
        grid_spec=pltpu.PrefetchScalarGridSpec(
            num_scalar_prefetch=1,
            grid=(count, 4 + groups),
            in_specs=[pl.BlockSpec((None, rows, width), lambda s, i, p: (s, 0, 0))] * 4
            + [pl.BlockSpec((1,) + mod.shape[1:], lambda s, i, p: (first + s, 0, 0))]
            + [whole(gain), whole(w_qkv), table, table],
            out_specs=[
                pl.BlockSpec((None, width, rows), lambda s, i, p: (s, 0, chunk(i, p))),
                pl.BlockSpec((None, rows, width), lambda s, i, p: (s, 0, 0)),
                piece, piece,
                pl.BlockSpec((None, rows, BLOCK), lambda s, i, p: (s, 0, group(i))),
                pl.BlockSpec((None, 1, 8, rows), lambda s, i, p: (s, group(i), 0, 0)),
            ],
            scratch_shapes=[
                pltpu.VMEM((groups, rows, BLOCK), BF),
                pltpu.VMEM((groups, slots, BLOCK), BF),
                pltpu.VMEM((groups, slots, BLOCK), BF),
            ],
        ),
        out_shape=[
            jax.ShapeDtypeStruct((count, width, slots), BF),
            jax.ShapeDtypeStruct((count, rows, width), BF),
            jax.ShapeDtypeStruct((count, slots, width), BF),
            jax.ShapeDtypeStruct((count, slots, width), BF),
            jax.ShapeDtypeStruct((count, rows, width), BF),
            jax.ShapeDtypeStruct((count, groups, 8, rows), F32),
        ],
        compiler_params=limits(40),
        cost_estimate=cost(2 * count * slots * width * width * 3, 15e6 * count),
        name="front",
    )(place, *pieces, mod, gain, w_qkv, cosine, sine)


def attend_back(
    place, at, queries, keys, values, grads, s, logs, cosine, sine, w_qkv, act_t, before, last, dp_size
):
    _, rows, width = queries.shape
    slots = keys.shape[1]
    groups = width // BLOCK
    own = pl.BlockSpec((None, rows, BLOCK), lambda j, p: (at, 0, j))
    full = pl.BlockSpec((None, slots, BLOCK), lambda j, p: (at, 0, j))
    own_table = pl.BlockSpec((rows, LANES), lambda j, p: (p[0], 0))
    full_table = pl.BlockSpec((slots, LANES), lambda j, p: (0, 0))
    every = pl.BlockSpec((1, width, 3 * BLOCK), lambda j, p: (j, 0, 0))
    blocks, piece, columns = dp_size // 2, width // dp_size, BLOCK + LANES
    more = before is not None
    if last:
        part = (blocks, piece, groups * columns)
        weight_specs = [pl.BlockSpec((blocks, piece, columns), lambda j, p: (0, 0, j))] * 4
        weight_shapes = [jax.ShapeDtypeStruct(part, F32), jax.ShapeDtypeStruct(part, BF)] * 2
    else:
        weight_specs = [every]
        weight_shapes = [jax.ShapeDtypeStruct((groups, width, 3 * BLOCK), F32)]
    return pl.pallas_call(
        functools.partial(attend_back_kernel, more, last),
        grid_spec=pltpu.PrefetchScalarGridSpec(
            num_scalar_prefetch=1,
            grid=(groups,),
            in_specs=[
                own, full, full,
                pl.BlockSpec((None, rows, BLOCK), lambda j, p: (s, 0, j)),
                pl.BlockSpec((None, 1, 8, rows), lambda j, p: (at, j, 0, 0)),
                own_table, own_table, full_table, full_table,
                pl.BlockSpec((width, BLOCK), lambda j, p: (0, j)),
                pl.BlockSpec((width, BLOCK), lambda j, p: (0, groups + j)),
                pl.BlockSpec((width, BLOCK), lambda j, p: (0, 2 * groups + j)),
                pl.BlockSpec(
                    (None, width, slots), lambda j, p: (at, 0, 0), pipeline_mode=pl.Buffered(1)
                ),
                pl.BlockSpec((None, width, rows), lambda j, p: (at, 0, p[0])),
            ]
            + [every] * more,
            out_specs=[pl.BlockSpec((2, rows, width), lambda j, p: (0, 0, 0))] * 2 + weight_specs,
            scratch_shapes=[
                pltpu.VMEM((slots, width), F32),
                pltpu.VMEM((rows, width), F32),
                pltpu.VMEM((rows, BLOCK), BF),
                pltpu.VMEM((slots, BLOCK), BF),
                pltpu.VMEM((slots, BLOCK), BF),
                pltpu.VMEM((width, 3 * BLOCK), F32),
            ],
        ),
        out_shape=[
            jax.ShapeDtypeStruct((2, rows, width), F32),
            jax.ShapeDtypeStruct((2, rows, width), BF),
        ]
        + weight_shapes,
        compiler_params=limits(),
        cost_estimate=cost(60 * rows * slots * width, 12e6),
        name="attend_back",
    )(
        place, queries, keys, values, grads, logs, cosine, sine, cosine, sine, w_qkv, w_qkv,
        w_qkv, act_t, act_t, *([before] if more else []),
    )


def norm_one_back(keep, core_got, near_got, tokens, at, grad_res, s, mod, gain, sums):
    _, rows, width = tokens.shape
    first = pl.BlockSpec((1, rows, width), lambda i: (0, 0, 0))
    return pl.pallas_call(
        functools.partial(norm_back_kernel, s, mod.shape[0]),
        grid=(1,),
        in_specs=[
            first, first, whole(near_got),
            pl.BlockSpec((None, rows, width), lambda i: (at, 0, 0)),
            pl.BlockSpec((1, rows, width), lambda i: (s, 0, 0)),
            pl.BlockSpec((1,) + mod.shape[1:], lambda i: (s, 0, 0)),
            whole(gain), whole(sums),
        ],
        out_specs=[pl.BlockSpec((rows, width), lambda i: (0, 0))] * 2
        + [pl.BlockSpec(sums.shape, lambda i: (0, 0))],
        out_shape=[
            jax.ShapeDtypeStruct((rows, width), F32),
            jax.ShapeDtypeStruct((rows, width), BF),
            jax.ShapeDtypeStruct(sums.shape, F32),
        ],
        compiler_params=limits(24),
        cost_estimate=cost(40 * rows * width, 6e6),
        name="norm_one_back",
    )(keep, core_got, near_got, tokens, grad_res, mod, gain, sums)


def feed_forward(core, mixes, tokens, pulls, mod, gain, w_out, b_down, w_up, b_up, w_down, dp_size):
    parts, rows, width = pulls.shape
    hidden = w_up.shape[1]
    tile = width
    tiles = hidden // tile
    total = parts * rows
    single = [
        pl.BlockSpec(
            (None, rows, width), lambda i, c, at=at: (at, 0, 0), pipeline_mode=pl.Buffered(1)
        )
        for _, at in mixes + tokens
    ]
    blocks, piece = dp_size // 2, width // dp_size
    tall_piece = hidden // dp_size
    per_tile = tile // (2 * tall_piece)
    late = lambda i: jnp.maximum(i - tiles, 0)
    last = lambda i: jnp.minimum(late(i), tiles - 1)
    turn = lambda i: jnp.minimum(jnp.where(i < tiles, i, i - tiles), tiles - 1)
    wide = pl.BlockSpec((width, tile), lambda i, c: (0, turn(i)))
    bias = pl.BlockSpec((1, tile), lambda i, c: (0, turn(i)))
    tall = pl.BlockSpec((tile, width), lambda i, c: (turn(i), 0))
    out_wide = pl.BlockSpec((blocks, piece, tile), lambda i, c: (0, 0, late(i)))
    out_tall = pl.BlockSpec((per_tile, tall_piece, width), lambda i, c: (last(i), 0, 0))
    outs = [
        jax.ShapeDtypeStruct(pulls.shape, BF),
        jax.ShapeDtypeStruct(pulls.shape, F32),
        jax.ShapeDtypeStruct(pulls.shape, BF),
        jax.ShapeDtypeStruct((6 * parts + 2 + hidden // width + 8, width), F32),
        jax.ShapeDtypeStruct((blocks, piece, hidden + width), BF),
        jax.ShapeDtypeStruct((blocks, piece, hidden + width), BF),
        jax.ShapeDtypeStruct((blocks, tall_piece, width), BF),
        jax.ShapeDtypeStruct((blocks, tall_piece, width), BF),
    ]
    return pl.pallas_call(
        mlp_kernel,
        grid_spec=pltpu.PrefetchScalarGridSpec(
            num_scalar_prefetch=1,
            grid=(2 * tiles + 1,),
            in_specs=single + [whole(a) for a in (pulls, mod, gain, w_out, b_down)]
            + [wide, bias, tall],
            out_specs=[whole(o) for o in outs[:4]]
            + [out_wide, out_wide, out_tall, out_tall],
            scratch_shapes=[
                pltpu.VMEM((total, width), F32),
                pltpu.VMEM((total, width), F32),
                pltpu.VMEM((total, width), BF),
                pltpu.VMEM((width, total), BF),
                pltpu.VMEM((tiles, total, tile), F32),
                pltpu.VMEM((tiles, total, tile), BF),
                pltpu.VMEM((total, width), F32),
                pltpu.VMEM((total, width), BF),
                pltpu.VMEM((total, width), F32),
                pltpu.VMEM((total, tile), BF),
            ],
        ),
        out_shape=outs,
        compiler_params=limits(),
        cost_estimate=cost(2 * total * width * (6 * hidden + 3 * width), 50e6),
        name="feed_forward",
    )(core, *[v for v, _ in mixes + tokens], pulls, mod, gain, w_out, b_down, w_up, b_up, w_down)


def combine(index, streams, turns, kept):
    in_specs, out_specs, shapes, inputs = [], [], [], []
    for which, (keep, got) in enumerate(streams):
        above, _, below, rows, columns = keep.shape
        tile = columns // turns
        block = (None, None, None, rows, tile)

        def place(i, c, p, flip, which=which, below=below):
            return (i // below, 1 - p[which] if flip else p[which], i % below, 0, c)

        mine = pl.BlockSpec(block, functools.partial(place, flip=False))
        other = pl.BlockSpec(block, functools.partial(place, flip=True))
        out = pl.BlockSpec((None, rows, tile), lambda i, c, p: (i, 0, c))
        in_specs += [mine, mine, other, other]
        inputs += [keep, got, keep, got]
        out_specs += [out, out]
        shape = (above * below, rows, columns)
        shapes += [jax.ShapeDtypeStruct(shape, kept), jax.ShapeDtypeStruct(shape, BF)]
        steps = above * below
    return pl.pallas_call(
        combine_kernel,
        grid_spec=pltpu.PrefetchScalarGridSpec(
            num_scalar_prefetch=1, grid=(steps, turns), in_specs=in_specs, out_specs=out_specs
        ),
        out_shape=shapes,
        compiler_params=limits(60 if turns > 1 else 24),
        cost_estimate=cost(inputs[0].size * 4, inputs[0].size * 18),
        name="combine",
    )(index, *inputs)


def spread(place, keep_a, got_a, keep_b, got_b, paired):
    _, rows, wide = keep_a.shape
    columns = wide + keep_b[0].size // rows
    if paired:
        shapes = [jax.ShapeDtypeStruct((2, rows, columns), t) for t in (F32, BF)]
    else:
        shapes = [jax.ShapeDtypeStruct((rows, columns), t) for t in (F32, BF, BF, BF)]
    arrays = (keep_a, got_a, keep_b, got_b)
    return pl.pallas_call(
        spread_kernel,
        grid_spec=pltpu.PrefetchScalarGridSpec(
            num_scalar_prefetch=1,
            grid=(1,),
            in_specs=[whole(v) for v in arrays],
            out_specs=[whole(v) for v in shapes],
        ),
        out_shape=shapes,
        compiler_params=limits(24),
        cost_estimate=cost(columns * rows * 8, columns * rows * 40),
        name="spread",
    )(place, *arrays)


def place_weights(kernel, own, near, far, shapes):
    return pl.pallas_call(
        kernel,
        grid=(1,),
        in_specs=[pl.BlockSpec((1,) + far.shape, lambda i: (0, 0, 0))] * 2 + [whole(far)],
        out_specs=[whole(v) for v in shapes],
        out_shape=shapes,
        compiler_params=limits(24),
        cost_estimate=cost(far.size * 2, far.size * 12),
        name="place_weights",
    )(own, near, far)


def after(value, *others):
    return lax.optimization_barrier((value,) + others)[0]


def body(
    dp_size, seq_size,
    tokens, cond, lengths, gain_one, gain_two, w_ada, b_ada, w_qkv, w_out, w_up, b_up, w_down,
    b_down, cotangent,
):
    parts, rows, width = tokens.shape
    hidden = w_up.shape[1]
    slots = rows * seq_size
    dp_bits = dp_size.bit_length() - 1
    dp, seq = lax.axis_index("dp").astype(jnp.int32), lax.axis_index("seq").astype(jnp.int32)
    core, side = dp & 1, lax.shift_right_logical(seq, jnp.int32(seq_size.bit_length() - 2))
    stays = core == side
    own = jnp.where(stays, seq, seq ^ 2).astype(jnp.int32)

    def dp_swap(value, bit):
        return lax.ppermute(value, "dp", [(i, i ^ (1 << bit)) for i in range(dp_size)])

    def seq_swap(value, bit):
        return lax.ppermute(value, "seq", [(i, i ^ (1 << bit)) for i in range(seq_size)])

    def swap(value, axis, bit):
        return dp_swap(value, bit) if axis == "dp" else seq_swap(value, bit)

    def bit_of(axis, bit):
        return ((dp if axis == "dp" else seq) >> bit) & 1

    pairs = []
    for i in range(dp_size):
        for j in range(seq_size):
            if (i & 1) != j // (seq_size // 2):
                pairs.append((i * seq_size + j, (i ^ 1) * seq_size + (j ^ 2)))

    def send_across(value):
        return lax.ppermute(value, ("dp", "seq"), pairs)

    def settle(value, moved, *others):
        return jnp.where(stays, value, after(moved, *others).astype(value.dtype))

    def regroup(value, moving=None):
        return settle(value, send_across(value if moving is None else moving))

    first_tokens, rest_tokens, both, order = arrange(lengths, tokens, cond.astype(F32))

    puts = jnp.concatenate([order[:parts], stays.astype(jnp.int32)[None]])

    mine_first = regroup(first_tokens)
    both = jnp.where(stays, both, dp_swap(both, 0))
    cond_here, lengths_here = both[:parts, :-LANES].astype(BF), both[:, -1].astype(jnp.int32)
    mod = jnp.dot(cond_here, w_ada, preferred_element_type=F32) + b_ada
    mod = mod.reshape(parts, 6, width)
    places = [jnp.stack([own, lengths_here[s], core]).astype(jnp.int32) for s in range(parts)]
    core_index = core.astype(jnp.int32)[None]
    frequency = np.power(10000.0, -np.arange(HD // 2) * 2.0 / HD).astype(np.float32)
    angles = np.arange(slots).astype(np.float32)[:, None] * frequency[None, :]
    angles = angles.astype(np.float64)
    cosine = jnp.asarray(np.tile(np.cos(angles), (1, LANES // (HD // 2))).astype(np.float32))
    sine = np.sin(angles)
    sine = jnp.asarray(np.tile(np.concatenate([-sine, sine], 1), (1, LANES // HD)).astype(np.float32))
    gain_one_row, gain_two_row = gain_one[None, :], gain_two[None, :]

    tie = lax.optimization_barrier
    forth = list(range(1, dp_bits))
    back = forth[::-1]
    halves = [jnp.stack([bit_of("dp", i), bit_of("dp", j)]) for i, j in zip(forth, back)]
    own_seq = seq[None]
    first_place = jnp.concatenate([own[None], lengths_here[:1]])
    rest_place = jnp.concatenate([own[None], lengths_here[1:]])
    mine_first = after(
        mine_first, mod, *places, *halves, own_seq, puts, core_index, first_place, rest_place
    )
    near = seq_swap(mine_first, 0)
    moving = send_across(rest_tokens)
    far = dp_swap(mine_first, 0)
    mine_rest = settle(rest_tokens, moving)
    group = (mine_first, near, far, dp_swap(near, 0))
    mine_rest = after(mine_rest, *group)
    near_rest, far_rest = seq_swap(mine_rest, 0), dp_swap(mine_rest, 0)
    pulls = arrange_pulls(order, after(cotangent, mine_first))
    group = tie((group, mine_rest))[0]
    fronts = [front(first_place, group, mod, 0, gain_one_row, w_qkv, cosine, sine)]
    near_rest, far_rest, pulls, _ = tie((near_rest, far_rest, pulls, fronts[0][4]))
    pulled = send_across(after(pulls, near_rest))
    group = (mine_rest, near_rest, far_rest, dp_swap(near_rest, 0))
    fronts.append(front(rest_place, group, mod, 1, gain_one_row, w_qkv, cosine, sine))
    pulls = settle(pulls, pulled, fronts[1][4])
    where = [(0, 0)] + [(1, k) for k in range(parts - 1)]
    mine = [((mine_first, mine_rest)[f], at) for f, at in where]
    mixes = [(fronts[f][4], at) for f, at in where]

    output, grad_res, grad_mix, sums, keep_up, send_up, keep_down, send_down = feed_forward(
        core_index, mixes, mine, pulls, mod, gain_two_row, w_out,
        b_down[None, :], w_up, b_up[None, :], w_down, dp_size,
    )
    output_moved = send_across(output)

    class Halving:
        def __init__(self, arrays, sends, turns):
            self.arrays, self.sends, self.turns, self.at = arrays, sends, turns, [0, 0]
            self.orders = [list(forth), list(back)]
            self.names = [forth[::-1], forth[::-1]]
            self.move()

        def merge(self, kept=F32):
            streams, self.at = [], []
            index = halves[len(forth) - len(self.orders[0])]
            for which in range(2):
                bit = self.orders[which].pop(0)
                names = self.names[which]
                place = names.index(bit)
                names.pop(place)
                keep = self.arrays[which]
                shape = (2**place, 2, 2 ** (len(names) - place)) + keep.shape[1:]
                streams.append((keep.reshape(shape), self.got[which].reshape(shape)))
                self.at.append(bit)
            keep_a, send_a, keep_b, send_b = combine(index, streams, self.turns, kept)
            self.arrays, self.sends, self.turns = [keep_a, keep_b], [send_a, send_b], 1
            return self.sends

        def move(self):
            self.got = [dp_swap(v, bit) for v, bit in zip(self.sends, self.at)]

        def spread(self, paired):
            pieces = [
                v.reshape(seq_size, v.shape[1] // seq_size, v.shape[2]) for v in self.arrays + self.got
            ]
            self.own, *self.sends = spread(
                own_seq, pieces[0], pieces[2], pieces[1], pieces[3], paired
            )
            return self.sends

        def send(self):
            self.got = [
                lax.ppermute(v, "seq", [(i, i ^ k) for i in range(seq_size)])
                for k, v in enumerate(self.sends, 1)
            ]

    mlp = Halving([keep_up, keep_down], [send_up, send_down], 3)

    shares, cores, nears, grad_tokens, moved = [], [], [], [], []

    def pass_on(s):
        there = (shares[s][0][1] + cores[s][1].astype(F32)).astype(BF)
        nears.append(seq_swap(there, 0))
        return there

    def finish(s, sums):
        grad, rounded, sums = norm_one_back(
            shares[s][0], cores[s], nears[s], *mine[s], grad_res, s, mod, gain_one_row, sums
        )
        grad_tokens.append(grad)
        return rounded, sums

    def give_back(s, rounded):
        moved.append(send_across(rounded))

    waits, weights = [], [None]
    for s in range(parts):
        at = where[s][1]
        act_t, queries, keys, values, _, logs = fronts[where[s][0]]
        keep, send, *weights = attend_back(
            places[s], at, after(queries, *waits), keys, values, grad_mix, s, logs, cosine,
            sine, w_qkv, act_t, weights[0], s == parts - 1, dp_size,
        )
        if s == 0:
            send, weights, mlp.got = tie((send, weights, mlp.got))
        elif s == 1:
            send, weights, mlp.got, nears[0], output_moved = tie(
                (send, weights, mlp.got, nears[0], output_moved)
            )
        else:
            send, weights, mlp.got, nears[1], moved[0] = tie(
                (send, weights, mlp.got, nears[1], moved[0])
            )
        shares.append((keep, send))
        cores.append(dp_swap(send, 0))
        if s == parts - 1:
            break
        if mlp.orders[0]:
            waits = list(mlp.merge(BF if s == 0 else F32))
            mlp.move()
        if s:
            rounded, sums = finish(s - 1, sums)
            give_back(s - 1, rounded)
            waits.append(rounded)
        cores[-1] = after(cores[-1], *waits)
        waits.append(pass_on(s))

    while mlp.orders[0]:
        mlp.merge()
        mlp.move()
    waits = mlp.spread(True)
    mlp.send()
    att = Halving([weights[0], weights[2]], [weights[1], weights[3]], 1)
    cores[-1] = after(cores[-1], *waits)
    passed = pass_on(parts - 1)
    nears[-2] = after(nears[-2], passed)
    rounded, sums = finish(parts - 2, sums)
    give_back(parts - 2, rounded)
    att.got = tie((att.got, rounded))[0]
    waits = att.merge()
    att.move()
    while att.orders[0]:
        att.got = tie((att.got, *waits))[0]
        waits = att.merge()
        att.move()
    mlp.got, mlp.own = tie((mlp.got, mlp.own, *waits))[:2]
    further = (mlp.own[1] + mlp.got[0][1].astype(F32)).astype(BF)
    att.got = tie((att.got, further))[0]
    further = seq_swap(further, 1)
    waits = att.spread(True)
    att.send()
    nears[-1] = after(nears[-1], *waits)
    rounded, sums = finish(parts - 1, sums)
    give_back(parts - 1, rounded)
    held = sums + dp_swap(sums, 0)
    across = seq_swap(held, 0)
    att.got, att.own, moved[-2] = tie((att.got, att.own, moved[-2], held))[:3]
    later = (att.own[1] + att.got[0][1].astype(F32)).astype(BF)
    held = held + after(across, later)
    later = seq_swap(later, 1)

    count, kept = 6 * parts, held.shape[0] - 7
    conds = cond_here.astype(F32).reshape(1, -1)
    conds = jnp.pad(conds, ((0, 0), (0, width - conds.shape[1])))
    ours = jnp.concatenate([held[:kept], conds]).astype(BF)[None]
    got = swap(ours, "seq", 1)
    piece, tall = width // (dp_size * seq_size), hidden // (dp_size * seq_size)
    shapes = [
        jax.ShapeDtypeStruct((piece, hidden), F32),
        jax.ShapeDtypeStruct((piece, width), F32),
        jax.ShapeDtypeStruct((tall, width), F32),
    ]
    g_w_up, g_w_out, g_w_down = place_weights(
        place_mlp_kernel, mlp.own, mlp.got[0], after(further, ours), shapes
    )
    got = after(got, g_w_up)
    mod_here = jnp.where(stays, held[:count], got[0, :count].astype(F32))
    ours = jnp.concatenate([ours, got])
    for bit in forth:
        got = swap(ours, "dp", bit)
        if bit == forth[-1]:
            shapes = [jax.ShapeDtypeStruct((piece, 3 * width), F32)]
            (g_w_qkv,) = place_weights(
                place_att_kernel, att.own, att.got[0], after(later, ours), shapes
            )
            moved[-1] = after(moved[-1], g_w_qkv)
            output, g_tokens = put(puts, output, output_moved, grad_tokens, tuple(moved))
            got = after(got, g_tokens)
        ours = jnp.concatenate([ours, got])
    ours = ours.astype(F32)
    totals = jnp.sum(ours[:, count:kept], axis=0)
    g_cond = sum(
        jnp.dot(
            mod_here[k * parts : (k + 1) * parts],
            w_ada[:, k * width : (k + 1) * width].astype(F32).T,
            precision=HIGH,
        )
        for k in range(6)
    )
    chosen = order[:parts, None] == jnp.arange(parts)[None, :]
    g_cond = jnp.sum(jnp.where(chosen[:, :, None], g_cond[:, None], 0.0), axis=0)
    groups = ours.shape[0]
    conds = ours[:, kept, : cond_here.size].reshape(groups * parts, -1)
    lanes = ours[:, :count].reshape(groups, 6, parts, width).transpose(0, 2, 1, 3)
    lanes = lanes.reshape(groups * parts, 6 * width)
    shards = dp_size * seq_size
    index = dp * seq_size + seq

    def mine_of(value):
        size = value.shape[-1] // shards
        starts = (jnp.int32(0),) * (value.ndim - 1) + (index * size,)
        sizes = value.shape[:-1] + (size,)
        return lax.dynamic_slice(value, starts, sizes, allow_negative_indices=False)

    lanes = mine_of(lanes)
    g_w_ada = jnp.dot(conds.T, lanes, precision=HIGH)
    g_b_ada = jnp.sum(lanes, axis=0)
    g_b_down, g_gain_two, g_gain_one = mine_of(totals[0]), mine_of(totals[1]), mine_of(totals[-1])
    g_b_up = mine_of(totals[2:-1].reshape(-1))
    return (
        output,
        g_tokens,
        g_cond,
        g_gain_one,
        g_gain_two,
        g_w_ada,
        g_b_ada,
        g_w_qkv,
        g_w_out,
        g_w_up,
        g_b_up,
        g_w_down,
        g_b_down,
    )


def solution(mesh):
    shards = ("dp", "seq")
    placed = (
        (P("dp", "seq", None), P("dp", None), P("dp"))
        + (P(),) * 10
        + (P("dp", "seq", None),)
    )
    return jax.shard_map(
        functools.partial(body, mesh.shape["dp"], mesh.shape["seq"]),
        mesh=mesh,
        in_specs=placed,
        out_specs=(
            P("dp", "seq", None),
            P("dp", "seq", None),
            P("dp", None),
            P(shards),
            P(shards),
            P(None, shards),
            P(shards),
            P(shards, None),
            P(shards, None),
            P(shards, None),
            P(shards),
            P(shards, None),
            P(shards),
        ),
        check_vma=False,
    )
```

```python
import functools

import jax
import jax.numpy as jnp
import numpy as np
from jax import lax
from jax.experimental import pallas as pl
from jax.experimental.pallas import tpu as pltpu
from jax.sharding import PartitionSpec as P

HEADS = 12
HD = 64
EPS = 1e-05
HIGH = lax.Precision.HIGHEST
BF = jnp.bfloat16
F32 = jnp.float32
PACK = 4
BLOCK = PACK * HD
LANES = 128
SPANS = (128, 512, 1024)
SCALE = 1000
GELU_C = float(np.sqrt(2.0 / np.pi))


def nn(left, right):
    return lax.dot_general(left, right, (((1,), (0,)), ((), ())), preferred_element_type=F32)


def nt(left, right):
    return lax.dot_general(left, right, (((1,), (1,)), ((), ())), preferred_element_type=F32)


def normalize(vector):
    average = jnp.mean(vector, axis=-1, keepdims=True)
    centred = vector - average
    inverse = lax.rsqrt(jnp.mean(centred * centred, axis=-1, keepdims=True) + EPS)
    return centred * inverse, inverse


def norm_back(grad_normed, normed, inverse):
    return inverse * (
        grad_normed
        - jnp.mean(grad_normed, axis=-1, keepdims=True)
        - normed * jnp.mean(grad_normed * normed, axis=-1, keepdims=True)
    )


def rows_sum(value):
    return jnp.sum(value, axis=0, keepdims=True)


def head_masks():
    lane = lax.broadcasted_iota(jnp.int32, (1, BLOCK), 1)
    return [(lane // HD == h).astype(F32).astype(BF) for h in range(PACK)]


def swap_halves(value):
    half = HD // 2
    lane = lax.broadcasted_iota(jnp.int32, value.shape, 1)
    ahead = pltpu.roll(value, LANES - half, 1)
    behind = pltpu.roll(value, half, 1)
    return jnp.where(lane % HD < half, ahead, behind)


def arrange_kernel(lengths, tok_ref, cond_ref, *refs):
    parts = tok_ref.shape[0]
    first_ref, rest_ref, both_ref, order_ref = refs
    rank = []
    for s in range(parts):
        ahead = jnp.int32(0)
        for k in range(parts):
            if k < s:
                ahead = ahead + (lengths[k] >= lengths[s]).astype(jnp.int32)
            elif k > s:
                ahead = ahead + (lengths[k] > lengths[s]).astype(jnp.int32)
        rank.append(ahead)
    both_ref[...] = jnp.zeros_like(both_ref)
    for r in range(parts):
        at = jnp.int32(0)
        for k in range(1, parts):
            at = jnp.where(rank[k] == r, k, at)
        if r == 0:
            first_ref[0] = tok_ref[at]
        else:
            rest_ref[r - 1] = tok_ref[at]
        width = cond_ref.shape[1]
        both_ref[r : r + 1, :width] = cond_ref[pl.ds(at, 1), :]
        both_ref[r : r + 1, width:] = jnp.full((1, LANES), lengths[at]).astype(F32)
        order_ref[r] = at
        order_ref[parts + r] = rank[r]


def arrange_pulls_kernel(order, pull_ref, out_ref):
    for r in range(pull_ref.shape[0]):
        out_ref[r] = pull_ref[order[r]]


def put_kernel(order, *refs):
    parts = (order.shape[0] - 1)
    step = pl.program_id(0)
    value_ref, moved_ref = refs[:2]
    grads, moves = refs[2 : 2 + parts], refs[2 + parts : 2 + 2 * parts]
    out_ref, grad_ref = refs[2 + 2 * parts :]
    stays = order[parts] == 1
    out_ref[...] = jnp.where(stays, value_ref[...], moved_ref[...])
    for s in range(parts):

        @pl.when((step == s) & stays)
        def _():
            grad_ref[0] = grads[s][...]

        @pl.when((step == s) & ~stays)
        def _():
            grad_ref[0] = moves[s][...].astype(F32)


def front_kernel(
    place, a_ref, b_ref, c_ref, d_ref, mod_ref, gain_ref, w_ref, cos_ref, sin_ref,
    actt_ref, q_ref, k_ref, v_ref, mix_ref, lse_ref, queries, keys, values,
):
    step, length = pl.program_id(1), place[1 + pl.program_id(0)]
    rows, width = a_ref.shape
    groups = width // BLOCK
    chunk = place[0] ^ jnp.minimum(step, 3)
    here = pl.ds(pl.multiple_of(chunk * rows, rows), rows)

    def turned(act, start, group):
        at = start + group * BLOCK
        both = nn(act, w_ref[:, at : at + BLOCK])
        cosine, sine = cos_ref[...], sin_ref[...]
        parts = []
        for lane in range(0, BLOCK, LANES):
            part = both[:, lane : lane + LANES]
            parts.append((part * cosine + swap_halves(part) * sine).astype(BF))
        return jnp.concatenate(parts, axis=1)

    @pl.when(step < 4)
    def _():
        source = jnp.where(
            step < 2,
            jnp.where(step == 0, a_ref[...], b_ref[...]),
            jnp.where(step == 2, c_ref[...], d_ref[...]),
        ).astype(F32)
        normed, _ = normalize(source)
        act = (normed * gain_ref[...] * (1.0 + mod_ref[0, 1:2, :]) + mod_ref[0, 0:1, :]).astype(BF)
        actt_ref[...] = act.T

        @pl.when(chunk * rows < length)
        def _():
            for group in range(groups):
                lanes = slice(group * BLOCK, (group + 1) * BLOCK)
                key = turned(act, width, group)
                k_ref[:, lanes] = key
                keys[group, here, :] = key
                at = 2 * width + group * BLOCK
                value = nn(act, w_ref[:, at : at + BLOCK]).astype(BF)
                v_ref[:, lanes] = value
                values[group, here, :] = value

        @pl.when(step == 0)
        def _():
            for group in range(groups):
                query = turned(act, 0, group) * BF(HD**-0.5)
                q_ref[:, group * BLOCK : (group + 1) * BLOCK] = query
                queries[group] = query

    masks = head_masks()
    lane = lax.broadcasted_iota(jnp.int32, (1, BLOCK), 1)
    narrow = lax.broadcasted_iota(jnp.int32, (1, LANES), 1)

    def work(span):
        group = step - 4
        query = queries[group]
        stacked = jnp.concatenate([query * masks[h] for h in range(PACK)], axis=0)
        scores = nt(stacked, keys[group, :span, :])
        top = jnp.max(scores, axis=-1, keepdims=True)
        raised = jnp.exp(scores - top)
        total = jnp.sum(raised, axis=-1, keepdims=True)
        probs = (raised * (1.0 / total)).astype(BF)
        level = top + jnp.log(total)
        logs = jnp.zeros((rows, LANES), F32)
        result = jnp.zeros((rows, BLOCK), F32)
        for head in range(PACK):
            part = slice(head * rows, (head + 1) * rows)
            result = jnp.where(lane // HD == head, nn(probs[part], values[group, :span, :]), result)
            logs = jnp.where(narrow == head, level[part], logs)
        mix_ref[...] = result.astype(BF)
        lse_ref[0] = logs.T[:8, :]

    for span in SPANS:
        pl.when((step >= 4) & (length == span))(functools.partial(work, span))


def attend_back_kernel(
    more, last, place, q_ref, k_ref, v_ref, g_ref, lse_ref, cosq_ref, sinq_ref, cosk_ref, sink_ref,
    wq_ref, wk_ref, wv_ref, actt_ref, owns_ref, *refs,
):
    refs = list(refs)
    before_ref = refs.pop(0) if more else None
    keep_ref, send_ref = refs.pop(0), refs.pop(0)
    outs = [refs.pop(0) for _ in range(4 if last else 1)]
    share, own_share, grad_q, grad_k, grad_v, weights = refs
    masks = head_masks()
    group = pl.program_id(0)
    rows = q_ref.shape[0]

    def unturn(value, cosine, sine, out_ref):
        for lane in range(0, BLOCK, LANES):
            part = value[:, lane : lane + LANES]
            out_ref[: value.shape[0], lane : lane + LANES] = (
                part * cosine - swap_halves(part) * sine
            ).astype(BF)

    @pl.when(group == 0)
    def _():
        share[...] = jnp.zeros_like(share)
        own_share[...] = jnp.zeros_like(own_share)

    def work(span):
        queries, grads = q_ref[...], g_ref[...]
        query_all = jnp.concatenate([queries * masks[h] for h in range(PACK)], axis=0)
        grad_all = jnp.concatenate([grads * masks[h] for h in range(PACK)], axis=0)
        head = lax.broadcasted_iota(jnp.int32, (BLOCK, 1), 0) // HD
        sides = [(head == h).astype(F32).astype(BF) for h in range(PACK)]
        queries_t, grads_t = queries.T, grads.T
        query_t = jnp.concatenate([queries_t * sides[h] for h in range(PACK)], axis=1)
        grad_t = jnp.concatenate([grads_t * sides[h] for h in range(PACK)], axis=1)
        keys, values = k_ref[:span, :], v_ref[:span, :]
        keys_t = keys.T
        raw_all, pull_all = nn(keys, query_t), nn(values, grad_t)
        turned, probs_all, scores_all = [], [], []
        for h in range(PACK):
            part = slice(h * rows, (h + 1) * rows)
            probs = jnp.exp(raw_all[:, part] - lse_ref[0, h : h + 1, :])
            pull = pull_all[:, part]
            scores = (probs * (pull - rows_sum(probs * pull))).astype(BF)
            probs_all.append(probs.astype(BF))
            scores_all.append(scores)
            turned.append(nn(keys_t[h * HD : (h + 1) * HD], scores))
        grad_v[:span, :] = nn(jnp.concatenate(probs_all, axis=1), grad_all).astype(BF)
        grad_keys = nn(jnp.concatenate(scores_all, axis=1), query_all)
        unturn(grad_keys, cosk_ref[:span, :], sink_ref[:span, :], grad_k)
        grad_queries = jnp.concatenate(turned, axis=0).T * HD**-0.5
        unturn(grad_queries, cosq_ref[...], sinq_ref[...], grad_q)
        share[:span, :] += nt(grad_k[:span, :], wk_ref[...]) + nt(grad_v[:span, :], wv_ref[...])
        act = actt_ref[:, :span]
        products = (
            nn(owns_ref[...], grad_q[...]),
            nn(act, grad_k[:span, :]),
            nn(act, grad_v[:span, :]),
        )
        for which, product in enumerate(products):
            lanes = slice(which * BLOCK, (which + 1) * BLOCK)
            if more:
                product = product + before_ref[0, :, lanes]
            if last:
                weights[:, lanes] = product
            else:
                outs[0][0, :, lanes] = product

    for span in SPANS:
        pl.when(place[1] == span)(functools.partial(work, span))
    own_share[...] += nt(grad_q[...], wq_ref[...])
    if last:
        cut = 2 * BLOCK + LANES
        first = jnp.concatenate([weights[:, :BLOCK], weights[:, 2 * BLOCK : cut]], axis=1)
        other = jnp.concatenate([weights[:, BLOCK : 2 * BLOCK], weights[:, cut:]], axis=1)
        part_rows(first, place[2], outs[0], outs[1])
        part_rows(other, place[2], outs[2], outs[3])

    @pl.when(group == pl.num_programs(0) - 1)
    def _():
        def piece(k):
            return share[pl.ds(pl.multiple_of((place[0] ^ k) * rows, rows), rows), :]

        keep_ref[0] = piece(0) + own_share[...]
        keep_ref[1] = piece(1)
        send_ref[0] = piece(2).astype(BF)
        send_ref[1] = piece(3).astype(BF)


def norm_back_kernel(
    s, parts, keep_ref, core_ref, near_ref, tok_ref, gres_ref, mod_ref, gain_ref, before_ref,
    grad_ref, send_ref, sums_ref,
):
    def add(row, value):
        sums_ref[row : row + 1, :] = before_ref[row : row + 1, :] + rows_sum(value)

    pull = keep_ref[0] + core_ref[0].astype(F32) + near_ref[...].astype(F32)
    normed, inverse = normalize(tok_ref[...].astype(F32))
    gain = gain_ref[...]
    sums_ref[...] = before_ref[...]
    add(s, pull)
    add(parts + s, pull * (normed * gain))
    scaled = pull * (1.0 + mod_ref[0, 1:2, :])
    add(sums_ref.shape[0] - 8, scaled * normed)
    grad = gres_ref[0] + norm_back(scaled * gain, normed, inverse)
    grad_ref[...] = grad
    send_ref[...] = grad.astype(BF)


def part_rows(value, core, keep_ref, send_ref):
    blocks, piece, columns = keep_ref.shape
    both = value.reshape(blocks, 2, piece, columns)
    keep_ref[...] = jnp.where(core == 0, both[:, 0], both[:, 1]).astype(keep_ref.dtype)
    send_ref[...] = jnp.where(core == 0, both[:, 1], both[:, 0]).astype(BF)


def combine_kernel(index, *refs):
    for which in range(2):
        mine, got, other, other_got = refs[4 * which : 4 * which + 4]
        keep_ref, send_ref = refs[8 + 2 * which : 10 + 2 * which]
        keep_ref[...] = (mine[...].astype(F32) + got[...].astype(F32)).astype(keep_ref.dtype)
        send_ref[...] = (other[...].astype(F32) + other_got[...].astype(F32)).astype(BF)


def spread_kernel(place, keep_a, got_a, keep_b, got_b, *out_refs):
    rows, wide = keep_a.shape[1:]
    columns = keep_b.shape[2]
    if len(out_refs) == 2:
        out_refs = (out_refs[0].at[0], out_refs[1].at[0], out_refs[0].at[1], out_refs[1].at[1])
    for turn, out_ref in enumerate(out_refs):
        at = place[0] ^ turn
        out_ref[:, :wide] = (keep_a[at].astype(F32) + got_a[at].astype(F32)).astype(out_ref.dtype)
        below = keep_b[at].astype(F32) + got_b[at].astype(F32)
        for k in range(keep_b.shape[1] // rows):
            lanes = slice(wide + k * columns, wide + (k + 1) * columns)
            out_ref[:, lanes] = below[k * rows : (k + 1) * rows].astype(out_ref.dtype)


def place_mlp_kernel(own_ref, near_ref, far_ref, up_ref, out_ref, down_ref):
    total = own_ref[0] + near_ref[0].astype(F32) + far_ref[...].astype(F32)
    rows, hidden = up_ref.shape
    width = out_ref.shape[1]
    up_ref[...] = total[:, :hidden]
    out_ref[...] = total[:, hidden : hidden + width]
    for k in range(down_ref.shape[0] // rows):
        at = hidden + (k + 1) * width
        down_ref[k * rows : (k + 1) * rows, :] = total[:, at : at + width]


def place_att_kernel(own_ref, near_ref, far_ref, qkv_ref):
    total = own_ref[0] + near_ref[0].astype(F32) + far_ref[...].astype(F32)
    width = qkv_ref.shape[1] // 3
    step, side = BLOCK + LANES, width // BLOCK * (BLOCK + LANES)
    for j in range(width // BLOCK):
        for which in range(2):
            at = which * side + j * step
            to = which * width + j * BLOCK
            qkv_ref[:, to : to + BLOCK] = total[:, at : at + BLOCK]
            to = 2 * width + j * BLOCK + which * LANES
            qkv_ref[:, to : to + LANES] = total[:, at + BLOCK : at + step]


def mlp_kernel(
    core, mix0_ref, mix1_ref, mix2_ref, tok0_ref, tok1_ref, tok2_ref, cot_ref, mod_ref, gain_ref, wout_ref, bdown_ref,
    wup_ref, bup_ref, wdown_ref,
    out_ref, gres_ref, gmix_ref, sums_ref,
    keepup_ref, sendup_ref, keepdown_ref, senddown_ref,
    resid, branch, act, act_t, slope, active, second, gsecond, gact, gpre,
):
    step = pl.program_id(0)
    tiles = pl.num_programs(0) // 2
    parts, rows, _ = cot_ref.shape
    mixes, tokens = (mix0_ref, mix1_ref, mix2_ref), (tok0_ref, tok1_ref, tok2_ref)

    def span(s):
        return slice(s * rows, (s + 1) * rows)

    def mod(s, which):
        return mod_ref[s, which : which + 1, :]

    @pl.when(step == 0)
    def _():
        sums_ref[...] = jnp.zeros_like(sums_ref)
        for s in range(parts):
            one = nn(mixes[s][...], wout_ref[...])
            res = tokens[s][...].astype(F32) + mod(s, 2) * one
            branch[span(s), :] = one
            resid[span(s), :] = res
            normed, _ = normalize(res)
            value = (normed * gain_ref[...] * (1.0 + mod(s, 4)) + mod(s, 3)).astype(BF)
            act[span(s), :] = value
            act_t[:, span(s)] = value.T
            second[span(s), :] = jnp.zeros_like(res)
            gact[span(s), :] = jnp.zeros_like(res)

    @pl.when(step < tiles)
    def _():
        for s in range(parts):
            u = nn(act[span(s), :], wup_ref[...]) + bup_ref[...]
            square = u * u
            bent = jnp.tanh(GELU_C * (u + 0.044715 * (square * u)))
            value = (0.5 * u * (1.0 + bent)).astype(BF)
            slope[step, span(s), :] = 0.5 * (1.0 + bent) + 0.5 * u * (1.0 - bent * bent) * (
                GELU_C * (1.0 + 3 * 0.044715 * square)
            )
            active[step, span(s), :] = value
            second[span(s), :] += nn(value, wdown_ref[...])

    @pl.when(step == tiles - 1)
    def _():
        total = jnp.zeros(bdown_ref.shape, F32)
        for s in range(parts):
            two = second[span(s), :] + bdown_ref[...]
            out_ref[s] = (resid[span(s), :] + mod(s, 5) * two).astype(BF)
            pull = cot_ref[s].astype(F32)
            sums_ref[5 * parts + s : 5 * parts + s + 1, :] = rows_sum(pull * two)
            down = (pull * mod(s, 5)).astype(BF)
            gsecond[span(s), :] = down
            total = total + rows_sum(down.astype(F32))
        sums_ref[6 * parts : 6 * parts + 1, :] = total

    @pl.when((step >= tiles) & (step < 2 * tiles))
    def _():
        at = step - tiles
        total = jnp.zeros(bup_ref.shape, F32)
        for s in range(parts):
            pulled = nt(gsecond[span(s), :], wdown_ref[...])
            value = (pulled * slope[at, span(s), :]).astype(BF)
            gpre[span(s), :] = value
            total = total + rows_sum(value.astype(F32))
            gact[span(s), :] += nt(value, wup_ref[...])
        sums_ref[pl.ds(6 * parts + 2 + at, 1), :] = total
        part_rows(nn(active[at].T, gsecond[...]), core[0], keepdown_ref, senddown_ref)
        part_rows(nn(act_t[...], gpre[...]), core[0], keepup_ref, sendup_ref)

    @pl.when(step == 2 * tiles)
    def _():
        total = jnp.zeros(bdown_ref.shape, F32)
        outer = jnp.zeros(resid.shape[1:] * 2, F32)
        for s in range(parts):
            normed, inverse = normalize(resid[span(s), :])
            pull = gact[span(s), :]
            sums_ref[3 * parts + s : 3 * parts + s + 1, :] = rows_sum(pull)
            sums_ref[4 * parts + s : 4 * parts + s + 1, :] = rows_sum(
                pull * (normed * gain_ref[...])
            )
            scaled = pull * (1.0 + mod(s, 4))
            total = total + rows_sum(scaled * normed)
            grad = cot_ref[s].astype(F32) + norm_back(scaled * gain_ref[...], normed, inverse)
            gres_ref[s] = grad
            sums_ref[2 * parts + s : 2 * parts + s + 1, :] = rows_sum(grad * branch[span(s), :])
            one = (grad * mod(s, 2)).astype(BF)
            gmix_ref[s] = nt(one, wout_ref[...]).astype(BF)
            outer = outer + nn(mixes[s][...].T, one)
        part_rows(outer, core[0], keepup_ref, sendup_ref)
        sums_ref[6 * parts + 1 : 6 * parts + 2, :] = total


def whole(array):
    rank = array.ndim
    return pl.BlockSpec(array.shape, lambda *_: (0,) * rank, pipeline_mode=pl.Buffered(1))


def limits(mib=60):
    return pltpu.CompilerParams(vmem_limit_bytes=mib * 2**20)


def cost(flops, bytes_accessed):
    return pl.CostEstimate(
        flops=int(flops) // SCALE, bytes_accessed=int(bytes_accessed) // SCALE, transcendentals=0
    )


def arrange(lengths, tokens, cond):
    parts, rows, width = tokens.shape
    shapes = [jax.ShapeDtypeStruct((n, rows, width), BF) for n in (1, parts - 1)]
    shapes.append(jax.ShapeDtypeStruct((8, cond.shape[1] + LANES), F32))
    return pl.pallas_call(
        arrange_kernel,
        grid_spec=pltpu.PrefetchScalarGridSpec(
            num_scalar_prefetch=1,
            grid=(1,),
            in_specs=[whole(tokens), whole(cond)],
            out_specs=[whole(v) for v in shapes] + [pl.BlockSpec(memory_space=pltpu.SMEM)],
        ),
        out_shape=shapes + [jax.ShapeDtypeStruct((2 * parts,), jnp.int32)],
        compiler_params=limits(32),
        cost_estimate=cost(1e6, 3e6),
        name="arrange",
    )(lengths, tokens, cond)


def arrange_pulls(order, pulls):
    return pl.pallas_call(
        arrange_pulls_kernel,
        grid_spec=pltpu.PrefetchScalarGridSpec(
            num_scalar_prefetch=1,
            grid=(1,),
            in_specs=[whole(pulls)],
            out_specs=whole(pulls),
        ),
        out_shape=jax.ShapeDtypeStruct(pulls.shape, BF),
        compiler_params=limits(32),
        cost_estimate=cost(1e6, 3e6),
        name="arrange_pulls",
    )(order, pulls)


def put(order, value, moved, grads, moves):
    parts, rows, width = value.shape
    block = pl.BlockSpec((1, rows, width), lambda i, p: (i, 0, 0))
    placed = pl.BlockSpec((1, rows, width), lambda i, p: (p[i], 0, 0))
    return pl.pallas_call(
        put_kernel,
        grid_spec=pltpu.PrefetchScalarGridSpec(
            num_scalar_prefetch=1,
            grid=(parts,),
            in_specs=[block, block] + [whole(v) for v in list(grads) + list(moves)],
            out_specs=[placed, placed],
        ),
        out_shape=[
            jax.ShapeDtypeStruct(value.shape, BF),
            jax.ShapeDtypeStruct(value.shape, F32),
        ],
        compiler_params=limits(40),
        cost_estimate=cost(1e6, 1e7),
        name="put",
    )(order, value, moved, *grads, *moves)


def front(place, pieces, mod, first, gain, w_qkv, cosine, sine):
    count, rows, width = pieces[0].shape
    slots, groups = 4 * rows, width // BLOCK
    chunk = lambda i, p: p[0] ^ jnp.minimum(i, 3)
    group = lambda i: jnp.maximum(i - 4, 0)
    table = pl.BlockSpec((rows, LANES), lambda s, i, p: (chunk(i, p), 0))
    piece = pl.BlockSpec((None, rows, width), lambda s, i, p: (s, chunk(i, p), 0))
    return pl.pallas_call(
        front_kernel,
        grid_spec=pltpu.PrefetchScalarGridSpec(
            num_scalar_prefetch=1,
            grid=(count, 4 + groups),
            in_specs=[pl.BlockSpec((None, rows, width), lambda s, i, p: (s, 0, 0))] * 4
            + [pl.BlockSpec((1,) + mod.shape[1:], lambda s, i, p: (first + s, 0, 0))]
            + [whole(gain), whole(w_qkv), table, table],
            out_specs=[
                pl.BlockSpec((None, width, rows), lambda s, i, p: (s, 0, chunk(i, p))),
                pl.BlockSpec((None, rows, width), lambda s, i, p: (s, 0, 0)),
                piece, piece,
                pl.BlockSpec((None, rows, BLOCK), lambda s, i, p: (s, 0, group(i))),
                pl.BlockSpec((None, 1, 8, rows), lambda s, i, p: (s, group(i), 0, 0)),
            ],
            scratch_shapes=[
                pltpu.VMEM((groups, rows, BLOCK), BF),
                pltpu.VMEM((groups, slots, BLOCK), BF),
                pltpu.VMEM((groups, slots, BLOCK), BF),
            ],
        ),
        out_shape=[
            jax.ShapeDtypeStruct((count, width, slots), BF),
            jax.ShapeDtypeStruct((count, rows, width), BF),
            jax.ShapeDtypeStruct((count, slots, width), BF),
            jax.ShapeDtypeStruct((count, slots, width), BF),
            jax.ShapeDtypeStruct((count, rows, width), BF),
            jax.ShapeDtypeStruct((count, groups, 8, rows), F32),
        ],
        compiler_params=limits(28),
        cost_estimate=cost(2 * count * slots * width * width * 3, 15e6 * count),
        name="front",
    )(place, *pieces, mod, gain, w_qkv, cosine, sine)


def attend_back(
    place, at, queries, keys, values, grads, s, logs, cosine, sine, w_qkv, act_t, before, last, dp_size
):
    _, rows, width = queries.shape
    slots = keys.shape[1]
    groups = width // BLOCK
    own = pl.BlockSpec((None, rows, BLOCK), lambda j, p: (at, 0, j))
    full = pl.BlockSpec((None, slots, BLOCK), lambda j, p: (at, 0, j))
    own_table = pl.BlockSpec((rows, LANES), lambda j, p: (p[0], 0))
    full_table = pl.BlockSpec((slots, LANES), lambda j, p: (0, 0))
    every = pl.BlockSpec((1, width, 3 * BLOCK), lambda j, p: (j, 0, 0))
    blocks, piece, columns = dp_size // 2, width // dp_size, BLOCK + LANES
    more = before is not None
    if last:
        part = (blocks, piece, groups * columns)
        weight_specs = [pl.BlockSpec((blocks, piece, columns), lambda j, p: (0, 0, j))] * 4
        weight_shapes = [jax.ShapeDtypeStruct(part, F32), jax.ShapeDtypeStruct(part, BF)] * 2
    else:
        weight_specs = [every]
        weight_shapes = [jax.ShapeDtypeStruct((groups, width, 3 * BLOCK), F32)]
    return pl.pallas_call(
        functools.partial(attend_back_kernel, more, last),
        grid_spec=pltpu.PrefetchScalarGridSpec(
            num_scalar_prefetch=1,
            grid=(groups,),
            in_specs=[
                own, full, full,
                pl.BlockSpec((None, rows, BLOCK), lambda j, p: (s, 0, j)),
                pl.BlockSpec((None, 1, 8, rows), lambda j, p: (at, j, 0, 0)),
                own_table, own_table, full_table, full_table,
                pl.BlockSpec((width, BLOCK), lambda j, p: (0, j)),
                pl.BlockSpec((width, BLOCK), lambda j, p: (0, groups + j)),
                pl.BlockSpec((width, BLOCK), lambda j, p: (0, 2 * groups + j)),
                pl.BlockSpec(
                    (None, width, slots), lambda j, p: (at, 0, 0), pipeline_mode=pl.Buffered(1)
                ),
                pl.BlockSpec((None, width, rows), lambda j, p: (at, 0, p[0])),
            ]
            + [every] * more,
            out_specs=[pl.BlockSpec((2, rows, width), lambda j, p: (0, 0, 0))] * 2 + weight_specs,
            scratch_shapes=[
                pltpu.VMEM((slots, width), F32),
                pltpu.VMEM((rows, width), F32),
                pltpu.VMEM((rows, BLOCK), BF),
                pltpu.VMEM((slots, BLOCK), BF),
                pltpu.VMEM((slots, BLOCK), BF),
                pltpu.VMEM((width, 3 * BLOCK), F32),
            ],
        ),
        out_shape=[
            jax.ShapeDtypeStruct((2, rows, width), F32),
            jax.ShapeDtypeStruct((2, rows, width), BF),
        ]
        + weight_shapes,
        compiler_params=limits(44),
        cost_estimate=cost(60 * rows * slots * width, 12e6),
        name="attend_back",
    )(
        place, queries, keys, values, grads, logs, cosine, sine, cosine, sine, w_qkv, w_qkv,
        w_qkv, act_t, act_t, *([before] if more else []),
    )


def norm_one_back(keep, core_got, near_got, tokens, at, grad_res, s, mod, gain, sums):
    _, rows, width = tokens.shape
    first = pl.BlockSpec((1, rows, width), lambda i: (0, 0, 0))
    return pl.pallas_call(
        functools.partial(norm_back_kernel, s, mod.shape[0]),
        grid=(1,),
        in_specs=[
            first, first, whole(near_got),
            pl.BlockSpec((None, rows, width), lambda i: (at, 0, 0)),
            pl.BlockSpec((1, rows, width), lambda i: (s, 0, 0)),
            pl.BlockSpec((1,) + mod.shape[1:], lambda i: (s, 0, 0)),
            whole(gain), whole(sums),
        ],
        out_specs=[pl.BlockSpec((rows, width), lambda i: (0, 0))] * 2
        + [pl.BlockSpec(sums.shape, lambda i: (0, 0))],
        out_shape=[
            jax.ShapeDtypeStruct((rows, width), F32),
            jax.ShapeDtypeStruct((rows, width), BF),
            jax.ShapeDtypeStruct(sums.shape, F32),
        ],
        compiler_params=limits(24),
        cost_estimate=cost(40 * rows * width, 6e6),
        name="norm_one_back",
    )(keep, core_got, near_got, tokens, grad_res, mod, gain, sums)


def feed_forward(core, mixes, tokens, pulls, mod, gain, w_out, b_down, w_up, b_up, w_down, dp_size):
    parts, rows, width = pulls.shape
    hidden = w_up.shape[1]
    tile = width
    tiles = hidden // tile
    total = parts * rows
    single = [
        pl.BlockSpec(
            (None, rows, width), lambda i, c, at=at: (at, 0, 0), pipeline_mode=pl.Buffered(1)
        )
        for _, at in mixes + tokens
    ]
    blocks, piece = dp_size // 2, width // dp_size
    tall_piece = hidden // dp_size
    per_tile = tile // (2 * tall_piece)
    late = lambda i: jnp.maximum(i - tiles, 0)
    last = lambda i: jnp.minimum(late(i), tiles - 1)
    turn = lambda i: jnp.minimum(jnp.where(i < tiles, i, i - tiles), tiles - 1)
    wide = pl.BlockSpec((width, tile), lambda i, c: (0, turn(i)))
    bias = pl.BlockSpec((1, tile), lambda i, c: (0, turn(i)))
    tall = pl.BlockSpec((tile, width), lambda i, c: (turn(i), 0))
    out_wide = pl.BlockSpec((blocks, piece, tile), lambda i, c: (0, 0, late(i)))
    out_tall = pl.BlockSpec((per_tile, tall_piece, width), lambda i, c: (last(i), 0, 0))
    outs = [
        jax.ShapeDtypeStruct(pulls.shape, BF),
        jax.ShapeDtypeStruct(pulls.shape, F32),
        jax.ShapeDtypeStruct(pulls.shape, BF),
        jax.ShapeDtypeStruct((6 * parts + 2 + hidden // width + 8, width), F32),
        jax.ShapeDtypeStruct((blocks, piece, hidden + width), BF),
        jax.ShapeDtypeStruct((blocks, piece, hidden + width), BF),
        jax.ShapeDtypeStruct((blocks, tall_piece, width), BF),
        jax.ShapeDtypeStruct((blocks, tall_piece, width), BF),
    ]
    return pl.pallas_call(
        mlp_kernel,
        grid_spec=pltpu.PrefetchScalarGridSpec(
            num_scalar_prefetch=1,
            grid=(2 * tiles + 1,),
            in_specs=single + [whole(a) for a in (pulls, mod, gain, w_out, b_down)]
            + [wide, bias, tall],
            out_specs=[whole(o) for o in outs[:4]]
            + [out_wide, out_wide, out_tall, out_tall],
            scratch_shapes=[
                pltpu.VMEM((total, width), F32),
                pltpu.VMEM((total, width), F32),
                pltpu.VMEM((total, width), BF),
                pltpu.VMEM((width, total), BF),
                pltpu.VMEM((tiles, total, tile), F32),
                pltpu.VMEM((tiles, total, tile), BF),
                pltpu.VMEM((total, width), F32),
                pltpu.VMEM((total, width), BF),
                pltpu.VMEM((total, width), F32),
                pltpu.VMEM((total, tile), BF),
            ],
        ),
        out_shape=outs,
        compiler_params=limits(53),
        cost_estimate=cost(2 * total * width * (6 * hidden + 3 * width), 50e6),
        name="feed_forward",
    )(core, *[v for v, _ in mixes + tokens], pulls, mod, gain, w_out, b_down, w_up, b_up, w_down)


def combine(index, streams, turns, kept, mib):
    in_specs, out_specs, shapes, inputs = [], [], [], []
    for which, (keep, got) in enumerate(streams):
        above, _, below, rows, columns = keep.shape
        tile = columns // turns
        block = (None, None, None, rows, tile)

        def place(i, c, p, flip, which=which, below=below):
            return (i // below, 1 - p[which] if flip else p[which], i % below, 0, c)

        mine = pl.BlockSpec(block, functools.partial(place, flip=False))
        other = pl.BlockSpec(block, functools.partial(place, flip=True))
        out = pl.BlockSpec((None, rows, tile), lambda i, c, p: (i, 0, c))
        in_specs += [mine, mine, other, other]
        inputs += [keep, got, keep, got]
        out_specs += [out, out]
        shape = (above * below, rows, columns)
        shapes += [jax.ShapeDtypeStruct(shape, kept), jax.ShapeDtypeStruct(shape, BF)]
        steps = above * below
    return pl.pallas_call(
        combine_kernel,
        grid_spec=pltpu.PrefetchScalarGridSpec(
            num_scalar_prefetch=1, grid=(steps, turns), in_specs=in_specs, out_specs=out_specs
        ),
        out_shape=shapes,
        compiler_params=limits(mib),
        cost_estimate=cost(inputs[0].size * 4, inputs[0].size * 18),
        name="combine",
    )(index, *inputs)


def spread(place, keep_a, got_a, keep_b, got_b, paired):
    _, rows, wide = keep_a.shape
    columns = wide + keep_b[0].size // rows
    if paired:
        shapes = [jax.ShapeDtypeStruct((2, rows, columns), t) for t in (F32, BF)]
    else:
        shapes = [jax.ShapeDtypeStruct((rows, columns), t) for t in (F32, BF, BF, BF)]
    arrays = (keep_a, got_a, keep_b, got_b)
    return pl.pallas_call(
        spread_kernel,
        grid_spec=pltpu.PrefetchScalarGridSpec(
            num_scalar_prefetch=1,
            grid=(1,),
            in_specs=[whole(v) for v in arrays],
            out_specs=[whole(v) for v in shapes],
        ),
        out_shape=shapes,
        compiler_params=limits(24),
        cost_estimate=cost(columns * rows * 8, columns * rows * 40),
        name="spread",
    )(place, *arrays)


def place_weights(kernel, own, near, far, shapes):
    return pl.pallas_call(
        kernel,
        grid=(1,),
        in_specs=[pl.BlockSpec((1,) + far.shape, lambda i: (0, 0, 0))] * 2 + [whole(far)],
        out_specs=[whole(v) for v in shapes],
        out_shape=shapes,
        compiler_params=limits(24),
        cost_estimate=cost(far.size * 2, far.size * 12),
        name="place_weights",
    )(own, near, far)


def after(value, *others):
    return lax.optimization_barrier((value,) + others)[0]


def body(
    dp_size, seq_size,
    tokens, cond, lengths, gain_one, gain_two, w_ada, b_ada, w_qkv, w_out, w_up, b_up, w_down,
    b_down, cotangent,
):
    parts, rows, width = tokens.shape
    hidden = w_up.shape[1]
    slots = rows * seq_size
    dp_bits = dp_size.bit_length() - 1
    dp, seq = lax.axis_index("dp").astype(jnp.int32), lax.axis_index("seq").astype(jnp.int32)
    core, side = dp & 1, lax.shift_right_logical(seq, jnp.int32(seq_size.bit_length() - 2))
    stays = core == side
    own = jnp.where(stays, seq, seq ^ 2).astype(jnp.int32)

    def dp_swap(value, bit):
        return lax.ppermute(value, "dp", [(i, i ^ (1 << bit)) for i in range(dp_size)])

    def seq_swap(value, bit):
        return lax.ppermute(value, "seq", [(i, i ^ (1 << bit)) for i in range(seq_size)])

    def swap(value, axis, bit):
        return dp_swap(value, bit) if axis == "dp" else seq_swap(value, bit)

    def bit_of(axis, bit):
        return ((dp if axis == "dp" else seq) >> bit) & 1

    pairs = []
    for i in range(dp_size):
        for j in range(seq_size):
            if (i & 1) != j // (seq_size // 2):
                pairs.append((i * seq_size + j, (i ^ 1) * seq_size + (j ^ 2)))

    def send_across(value):
        return lax.ppermute(value, ("dp", "seq"), pairs)

    def settle(value, moved, *others):
        return jnp.where(stays, value, after(moved, *others).astype(value.dtype))

    def regroup(value, moving=None):
        return settle(value, send_across(value if moving is None else moving))

    first_tokens, rest_tokens, both, order = arrange(lengths, tokens, cond.astype(F32))

    puts = jnp.concatenate([order[:parts], stays.astype(jnp.int32)[None]])

    mine_first = regroup(first_tokens)
    both = jnp.where(stays, both, dp_swap(both, 0))
    cond_here, lengths_here = both[:parts, :-LANES].astype(BF), both[:, -1].astype(jnp.int32)
    mod = jnp.dot(cond_here, w_ada, preferred_element_type=F32) + b_ada
    mod = mod.reshape(parts, 6, width)
    places = [jnp.stack([own, lengths_here[s], core]).astype(jnp.int32) for s in range(parts)]
    core_index = core.astype(jnp.int32)[None]
    frequency = np.power(10000.0, -np.arange(HD // 2) * 2.0 / HD).astype(np.float32)
    angles = np.arange(slots).astype(np.float32)[:, None] * frequency[None, :]
    angles = angles.astype(np.float64)
    cosine = jnp.asarray(np.tile(np.cos(angles), (1, LANES // (HD // 2))).astype(np.float32))
    sine = np.sin(angles)
    sine = jnp.asarray(np.tile(np.concatenate([-sine, sine], 1), (1, LANES // HD)).astype(np.float32))
    gain_one_row, gain_two_row = gain_one[None, :], gain_two[None, :]

    tie = lax.optimization_barrier
    forth = list(range(1, dp_bits))
    back = forth[::-1]
    halves = [jnp.stack([bit_of("dp", i), bit_of("dp", j)]) for i, j in zip(forth, back)]
    own_seq = seq[None]
    first_place = jnp.concatenate([own[None], lengths_here[:1]])
    rest_place = jnp.concatenate([own[None], lengths_here[1:]])
    mine_first = after(
        mine_first, mod, *places, *halves, own_seq, puts, core_index, first_place, rest_place
    )
    near = seq_swap(mine_first, 0)
    moving = send_across(rest_tokens)
    far = dp_swap(mine_first, 0)
    mine_rest = settle(rest_tokens, moving)
    group = (mine_first, near, far, dp_swap(near, 0))
    mine_rest = after(mine_rest, *group)
    near_rest, far_rest = seq_swap(mine_rest, 0), dp_swap(mine_rest, 0)
    pulls = arrange_pulls(order, after(cotangent, mine_first))
    group = tie((group, mine_rest))[0]
    fronts = [front(first_place, group, mod, 0, gain_one_row, w_qkv, cosine, sine)]
    near_rest, far_rest, pulls, _ = tie((near_rest, far_rest, pulls, fronts[0][4]))
    pulled = send_across(after(pulls, near_rest))
    group = (mine_rest, near_rest, far_rest, dp_swap(near_rest, 0))
    fronts.append(front(rest_place, group, mod, 1, gain_one_row, w_qkv, cosine, sine))
    pulls = settle(pulls, pulled, fronts[1][4])
    where = [(0, 0)] + [(1, k) for k in range(parts - 1)]
    mine = [((mine_first, mine_rest)[f], at) for f, at in where]
    mixes = [(fronts[f][4], at) for f, at in where]

    output, grad_res, grad_mix, sums, keep_up, send_up, keep_down, send_down = feed_forward(
        core_index, mixes, mine, pulls, mod, gain_two_row, w_out,
        b_down[None, :], w_up, b_up[None, :], w_down, dp_size,
    )
    output_moved = send_across(output)

    class Halving:
        def __init__(self, arrays, sends, turns, mib):
            self.mib = mib
            self.arrays, self.sends, self.turns, self.at = arrays, sends, turns, [0, 0]
            self.orders = [list(forth), list(back)]
            self.names = [forth[::-1], forth[::-1]]
            self.move()

        def merge(self, kept=F32):
            streams, self.at = [], []
            index = halves[len(forth) - len(self.orders[0])]
            for which in range(2):
                bit = self.orders[which].pop(0)
                names = self.names[which]
                place = names.index(bit)
                names.pop(place)
                keep = self.arrays[which]
                shape = (2**place, 2, 2 ** (len(names) - place)) + keep.shape[1:]
                streams.append((keep.reshape(shape), self.got[which].reshape(shape)))
                self.at.append(bit)
            keep_a, send_a, keep_b, send_b = combine(index, streams, self.turns, kept, self.mib)
            self.arrays, self.sends, self.turns = [keep_a, keep_b], [send_a, send_b], 1
            return self.sends

        def move(self):
            self.got = [dp_swap(v, bit) for v, bit in zip(self.sends, self.at)]

        def spread(self, paired):
            pieces = [
                v.reshape(seq_size, v.shape[1] // seq_size, v.shape[2]) for v in self.arrays + self.got
            ]
            self.own, *self.sends = spread(
                own_seq, pieces[0], pieces[2], pieces[1], pieces[3], paired
            )
            return self.sends

        def send(self):
            self.got = [
                lax.ppermute(v, "seq", [(i, i ^ k) for i in range(seq_size)])
                for k, v in enumerate(self.sends, 1)
            ]

    mlp = Halving([keep_up, keep_down], [send_up, send_down], 2, 60)

    shares, cores, nears, grad_tokens, moved = [], [], [], [], []

    def pass_on(s):
        there = (shares[s][0][1] + cores[s][1].astype(F32)).astype(BF)
        nears.append(seq_swap(there, 0))
        return there

    def finish(s, sums):
        grad, rounded, sums = norm_one_back(
            shares[s][0], cores[s], nears[s], *mine[s], grad_res, s, mod, gain_one_row, sums
        )
        grad_tokens.append(grad)
        return rounded, sums

    def give_back(s, rounded):
        moved.append(send_across(rounded))

    waits, weights = [], [None]
    for s in range(parts):
        at = where[s][1]
        act_t, queries, keys, values, _, logs = fronts[where[s][0]]
        keep, send, *weights = attend_back(
            places[s], at, after(queries, *waits), keys, values, grad_mix, s, logs, cosine,
            sine, w_qkv, act_t, weights[0], s == parts - 1, dp_size,
        )
        if s == 0:
            send, weights, mlp.got = tie((send, weights, mlp.got))
        elif s == 1:
            send, weights, mlp.got, nears[0], output_moved = tie(
                (send, weights, mlp.got, nears[0], output_moved)
            )
        else:
            send, weights, mlp.got, nears[1], moved[0] = tie(
                (send, weights, mlp.got, nears[1], moved[0])
            )
        shares.append((keep, send))
        cores.append(dp_swap(send, 0))
        if s == parts - 1:
            break
        if mlp.orders[0]:
            waits = list(mlp.merge(BF if s == 0 else F32))
            mlp.move()
        if s:
            rounded, sums = finish(s - 1, sums)
            give_back(s - 1, rounded)
            waits.append(rounded)
        cores[-1] = after(cores[-1], *waits)
        waits.append(pass_on(s))

    while mlp.orders[0]:
        mlp.merge()
        mlp.move()
    waits = mlp.spread(True)
    mlp.send()
    att = Halving([weights[0], weights[2]], [weights[1], weights[3]], 1, 24)
    cores[-1] = after(cores[-1], *waits)
    passed = pass_on(parts - 1)
    nears[-2] = after(nears[-2], passed)
    rounded, sums = finish(parts - 2, sums)
    give_back(parts - 2, rounded)
    att.got = tie((att.got, rounded))[0]
    waits = att.merge()
    att.move()
    while att.orders[0]:
        att.got = tie((att.got, *waits))[0]
        waits = att.merge()
        att.move()
    mlp.got, mlp.own = tie((mlp.got, mlp.own, *waits))[:2]
    further = (mlp.own[1] + mlp.got[0][1].astype(F32)).astype(BF)
    att.got = tie((att.got, further))[0]
    further = seq_swap(further, 1)
    waits = att.spread(True)
    att.send()
    nears[-1] = after(nears[-1], *waits)
    rounded, sums = finish(parts - 1, sums)
    give_back(parts - 1, rounded)
    held = sums + dp_swap(sums, 0)
    across = seq_swap(held, 0)
    att.got, att.own, moved[-2] = tie((att.got, att.own, moved[-2], held))[:3]
    later = (att.own[1] + att.got[0][1].astype(F32)).astype(BF)
    held = held + after(across, later)
    later = seq_swap(later, 1)

    count, kept = 6 * parts, held.shape[0] - 7
    conds = cond_here.astype(F32).reshape(1, -1)
    conds = jnp.pad(conds, ((0, 0), (0, width - conds.shape[1])))
    ours = jnp.concatenate([held[:kept], conds]).astype(BF)[None]
    got = swap(ours, "seq", 1)
    piece, tall = width // (dp_size * seq_size), hidden // (dp_size * seq_size)
    shapes = [
        jax.ShapeDtypeStruct((piece, hidden), F32),
        jax.ShapeDtypeStruct((piece, width), F32),
        jax.ShapeDtypeStruct((tall, width), F32),
    ]
    g_w_up, g_w_out, g_w_down = place_weights(
        place_mlp_kernel, mlp.own, mlp.got[0], after(further, ours), shapes
    )
    got = after(got, g_w_up)
    mod_here = jnp.where(stays, held[:count], got[0, :count].astype(F32))
    ours = jnp.concatenate([ours, got])
    for bit in forth:
        got = swap(ours, "dp", bit)
        if bit == forth[-1]:
            shapes = [jax.ShapeDtypeStruct((piece, 3 * width), F32)]
            (g_w_qkv,) = place_weights(
                place_att_kernel, att.own, att.got[0], after(later, ours), shapes
            )
            moved[-1] = after(moved[-1], g_w_qkv)
            output, g_tokens = put(puts, output, output_moved, grad_tokens, tuple(moved))
            got = after(got, g_tokens)
        ours = jnp.concatenate([ours, got])
    ours = ours.astype(F32)
    totals = jnp.sum(ours[:, count:kept], axis=0)
    g_cond = sum(
        jnp.dot(
            mod_here[k * parts : (k + 1) * parts],
            w_ada[:, k * width : (k + 1) * width].astype(F32).T,
            precision=HIGH,
        )
        for k in range(6)
    )
    chosen = order[:parts, None] == jnp.arange(parts)[None, :]
    g_cond = jnp.sum(jnp.where(chosen[:, :, None], g_cond[:, None], 0.0), axis=0)
    groups = ours.shape[0]
    conds = ours[:, kept, : cond_here.size].reshape(groups * parts, -1)
    lanes = ours[:, :count].reshape(groups, 6, parts, width).transpose(0, 2, 1, 3)
    lanes = lanes.reshape(groups * parts, 6 * width)
    shards = dp_size * seq_size
    index = dp * seq_size + seq

    def mine_of(value):
        size = value.shape[-1] // shards
        starts = (jnp.int32(0),) * (value.ndim - 1) + (index * size,)
        sizes = value.shape[:-1] + (size,)
        return lax.dynamic_slice(value, starts, sizes, allow_negative_indices=False)

    lanes = mine_of(lanes)
    g_w_ada = jnp.dot(conds.T, lanes, precision=HIGH)
    g_b_ada = jnp.sum(lanes, axis=0)
    g_b_down, g_gain_two, g_gain_one = mine_of(totals[0]), mine_of(totals[1]), mine_of(totals[-1])
    g_b_up = mine_of(totals[2:-1].reshape(-1))
    return (
        output,
        g_tokens,
        g_cond,
        g_gain_one,
        g_gain_two,
        g_w_ada,
        g_b_ada,
        g_w_qkv,
        g_w_out,
        g_w_up,
        g_b_up,
        g_w_down,
        g_b_down,
    )


def solution(mesh):
    shards = ("dp", "seq")
    placed = (
        (P("dp", "seq", None), P("dp", None), P("dp"))
        + (P(),) * 10
        + (P("dp", "seq", None),)
    )
    return jax.shard_map(
        functools.partial(body, mesh.shape["dp"], mesh.shape["seq"]),
        mesh=mesh,
        in_specs=placed,
        out_specs=(
            P("dp", "seq", None),
            P("dp", "seq", None),
            P("dp", None),
            P(shards),
            P(shards),
            P(None, shards),
            P(shards),
            P(shards, None),
            P(shards, None),
            P(shards, None),
            P(shards),
            P(shards, None),
            P(shards),
        ),
        check_vma=False,
    )
```
